32 devices in a mesh: tm: 4 (over y, x), space: 8 (over z, core).
Axes of the slice: x: 2, y: 2, z: 4, core: 2. Of those that a mesh axis runs over, the one named last changes fastest.
Arguments:
- frames_in: bfloat16 [16, 32, 64, 512], P('tm', 'space'), may hold values from -6 to 6
- spatial_kernel: bfloat16 [3, 3, 512, 512], replicated, may hold values from -0.09375 to 0.09375
- temporal_kernel: bfloat16 [3, 512, 512], replicated, may hold values from -0.15625 to 0.15625
- norm_gain: float32 [512], replicated, may hold values from 0.1 to 1.9
- query_weight: bfloat16 [512, 512], replicated, may hold values from -2 to 2
- key_weight: bfloat16 [512, 512], replicated, may hold values from -2 to 2
- value_weight: bfloat16 [512, 512], replicated, may hold values from -0.25 to 0.25
- out_weight: bfloat16 [512, 512], replicated, may hold values from -0.25 to 0.25
- cotangent: bfloat16 [16, 32, 64, 512], P('tm', 'space'), may hold values from -6 to 6
Outputs:
- encoded: bfloat16 [16, 32, 64, 512], P('tm', 'space')
- kernel_grad: float32 [3, 512, 512], P(None, 'tm', 'space')
The draws below stay inside these ranges and needn't reach their ends.
All inputs are finite; a program needn't handle non-finite values.
Results may differ from the reference program's by a relative error of at most 0.007.
Values may be sent and summed in bfloat16 or wider, within the bound.
No kernel may reach another device: no remote copies, remote signals or barrier semaphores. Data moves between devices by JAX's collectives and lax.ppermute only.
A program may use at most 128 MiB of HBM per device.

```python
import jax
import jax.numpy as jnp
from jax import lax

C = 512
WCOL = 64
FRAMES = 16
ROWS = 32


def pair_weights(key):
    base = jax.random.normal(jax.random.fold_in(key, 11), (C, C), jnp.float32) * C ** (-0.5)
    other = jax.random.normal(jax.random.fold_in(key, 12), (C, C), jnp.float32) * C ** (-0.5)
    query = other
    return (jnp.clip(query, -2.0, 2.0), jnp.clip(base, -2.0, 2.0))


def draw_query_weight(key, part):
    return pair_weights(key)[0].astype(jnp.bfloat16)


def draw_key_weight(key, part):
    return pair_weights(key)[1].astype(jnp.bfloat16)


def draw_frames_in(key, part):
    values = jax.random.normal(jax.random.fold_in(key, 24), (FRAMES, ROWS, WCOL, C), jnp.float32)
    return jnp.clip(values, -6.0, 6.0).astype(jnp.bfloat16)


def spiked(drawn, rng, source, target, parts, factor):
    owner, partner = [(jnp.arange(drawn.shape[axis_at]) // (drawn.shape[axis_at] // parts)).reshape([-1 if axis == axis_at else 1 for axis in range(drawn.ndim)]) for axis_at in (source, target)]
    chosen = jax.random.permutation(rng, parts)[partner]
    strong = (owner == chosen) | (owner == (partner + parts // 2) % parts)
    return jnp.where(strong, factor * drawn, drawn)


def level_of(key, extent, cuts, low, high):
    def one(axis_at, parts):
        draws = jax.random.uniform(jax.random.fold_in(jax.random.fold_in(key, 6), axis_at), (parts,), jnp.float32, low / len(cuts), high / len(cuts))
        return jnp.repeat(jnp.exp(draws), extent[axis_at] // parts).reshape((-1,) + (1,) * (len(extent) - axis_at - 1))

    level = one(*cuts[0])
    for cut in cuts[1:]:
        level = level * one(*cut)
    return level


def centred(stream_key, shape, width, most, split=(), dtype=jnp.bfloat16):
    loudness = level_of(stream_key, shape, split, -0.22, 0.18) if split else 1.0
    drawn = jax.random.normal(stream_key, shape, jnp.float32) * width * loudness
    return jnp.minimum(jnp.maximum(drawn, -most), most).astype(dtype)


def bell_draw_with(own_key, shape, spread, limit, split, heavy, kind=jnp.bfloat16):
    values = spread * jax.random.normal(own_key, shape, jnp.float32)
    if split:
        values = values * level_of(own_key, shape, split, -0.22, 0.18)
    return jnp.clip(spiked(values, jax.random.fold_in(own_key, 3), *heavy), -limit, limit).astype(kind)


def setup_inputs(seed: int = 0) -> dict:
    keys = jax.random.split(jax.random.key(seed), 10)
    frames_in = draw_frames_in(jax.random.fold_in(keys[9], 71), 0)
    spatial_kernel = centred(keys[1], (3, 3, C, C), (9 * C) ** -0.5, 0.09375)
    temporal_kernel = centred(keys[2], (3, C, C), (3 * C) ** -0.5, 0.15625)
    norm_gain = jnp.clip(1.0 + 0.18 * jax.random.normal(keys[3], (C,), jnp.float32), 0.1, 1.9)
    query_weight = draw_query_weight(jax.random.fold_in(keys[9], 71), 0)
    key_weight = draw_key_weight(jax.random.fold_in(keys[9], 71), 0)
    value_weight = centred(keys[6], (C, C), C ** -0.5, 0.25)
    out_weight = centred(keys[7], (C, C), C ** -0.5, 0.25)
    cotangent = bell_draw_with(keys[8], (FRAMES, ROWS, WCOL, C), 1.0, 6.0, ((0, 4), (1, 8)), (1, 3, 8, 2.0))
    return dict(frames_in=frames_in, spatial_kernel=spatial_kernel, temporal_kernel=temporal_kernel, norm_gain=norm_gain, query_weight=query_weight, key_weight=key_weight, value_weight=value_weight, out_weight=out_weight, cotangent=cotangent)


def causal_attend(query, key, value):
    frames = query.shape[0]
    scores = jnp.einsum('anc,bnc->abn', query.astype(jnp.float32), key.astype(jnp.float32)) / jnp.sqrt(jnp.float32(query.shape[2]))
    rows = jnp.arange(frames)[:, None, None]
    cols = jnp.arange(frames)[None, :, None]
    allowed = cols <= rows
    scores = jnp.where(allowed, scores, jnp.float32(-1e+30))
    top = lax.optimization_barrier(jnp.max(scores, axis=1, keepdims=True))
    expon = jnp.where(allowed, jnp.exp(scores - top), jnp.float32(0.0))
    total = lax.optimization_barrier(jnp.sum(expon, axis=1))
    mixed = jnp.einsum('abn,bnc->anc', expon, value.astype(jnp.float32))
    return mixed / total[:, :, None]

def reference(frames_in, spatial_kernel, temporal_kernel, norm_gain, query_weight, key_weight, value_weight, out_weight, cotangent):
    frames, rows, cols, chans = frames_in.shape
    padded = jnp.pad(frames_in, ((0, 0), (1, 1), (1, 1), (0, 0)))
    spatial = jnp.zeros((frames * rows * cols, chans), jnp.float32)
    for di in range(3):
        for dj in range(3):
            piece = padded[:, di:di + rows, dj:dj + cols, :].reshape(-1, chans)
            spatial = spatial + jnp.dot(piece, spatial_kernel[di, dj], preferred_element_type=jnp.float32)
    act = jax.nn.silu(spatial).astype(jnp.bfloat16).reshape(frames, rows, cols, chans)
    extended = jnp.pad(act, ((2, 0), (0, 0), (0, 0), (0, 0)))
    temporal = jnp.zeros((frames * rows * cols, chans), jnp.float32)
    flat_grad = cotangent.reshape(-1, chans)
    grads = []
    for tap in range(3):
        shifted = extended[2 - tap:2 - tap + frames].reshape(-1, chans)
        temporal = temporal + jnp.dot(shifted, temporal_kernel[tap], preferred_element_type=jnp.float32)
        grads.append(jnp.einsum('nc,nd->cd', shifted, flat_grad, preferred_element_type=jnp.float32))
    hidden = (frames_in.reshape(-1, chans).astype(jnp.float32) + temporal).astype(jnp.bfloat16)
    wide = hidden.astype(jnp.float32)
    normed = (wide / jnp.sqrt(lax.optimization_barrier(jnp.mean(wide * wide, axis=1, keepdims=True)) + 1e-06) * norm_gain).astype(jnp.bfloat16)
    query = jnp.dot(normed, query_weight, preferred_element_type=jnp.float32).astype(jnp.bfloat16).reshape(frames, rows * cols, chans)
    key = jnp.dot(normed, key_weight, preferred_element_type=jnp.float32).astype(jnp.bfloat16).reshape(frames, rows * cols, chans)
    value = jnp.dot(normed, value_weight, preferred_element_type=jnp.float32).astype(jnp.bfloat16).reshape(frames, rows * cols, chans)
    attended = causal_attend(query, key, value).astype(jnp.bfloat16).reshape(-1, chans)
    encoded = (wide + jnp.dot(attended, out_weight, preferred_element_type=jnp.float32)).astype(jnp.bfloat16)
    return (encoded.reshape(frames, rows, cols, chans), jnp.stack(grads, axis=0))
```

```python
import functools

import jax
import jax.numpy as jnp
from jax import lax
from jax.experimental import pallas as pl
from jax.experimental.pallas import tpu as pltpu
from jax.sharding import PartitionSpec as P

BF = jnp.bfloat16
F32 = jnp.float32
VMEM = pl.BlockSpec(memory_space=pltpu.VMEM)
SMEM = pl.BlockSpec(memory_space=pltpu.SMEM)


def call(kernel, outs, *args, flops=0, scratch=()):
    moved = sum(a.size * a.dtype.itemsize for a in args)
    moved += sum(o.size * o.dtype.itemsize for o in outs)
    return pl.pallas_call(
        kernel,
        out_shape=tuple(outs),
        in_specs=[SMEM if a.dtype == jnp.int32 else VMEM for a in args],
        out_specs=tuple(VMEM for _ in outs),
        scratch_shapes=scratch,
        compiler_params=pltpu.CompilerParams(vmem_limit_bytes=40 * 2**20),
        cost_estimate=pl.CostEstimate(flops=flops, bytes_accessed=moved, transcendentals=0),
    )(*args)


def shape(dims, kind=BF):
    return jax.ShapeDtypeStruct(dims, kind)


def chooser(rows, cols, source):
    q = lax.broadcasted_iota(jnp.int32, (rows, cols), 0)
    m = lax.broadcasted_iota(jnp.int32, (rows, cols), 1)
    return jnp.where(source(q) == m, 1.0, 0.0).astype(BF)


def moved(matrix, rows):
    return jnp.dot(matrix, rows, preferred_element_type=F32).astype(BF)


class Sizes:
    def __init__(self, count, frames, rows, cols, chans):
        self.n, self.fl, self.r, self.w, self.c = count, frames, rows, cols, chans
        self.f = count * frames
        self.wc = cols // count
        self.block = self.f * self.wc
        self.piece = frames * self.wc
        self.main = rows * self.piece
        self.sides = 2 * rows * frames


def pack_kernel(z, halo, me_ref, x_ref, *outs):
    me = me_ref[0]

    def source(q):
        k = q // z.piece
        f = q % z.piece // z.wc
        return f * z.w + (me ^ k) * z.wc + q % z.wc

    matrix = chooser(z.n * z.piece, z.fl * z.w, source)
    for r in range(z.r):
        rows = x_ref[:, r].reshape(z.fl * z.w, z.c)
        cut = moved(matrix, rows)
        for k in range(z.n):
            outs[k][r * z.piece : (r + 1) * z.piece] = cut[k * z.piece : (k + 1) * z.piece]
    if not halo:
        return

    def edge(q):
        k = q // z.sides
        side = q % z.sides // (z.r * z.fl)
        r = q % (z.r * z.fl) // z.fl
        f = q % z.fl
        col = (me ^ k) * z.wc - 1 + side * (z.wc + 1)
        inside = (col >= 0) & (col < z.w)
        return jnp.where(inside, (f * z.r + r) * z.w + col, -1)

    total = z.fl * z.r * z.w
    cut = moved(chooser(z.n * z.sides, total, edge), x_ref[...].reshape(total, z.c))
    for k in range(z.n):
        outs[k][z.main : z.main + z.sides] = cut[k * z.sides : (k + 1) * z.sides]


def gather_matrix(z, me):
    def source(q):
        s = q % z.f // z.fl
        return ((me ^ s) * z.fl + q % z.fl) * z.wc + q // z.f

    return chooser(z.block, z.block, source)


def assemble_kernel(z, me_ref, *refs):
    parts, (out, top, bottom) = refs[: z.n], refs[z.n :]
    me = me_ref[0]
    matrix = gather_matrix(z, me)

    def edge(q):
        head = q // z.f
        s = q % z.f // z.fl
        return ((me ^ s) * 2 * z.r + head) * z.fl + q % z.fl

    count = z.n * z.sides
    tails = jnp.concatenate([p[z.main : z.main + z.sides] for p in parts], axis=0)
    tails = moved(chooser(count, count, edge), tails)
    last = z.f + z.block
    for r in range(z.r):
        rows = jnp.concatenate([p[r * z.piece : (r + 1) * z.piece] for p in parts], axis=0)
        rows = moved(matrix, rows)
        left = tails[r * z.f : (r + 1) * z.f]
        right = tails[(z.r + r) * z.f : (z.r + r + 1) * z.f]
        copies = [out.at[r]]
        if r == 0:
            copies.append(top)
        if r == z.r - 1:
            copies.append(bottom)
        for ref in copies:
            ref[0 : z.f] = left
            ref[z.f : last] = rows
            ref[last : last + z.f] = right


def inner_kernel(z, x_ref, w_ref, out):
    for r in range(z.r):
        total = jnp.zeros((z.block, z.c), F32)
        for di in range(3):
            if not 0 <= r + di - 1 < z.r:
                continue
            for dj in range(3):
                total += jnp.dot(
                    x_ref[r + di - 1, dj * z.f : dj * z.f + z.block],
                    w_ref[di, dj],
                    preferred_element_type=F32,
                )
        out[r] = total


def act_kernel(z, part_ref, up_ref, down_ref, w_ref, out):
    frame = lax.broadcasted_iota(jnp.int32, (z.block, z.c), 0) % z.f
    for r in range(z.r):
        total = part_ref[r]
        for edge, di, ref in ((0, 0, up_ref), (z.r - 1, 2, down_ref)):
            if r == edge:
                for dj in range(3):
                    total += jnp.dot(
                        ref[dj * z.f : dj * z.f + z.block],
                        w_ref[di, dj],
                        preferred_element_type=F32,
                    )
        act = (total / (1.0 + jnp.exp(-total))).astype(BF)
        out[r, :, 0 : z.c] = act
        wide = act.astype(F32)
        for k in (1, 2):
            late = jnp.where(frame >= k, pltpu.roll(wide, k, 0), 0.0)
            out[r, :, k * z.c : (k + 1) * z.c] = late.astype(BF)


def main_kernel(z, x_ref, act_ref, t_ref, gain_ref, q_ref, k_ref, v_ref, o_ref, out):
    a = lax.broadcasted_iota(jnp.int32, (z.block, z.block), 0)
    b = lax.broadcasted_iota(jnp.int32, (z.block, z.block), 1)
    allowed = (a // z.f == b // z.f) & (b % z.f <= a % z.f)
    scale = float(z.c) ** -0.5
    back = chooser(z.block, z.block, lambda q: q % z.wc * z.f + q // z.wc)
    gain = gain_ref[...]
    for r in range(z.r):
        temporal = jnp.dot(act_ref[r], t_ref[...], preferred_element_type=F32)
        hidden = (x_ref[r, z.f : z.f + z.block].astype(F32) + temporal).astype(BF)
        wide = hidden.astype(F32)
        mean = jnp.mean(wide * wide, axis=1, keepdims=True)
        normed = (wide / jnp.sqrt(mean + 1e-06) * gain).astype(BF)
        query = jnp.dot(normed, q_ref[...], preferred_element_type=F32).astype(BF)
        key = jnp.dot(normed, k_ref[...], preferred_element_type=F32).astype(BF)
        value = jnp.dot(normed, v_ref[...], preferred_element_type=F32).astype(BF)
        scores = lax.dot_general(
            query, key, (((1,), (1,)), ((), ())), preferred_element_type=F32
        )
        scores = jnp.where(allowed, scores * scale, -1e30)
        top = jnp.max(scores, axis=1, keepdims=True)
        expon = jnp.where(allowed, jnp.exp(scores - top), 0.0)
        total = jnp.sum(expon, axis=1, keepdims=True)
        mixed = jnp.dot(expon.astype(BF), value, preferred_element_type=F32)
        attended = (mixed / total).astype(BF)
        encoded = wide + jnp.dot(attended, o_ref[...], preferred_element_type=F32)
        encoded = moved(back, encoded.astype(BF))
        for i in range(z.n):
            out[i, r] = encoded[i * z.piece : (i + 1) * z.piece]


def grad_kernel(z, width, me_ref, *refs):
    parts, (act_ref, keep, send, cot) = refs[: z.n], refs[z.n :]
    matrix = gather_matrix(z, me_ref[0])
    mine = me_ref[1] == 0
    for r in range(z.r):
        rows = jnp.concatenate([p[r * z.piece : (r + 1) * z.piece] for p in parts], axis=0)
        cot[r * z.block : (r + 1) * z.block] = moved(matrix, rows)
    flat = cot[...]
    for k in range(3):
        lanes = slice(k * z.c, (k + 1) * z.c)
        grad = lax.dot_general(
            flat,
            act_ref[:, :, lanes].reshape(z.r * z.block, z.c),
            (((0,), (0,)), ((), ())),
            preferred_element_type=F32,
        )
        for i in range(z.c // (2 * width)):
            low = grad[2 * i * width : (2 * i + 1) * width]
            high = grad[(2 * i + 1) * width : (2 * i + 2) * width]
            keep[i * width : (i + 1) * width, lanes] = jnp.where(mine, low, high)
            send[i * width : (i + 1) * width, lanes] = jnp.where(mine, high, low).astype(BF)


def split_kernel(z, me_ref, keep_ref, got_ref, *outs):
    me = me_ref[0]
    wide = z.c // z.n
    for tap in range(3):
        place = slice(tap * wide, (tap + 1) * wide)
        if wide % 128 == 0:
            for k in range(z.n):
                lanes = pl.ds(pl.multiple_of(tap * z.c + (me ^ k) * wide, 128), wide)
                total = keep_ref[:, lanes] + got_ref[:, lanes].astype(F32)
                outs[k][:, place] = total.astype(outs[k].dtype)
            continue
        lanes = slice(tap * z.c, (tap + 1) * z.c)
        total = keep_ref[:, lanes] + got_ref[:, lanes].astype(F32)
        for k in range(z.n):
            cut = total[:, 0:wide]
            for i in range(1, z.n):
                cut = jnp.where((me ^ k) == i, total[:, i * wide : (i + 1) * wide], cut)
            outs[k][:, place] = cut.astype(outs[k].dtype)


def swap(value, axis, k):
    count = lax.axis_size(axis)
    return lax.ppermute(value, axis, [(i, i ^ k) for i in range(count)])


def on_device(frames_in, spatial, temporal, gain, q_w, k_w, v_w, o_w, cotangent):
    n = lax.axis_size("tm")
    space = lax.axis_size("space")
    z = Sizes(n, *frames_in.shape)
    me = lax.axis_index("tm")
    here = lax.axis_index("space")
    ids = jnp.stack([me, here % 2]).astype(jnp.int32)
    part = [shape((z.main + z.sides, z.c))] * n
    packed = call(functools.partial(pack_kernel, z, True), part, ids, frames_in)
    got = [packed[0]] + [swap(packed[k], "tm", k) for k in range(1, n)]
    line = z.block + 2 * z.f
    x, top, bottom = call(
        functools.partial(assemble_kernel, z),
        [shape((z.r, line, z.c)), shape((line, z.c)), shape((line, z.c))],
        ids,
        *got,
    )
    up = lax.ppermute(bottom, "space", [(i, i + 1) for i in range(space - 1)])
    down = lax.ppermute(top, "space", [(i + 1, i) for i in range(space - 1)])
    part = [shape((z.main, z.c))] * n
    cot = call(functools.partial(pack_kernel, z, False), part, ids, cotangent)
    cot = [cot[0]] + [swap(cot[k], "tm", k) for k in range(1, n)]
    one = 2 * z.r * z.block * z.c * z.c
    (inner,) = call(
        functools.partial(inner_kernel, z),
        [shape((z.r, z.block, z.c), F32)],
        x,
        spatial,
        flops=9 * one * (3 * z.r - 2) // (3 * z.r),
    )
    (acts,) = call(
        functools.partial(act_kernel, z),
        [shape((z.r, z.block, 3 * z.c))],
        inner,
        up,
        down,
        spatial,
        flops=6 * one // z.r,
    )
    width = z.c // space
    keep, send = call(
        functools.partial(grad_kernel, z, width),
        [shape((z.c // 2, 3 * z.c), F32), shape((z.c // 2, 3 * z.c))],
        ids,
        *cot,
        acts,
        flops=3 * one,
        scratch=[pltpu.VMEM((z.r * z.block, z.c), BF)],
    )
    other = swap(send, "space", 1)
    (encoded,) = call(
        functools.partial(main_kernel, z),
        [shape((n, z.r, z.piece, z.c))],
        x,
        acts,
        temporal.reshape(3 * z.c, z.c),
        gain.reshape(1, z.c),
        q_w,
        k_w,
        v_w,
        o_w,
        flops=8 * one,
    )
    wide = z.c // n
    pieces = call(
        functools.partial(split_kernel, z),
        [shape((z.c // 2, 3 * wide), F32)] + [shape((z.c // 2, 3 * wide))] * (n - 1),
        ids,
        keep,
        other,
    )
    back = [lax.dynamic_index_in_dim(encoded, me ^ k, 0, False) for k in range(n)]
    back = [back[0]] + [swap(back[k], "tm", k) for k in range(1, n)]
    total = pieces[0]
    for k in range(1, n):
        total = total + swap(pieces[k], "tm", k).astype(F32)
    chips = space // 2
    total = total.reshape(chips, width, 3 * wide)
    sums = lax.dynamic_index_in_dim(total, here // 2, 0, False)
    total = total.astype(BF)
    for k in range(1, chips):
        mine = lax.dynamic_index_in_dim(total, here // 2 ^ k, 0, False)
        sums = sums + swap(mine, "space", 2 * k).astype(F32)
    kernel_grad = sums.reshape(width, 3, wide).transpose(1, 2, 0)
    whole = jnp.zeros((z.fl, z.r, n, z.wc, z.c), BF)
    for k in range(n):
        rows = back[k].reshape(z.r, z.fl, 1, z.wc, z.c).transpose(1, 0, 2, 3, 4)
        whole = lax.dynamic_update_slice_in_dim(whole, rows, me ^ k, 2)
    return whole.reshape(frames_in.shape), kernel_grad


def solution(mesh):
    tiles = P("tm", "space", None, None)
    return jax.shard_map(
        on_device,
        mesh=mesh,
        in_specs=(tiles,) + (P(),) * 7 + (tiles,),
        out_specs=(tiles, P(None, "tm", "space")),
        check_vma=False,
    )
```

```python
import functools

import jax
import jax.numpy as jnp
from jax import lax
from jax.experimental import pallas as pl
from jax.experimental.pallas import tpu as pltpu
from jax.sharding import PartitionSpec as P

BF = jnp.bfloat16
F32 = jnp.float32
VMEM = pl.BlockSpec(memory_space=pltpu.VMEM)
SMEM = pl.BlockSpec(memory_space=pltpu.SMEM)


def call(kernel, outs, *args, flops=0, scratch=()):
    moved = sum(a.size * a.dtype.itemsize for a in args)
    moved += sum(o.size * o.dtype.itemsize for o in outs)
    return pl.pallas_call(
        kernel,
        out_shape=tuple(outs),
        in_specs=[SMEM if a.dtype == jnp.int32 else VMEM for a in args],
        out_specs=tuple(VMEM for _ in outs),
        scratch_shapes=scratch,
        compiler_params=pltpu.CompilerParams(vmem_limit_bytes=40 * 2**20),
        cost_estimate=pl.CostEstimate(flops=flops, bytes_accessed=moved, transcendentals=0),
    )(*args)


def shape(dims, kind=BF):
    return jax.ShapeDtypeStruct(dims, kind)


def chooser(rows, cols, source):
    q = lax.broadcasted_iota(jnp.int32, (rows, cols), 0)
    m = lax.broadcasted_iota(jnp.int32, (rows, cols), 1)
    return jnp.where(source(q) == m, 1.0, 0.0).astype(BF)


def moved(matrix, rows):
    return jnp.dot(matrix, rows, preferred_element_type=F32).astype(BF)


class Sizes:
    def __init__(self, count, frames, rows, cols, chans):
        self.n, self.fl, self.r, self.w, self.c = count, frames, rows, cols, chans
        self.f = count * frames
        self.wc = cols // count
        self.block = self.f * self.wc
        self.piece = frames * self.wc
        self.main = rows * self.piece
        self.sides = 2 * rows * frames


def pack_kernel(z, halo, me_ref, x_ref, outs):
    me = me_ref[0]

    def source(q):
        k = q // z.piece
        f = q % z.piece // z.wc
        return f * z.w + (me ^ k) * z.wc + q % z.wc

    matrix = chooser(z.n * z.piece, z.fl * z.w, source)
    for r in range(z.r):
        rows = x_ref[:, r].reshape(z.fl * z.w, z.c)
        cut = moved(matrix, rows)
        for k in range(z.n):
            outs[k, r * z.piece : (r + 1) * z.piece] = cut[k * z.piece : (k + 1) * z.piece]
    if not halo:
        return

    def edge(q):
        k = q // z.sides
        side = q % z.sides // (z.r * z.fl)
        r = q % (z.r * z.fl) // z.fl
        f = q % z.fl
        col = (me ^ k) * z.wc - 1 + side * (z.wc + 1)
        inside = (col >= 0) & (col < z.w)
        return jnp.where(inside, (f * z.r + r) * z.w + col, -1)

    total = z.fl * z.r * z.w
    cut = moved(chooser(z.n * z.sides, total, edge), x_ref[...].reshape(total, z.c))
    for k in range(z.n):
        outs[k, z.main : z.main + z.sides] = cut[k * z.sides : (k + 1) * z.sides]


def gather_matrix(z, me):
    def source(q):
        s = q % z.f // z.fl
        return ((me ^ s) * z.fl + q % z.fl) * z.wc + q // z.f

    return chooser(z.block, z.block, source)


def assemble_kernel(z, me_ref, parts, out, top, bottom):
    me = me_ref[0]
    matrix = gather_matrix(z, me)

    def edge(q):
        head = q // z.f
        s = q % z.f // z.fl
        return ((me ^ s) * 2 * z.r + head) * z.fl + q % z.fl

    count = z.n * z.sides
    tails = jnp.concatenate([parts[k, z.main : z.main + z.sides] for k in range(z.n)], axis=0)
    tails = moved(chooser(count, count, edge), tails)
    last = z.f + z.block
    for r in range(z.r):
        cut = slice(r * z.piece, (r + 1) * z.piece)
        rows = jnp.concatenate([parts[k, cut] for k in range(z.n)], axis=0)
        rows = moved(matrix, rows)
        left = tails[r * z.f : (r + 1) * z.f]
        right = tails[(z.r + r) * z.f : (z.r + r + 1) * z.f]
        copies = [out.at[r]]
        if r == 0:
            copies.append(top)
        if r == z.r - 1:
            copies.append(bottom)
        for ref in copies:
            ref[0 : z.f] = left
            ref[z.f : last] = rows
            ref[last : last + z.f] = right


def inner_kernel(z, x_ref, w_ref, out):
    for r in range(z.r):
        total = jnp.zeros((z.block, z.c), F32)
        for di in range(3):
            if not 0 <= r + di - 1 < z.r:
                continue
            for dj in range(3):
                total += jnp.dot(
                    x_ref[r + di - 1, dj * z.f : dj * z.f + z.block],
                    w_ref[di, dj],
                    preferred_element_type=F32,
                )
        out[r] = total


def act_kernel(z, part_ref, up_ref, down_ref, w_ref, out):
    frame = lax.broadcasted_iota(jnp.int32, (z.block, z.c), 0) % z.f
    for r in range(z.r):
        total = part_ref[r]
        for edge, di, ref in ((0, 0, up_ref), (z.r - 1, 2, down_ref)):
            if r == edge:
                for dj in range(3):
                    total += jnp.dot(
                        ref[dj * z.f : dj * z.f + z.block],
                        w_ref[di, dj],
                        preferred_element_type=F32,
                    )
        act = (total / (1.0 + jnp.exp(-total))).astype(BF)
        out[r, :, 0 : z.c] = act
        wide = act.astype(F32)
        for k in (1, 2):
            late = jnp.where(frame >= k, pltpu.roll(wide, k, 0), 0.0)
            out[r, :, k * z.c : (k + 1) * z.c] = late.astype(BF)


def main_kernel(z, x_ref, act_ref, t_ref, gain_ref, q_ref, k_ref, v_ref, o_ref, out):
    a = lax.broadcasted_iota(jnp.int32, (z.block, z.block), 0)
    b = lax.broadcasted_iota(jnp.int32, (z.block, z.block), 1)
    allowed = (a // z.f == b // z.f) & (b % z.f <= a % z.f)
    scale = float(z.c) ** -0.5
    back = chooser(z.block, z.block, lambda q: q % z.wc * z.f + q // z.wc)
    gain = gain_ref[...]
    for r in range(z.r):
        temporal = jnp.dot(act_ref[r], t_ref[...], preferred_element_type=F32)
        hidden = (x_ref[r, z.f : z.f + z.block].astype(F32) + temporal).astype(BF)
        wide = hidden.astype(F32)
        mean = jnp.mean(wide * wide, axis=1, keepdims=True)
        normed = (wide / jnp.sqrt(mean + 1e-06) * gain).astype(BF)
        query = jnp.dot(normed, q_ref[...], preferred_element_type=F32).astype(BF)
        key = jnp.dot(normed, k_ref[...], preferred_element_type=F32).astype(BF)
        value = jnp.dot(normed, v_ref[...], preferred_element_type=F32).astype(BF)
        scores = lax.dot_general(
            query, key, (((1,), (1,)), ((), ())), preferred_element_type=F32
        )
        scores = jnp.where(allowed, scores * scale, -1e30)
        top = jnp.max(scores, axis=1, keepdims=True)
        expon = jnp.where(allowed, jnp.exp(scores - top), 0.0)
        total = jnp.sum(expon, axis=1, keepdims=True)
        mixed = jnp.dot(expon.astype(BF), value, preferred_element_type=F32)
        attended = (mixed / total).astype(BF)
        encoded = wide + jnp.dot(attended, o_ref[...], preferred_element_type=F32)
        encoded = moved(back, encoded.astype(BF))
        for i in range(z.n):
            out[i, r] = encoded[i * z.piece : (i + 1) * z.piece]


def grad_kernel(z, width, me_ref, parts, act_ref, keep, send, cot):
    matrix = gather_matrix(z, me_ref[0])
    mine = me_ref[1] == 0
    for r in range(z.r):
        cut = slice(r * z.piece, (r + 1) * z.piece)
        rows = jnp.concatenate([parts[k, cut] for k in range(z.n)], axis=0)
        cot[r * z.block : (r + 1) * z.block] = moved(matrix, rows)
    flat = cot[...]
    for k in range(3):
        lanes = slice(k * z.c, (k + 1) * z.c)
        grad = lax.dot_general(
            flat,
            act_ref[:, :, lanes].reshape(z.r * z.block, z.c),
            (((0,), (0,)), ((), ())),
            preferred_element_type=F32,
        )
        for i in range(z.c // (2 * width)):
            low = grad[2 * i * width : (2 * i + 1) * width]
            high = grad[(2 * i + 1) * width : (2 * i + 2) * width]
            keep[i * width : (i + 1) * width, lanes] = jnp.where(mine, low, high)
            send[i * width : (i + 1) * width, lanes] = jnp.where(mine, high, low).astype(BF)


def split_kernel(z, keep_ref, got_ref, out):
    wide = z.c // z.n
    for tap in range(3):
        lanes = slice(tap * z.c, (tap + 1) * z.c)
        total = (keep_ref[:, lanes] + got_ref[:, lanes].astype(F32)).astype(BF)
        for k in range(z.n):
            out[k, :, tap * wide : (tap + 1) * wide] = total[:, k * wide : (k + 1) * wide]


def load_kernel(count, after_ref, *refs):
    sources, places, sem = refs[:count], refs[count : 2 * count], refs[2 * count]
    copies = [
        pltpu.make_async_copy(source, place, sem.at[i])
        for i, (source, place) in enumerate(zip(sources, places))
    ]
    for copy in copies:
        copy.start()
    for copy in copies:
        copy.wait()


def swap(value, axis, k):
    count = lax.axis_size(axis)
    return lax.ppermute(value, axis, [(i, i ^ k) for i in range(count)])


def on_device(frames_in, spatial, temporal, gain, q_w, k_w, v_w, o_w, cotangent):
    n = lax.axis_size("tm")
    space = lax.axis_size("space")
    z = Sizes(n, *frames_in.shape)
    here = lax.axis_index("space")
    ids = jnp.stack([0 * here, here % 2]).astype(jnp.int32)
    temporal = temporal.reshape(3 * z.c, z.c)

    def exchange(value):
        return lax.all_to_all(value, "tm", 0, 0, tiled=True)

    (packed,) = call(
        functools.partial(pack_kernel, z, True),
        [shape((n, z.main + z.sides, z.c))],
        ids,
        frames_in,
    )
    got = exchange(packed)
    weights = (spatial, temporal, q_w, k_w, v_w, o_w)
    spatial, temporal, q_w, k_w, v_w, o_w = pl.pallas_call(
        functools.partial(load_kernel, len(weights)),
        out_shape=tuple(shape(w.shape) for w in weights),
        in_specs=[pl.BlockSpec(memory_space=pl.ANY)] * (1 + len(weights)),
        out_specs=tuple(VMEM for _ in weights),
        scratch_shapes=[pltpu.SemaphoreType.DMA((len(weights),))],
        compiler_params=pltpu.CompilerParams(vmem_limit_bytes=40 * 2**20),
        cost_estimate=pl.CostEstimate(flops=0, bytes_accessed=16 * 2**20, transcendentals=0),
    )(packed, *weights)
    line = z.block + 2 * z.f
    x, top, bottom = call(
        functools.partial(assemble_kernel, z),
        [shape((z.r, line, z.c)), shape((line, z.c)), shape((line, z.c))],
        ids,
        got,
    )
    up = lax.ppermute(bottom, "space", [(i, i + 1) for i in range(space - 1)])
    down = lax.ppermute(top, "space", [(i + 1, i) for i in range(space - 1)])
    (cot,) = call(
        functools.partial(pack_kernel, z, False),
        [shape((n, z.main, z.c))],
        ids,
        cotangent,
    )
    cot, x = lax.optimization_barrier((cot, x))
    cot = exchange(cot)
    one = 2 * z.r * z.block * z.c * z.c
    (inner,) = call(
        functools.partial(inner_kernel, z),
        [shape((z.r, z.block, z.c), F32)],
        x,
        spatial,
        flops=9 * one * (3 * z.r - 2) // (3 * z.r),
    )
    (acts,) = call(
        functools.partial(act_kernel, z),
        [shape((z.r, z.block, 3 * z.c))],
        inner,
        up,
        down,
        spatial,
        flops=6 * one // z.r,
    )
    width = z.c // space
    keep, send = call(
        functools.partial(grad_kernel, z, width),
        [shape((z.c // 2, 3 * z.c), F32), shape((z.c // 2, 3 * z.c))],
        ids,
        cot,
        acts,
        flops=3 * one,
        scratch=[pltpu.VMEM((z.r * z.block, z.c), BF)],
    )
    other = lax.ppermute(send, "space", [(i, i ^ 1) for i in range(space)])
    (encoded,) = call(
        functools.partial(main_kernel, z),
        [shape((n, z.r, z.piece, z.c))],
        x,
        acts,
        temporal,
        gain.reshape(1, z.c),
        q_w,
        k_w,
        v_w,
        o_w,
        flops=8 * one,
    )
    wide = z.c // n
    (pieces,) = call(
        functools.partial(split_kernel, z), [shape((n, z.c // 2, 3 * wide))], keep, other
    )
    back = exchange(encoded)
    chips = space // 2
    total = jnp.sum(exchange(pieces).astype(F32), axis=0).astype(BF)
    total = lax.all_to_all(
        total.reshape(chips, width, 3 * wide),
        "space",
        0,
        0,
        axis_index_groups=[list(range(i, space, 2)) for i in range(2)],
        tiled=True,
    )
    sums = jnp.sum(total.astype(F32), axis=0)
    kernel_grad = sums.reshape(width, 3, wide).transpose(1, 2, 0)
    whole = back.reshape(n, z.r, z.fl, z.wc, z.c).transpose(2, 1, 0, 3, 4)
    return whole.reshape(frames_in.shape), kernel_grad


def solution(mesh):
    tiles = P("tm", "space", None, None)
    return jax.shard_map(
        on_device,
        mesh=mesh,
        in_specs=(tiles,) + (P(),) * 7 + (tiles,),
        out_specs=(tiles, P(None, "tm", "space")),
        check_vma=False,
    )
```

```python
import functools

import jax
import jax.numpy as jnp
from jax import lax
from jax.experimental import pallas as pl
from jax.experimental.pallas import tpu as pltpu
from jax.sharding import PartitionSpec as P

BF = jnp.bfloat16
F32 = jnp.float32
VMEM = pl.BlockSpec(memory_space=pltpu.VMEM)


def call(kernel, outs, *args, flops=0, scratch=(), limit=16):
    moved = sum(a.size * a.dtype.itemsize for a in args)
    moved += sum(o.size * o.dtype.itemsize for o in outs)
    return pl.pallas_call(
        kernel,
        out_shape=tuple(outs),
        in_specs=[VMEM] * len(args),
        out_specs=tuple(VMEM for _ in outs),
        scratch_shapes=scratch,
        compiler_params=pltpu.CompilerParams(vmem_limit_bytes=limit * 2**20),
        cost_estimate=pl.CostEstimate(flops=flops, bytes_accessed=moved, transcendentals=0),
    )(*args)


def shape(dims, kind=BF):
    return jax.ShapeDtypeStruct(dims, kind)


def chooser(rows, cols, source):
    q = lax.broadcasted_iota(jnp.int32, (rows, cols), 0)
    m = lax.broadcasted_iota(jnp.int32, (rows, cols), 1)
    return jnp.where(source(q) == m, 1.0, 0.0).astype(BF)


def moved(matrix, rows):
    return jnp.dot(matrix, rows, preferred_element_type=F32).astype(BF)


class Sizes:
    def __init__(self, count, frames, rows, cols, chans):
        self.n, self.fl, self.r, self.w, self.c = count, frames, rows, cols, chans
        self.f = count * frames
        self.wc = cols // count
        self.block = self.f * self.wc
        self.piece = frames * self.wc
        self.main = rows * self.piece
        self.sides = 2 * rows * frames


def pack_kernel(z, halo, x_ref, *refs):
    outs, (x, sem) = refs[: z.n], refs[z.n :]
    copies = [pltpu.make_async_copy(x_ref.at[:, r], x.at[r], sem.at[r]) for r in range(z.r)]
    for copy in copies:
        copy.start()
    me = lax.axis_index("tm")

    def source(q):
        k = q // z.piece
        f = q % z.piece // z.wc
        return f * z.w + (me ^ k) * z.wc + q % z.wc

    def edge(r, q):
        k = q // z.sides
        side = q % z.sides // (z.r * z.fl)
        row = q % (z.r * z.fl) // z.fl
        col = (me ^ k) * z.wc - 1 + side * (z.wc + 1)
        inside = (col >= 0) & (col < z.w) & (row == r)
        return jnp.where(inside, q % z.fl * z.w + col, -1)

    matrix = chooser(z.n * z.piece, z.fl * z.w, source)
    if halo:
        edges = [chooser(z.n * z.sides, z.fl * z.w, functools.partial(edge, r)) for r in range(z.r)]
        tails = jnp.zeros((z.n * z.sides, z.c), F32)
    for r in range(z.r):
        copies[r].wait()
        rows = x[r].reshape(z.fl * z.w, z.c)
        cut = moved(matrix, rows)
        for k in range(z.n):
            outs[k][r * z.piece : (r + 1) * z.piece] = cut[k * z.piece : (k + 1) * z.piece]
        if halo:
            tails += jnp.dot(edges[r], rows, preferred_element_type=F32)
    if halo:
        tails = tails.astype(BF)
        for k in range(z.n):
            outs[k][z.main : z.main + z.sides] = tails[k * z.sides : (k + 1) * z.sides]


def gather_matrix(z, me):
    def source(q):
        s = q % z.f // z.fl
        return ((me ^ s) * z.fl + q % z.fl) * z.wc + q // z.f

    return chooser(z.block, z.block, source)


def assemble_kernel(z, *refs):
    parts, (out, top, bottom) = refs[: z.n], refs[z.n :]
    me = lax.axis_index("tm")
    matrix = gather_matrix(z, me)

    def edge(q):
        head = q // z.f
        s = q % z.f // z.fl
        return ((me ^ s) * 2 * z.r + head) * z.fl + q % z.fl

    count = z.n * z.sides
    tails = jnp.concatenate([p[z.main : z.main + z.sides] for p in parts], axis=0)
    tails = moved(chooser(count, count, edge), tails)
    last = z.f + z.block
    for r in range(z.r):
        rows = jnp.concatenate([p[r * z.piece : (r + 1) * z.piece] for p in parts], axis=0)
        rows = moved(matrix, rows)
        left = tails[r * z.f : (r + 1) * z.f]
        right = tails[(z.r + r) * z.f : (z.r + r + 1) * z.f]
        copies = [out.at[r]]
        if r == 0:
            copies.append(top)
        if r == z.r - 1:
            copies.append(bottom)
        for ref in copies:
            ref[0 : z.f] = left
            ref[z.f : last] = rows
            ref[last : last + z.f] = right


def inner_kernel(z, x_ref, w_ref, out):
    for r in range(z.r):
        total = jnp.zeros((z.block, z.c), F32)
        for di in range(3):
            if not 0 <= r + di - 1 < z.r:
                continue
            for dj in range(3):
                total += jnp.dot(
                    x_ref[r + di - 1, dj * z.f : dj * z.f + z.block],
                    w_ref[di, dj],
                    preferred_element_type=F32,
                )
        out[r] = total


def act_kernel(z, part_ref, up_ref, down_ref, w_ref, out):
    frame = lax.broadcasted_iota(jnp.int32, (z.block, z.c), 0) % z.f
    for r in range(z.r):
        total = part_ref[r]
        for edge, di, ref in ((0, 0, up_ref), (z.r - 1, 2, down_ref)):
            if r == edge:
                for dj in range(3):
                    total += jnp.dot(
                        ref[dj * z.f : dj * z.f + z.block],
                        w_ref[di, dj],
                        preferred_element_type=F32,
                    )
        act = (total / (1.0 + jnp.exp(-total))).astype(BF)
        out[r, :, 0 : z.c] = act
        wide = act.astype(F32)
        for k in (1, 2):
            late = jnp.where(frame >= k, pltpu.roll(wide, k, 0), 0.0)
            out[r, :, k * z.c : (k + 1) * z.c] = late.astype(BF)


def norm_kernel(z, x_ref, act_ref, t_ref, gain_ref, hidden_ref, normed_ref):
    gain = gain_ref[...]
    for r in range(z.r):
        temporal = jnp.dot(act_ref[r], t_ref[...], preferred_element_type=F32)
        hidden = (x_ref[r, z.f : z.f + z.block].astype(F32) + temporal).astype(BF)
        wide = hidden.astype(F32)
        mean = jnp.mean(wide * wide, axis=1, keepdims=True)
        hidden_ref[r] = hidden
        normed_ref[r] = (wide * (1.0 / jnp.sqrt(mean + 1e-06)) * gain).astype(BF)


def attend_kernel(z, hidden_ref, normed_ref, q_ref, k_ref, v_ref, o_ref, *outs):
    me = lax.axis_index("tm")
    a = lax.broadcasted_iota(jnp.int32, (z.block, z.block), 0)
    b = lax.broadcasted_iota(jnp.int32, (z.block, z.block), 1)
    allowed = (a // z.f == b // z.f) & (b % z.f <= a % z.f)
    scale = float(z.c) ** -0.5

    def source(q):
        t = ((me ^ (q // z.piece)) * z.fl) + q % z.piece // z.wc
        return q % z.wc * z.f + t

    back = chooser(z.block, z.block, source)
    held = {}

    def project(r):
        rows = normed_ref[r]
        held["q", r], held["k", r], held["v", r] = (
            jnp.dot(rows, w[...], preferred_element_type=F32).astype(BF)
            for w in (q_ref, k_ref, v_ref)
        )

    def score(r):
        held["s", r] = lax.dot_general(
            held.pop(("q", r)),
            held.pop(("k", r)),
            (((1,), (1,)), ((), ())),
            preferred_element_type=F32,
        )

    def weigh(r):
        scores = jnp.where(allowed, held.pop(("s", r)) * scale, -1e30)
        top = jnp.max(scores, axis=1, keepdims=True)
        expon = jnp.where(allowed, jnp.exp(scores - top), 0.0)
        held["t", r] = 1.0 / jnp.sum(expon, axis=1, keepdims=True)
        held["p", r] = expon.astype(BF)

    def mix(r):
        mixed = jnp.dot(held.pop(("p", r)), held.pop(("v", r)), preferred_element_type=F32)
        held["a", r] = (mixed * held.pop(("t", r))).astype(BF)

    def finish(r):
        encoded = hidden_ref[r].astype(F32) + jnp.dot(
            held.pop(("a", r)), o_ref[...], preferred_element_type=F32
        )
        held["e", r] = encoded.astype(BF)

    def spread(r):
        encoded = moved(back, held.pop(("e", r)))
        for k in range(z.n):
            outs[k][r] = encoded[k * z.piece : (k + 1) * z.piece]

    stages = (project, score, weigh, mix, finish, spread)
    for step in range(z.r + len(stages) - 1):
        for late, stage in reversed(list(enumerate(stages))):
            if 0 <= step - late < z.r:
                stage(step - late)


def grad_kernel(z, width, *refs):
    parts, (act_ref, keep, send, cot) = refs[: z.n], refs[z.n :]
    matrix = gather_matrix(z, lax.axis_index("tm"))
    mine = lax.axis_index("space") % 2 == 0
    for r in range(z.r):
        rows = jnp.concatenate([p[r * z.piece : (r + 1) * z.piece] for p in parts], axis=0)
        cot[r * z.block : (r + 1) * z.block] = moved(matrix, rows)
    flat = cot[...]
    for k in range(3):
        lanes = slice(k * z.c, (k + 1) * z.c)
        grad = lax.dot_general(
            flat,
            act_ref[:, :, lanes].reshape(z.r * z.block, z.c),
            (((0,), (0,)), ((), ())),
            preferred_element_type=F32,
        )
        for i in range(z.c // (2 * width)):
            low = grad[2 * i * width : (2 * i + 1) * width]
            high = grad[(2 * i + 1) * width : (2 * i + 2) * width]
            keep[i * width : (i + 1) * width, lanes] = jnp.where(mine, low, high)
            send[i * width : (i + 1) * width, lanes] = jnp.where(mine, high, low).astype(BF)


def split_kernel(z, keep_ref, got_ref, *outs):
    me = lax.axis_index("tm")
    wide = z.c // z.n
    for tap in range(3):
        place = slice(tap * wide, (tap + 1) * wide)
        if wide % 128 == 0:
            for k in range(z.n):
                lanes = pl.ds(pl.multiple_of(tap * z.c + (me ^ k) * wide, 128), wide)
                total = keep_ref[:, lanes] + got_ref[:, lanes].astype(F32)
                outs[k][:, place] = total.astype(outs[k].dtype)
            continue
        lanes = slice(tap * z.c, (tap + 1) * z.c)
        total = keep_ref[:, lanes] + got_ref[:, lanes].astype(F32)
        for k in range(z.n):
            cut = total[:, 0:wide]
            for i in range(1, z.n):
                cut = jnp.where((me ^ k) == i, total[:, i * wide : (i + 1) * wide], cut)
            outs[k][:, place] = cut.astype(outs[k].dtype)


def swap(value, axis, k):
    count = lax.axis_size(axis)
    return lax.ppermute(value, axis, [(i, i ^ k) for i in range(count)])


def load_kernel(count, after_ref, *refs):
    sources, places, sem = refs[:count], refs[count : 2 * count], refs[2 * count]
    copies = [
        pltpu.make_async_copy(source, place, sem.at[i])
        for i, (source, place) in enumerate(zip(sources, places))
    ]
    for copy in copies:
        copy.start()
    for copy in copies:
        copy.wait()


def write_kernel(z, k, piece_ref, *refs):
    out, sem = refs[-2:]
    first = pl.multiple_of((lax.axis_index("tm") ^ k) * z.wc, z.wc)
    copies = [
        pltpu.make_async_copy(
            piece_ref.at[r], out.at[:, r, pl.ds(first, z.wc)], sem.at[r]
        )
        for r in range(z.r)
    ]
    for copy in copies:
        copy.start()
    for copy in copies:
        copy.wait()


def write(z, k, piece, *whole):
    return pl.pallas_call(
        functools.partial(write_kernel, z, k),
        out_shape=shape((z.fl, z.r, z.w, z.c)),
        in_specs=[pl.BlockSpec(memory_space=pl.ANY)] * (1 + len(whole)),
        out_specs=pl.BlockSpec(memory_space=pl.ANY),
        input_output_aliases={1: 0} if whole else {},
        scratch_shapes=[pltpu.SemaphoreType.DMA((z.r,))],
        cost_estimate=pl.CostEstimate(
            flops=0, bytes_accessed=4 * z.main * z.c, transcendentals=0
        ),
    )(piece.reshape(z.r, z.fl, z.wc, z.c), *whole)


def on_device(frames_in, spatial, temporal, gain, q_w, k_w, v_w, o_w, cotangent):
    n = lax.axis_size("tm")
    space = lax.axis_size("space")
    z = Sizes(n, *frames_in.shape)
    me = lax.axis_index("tm")
    here = lax.axis_index("space")
    one = 2 * z.r * z.block * z.c * z.c
    others = sorted(range(1, n), key=lambda k: -k.bit_count())

    def pack(value, halo):
        rows = z.main + (z.sides if halo else 0)
        return pl.pallas_call(
            functools.partial(pack_kernel, z, halo),
            out_shape=tuple([shape((rows, z.c))] * n),
            in_specs=[pl.BlockSpec(memory_space=pltpu.HBM)],
            out_specs=tuple([VMEM] * n),
            scratch_shapes=[
                pltpu.VMEM((z.r, z.fl, z.w, z.c), BF),
                pltpu.SemaphoreType.DMA((z.r,)),
            ],
            compiler_params=pltpu.CompilerParams(vmem_limit_bytes=16 * 2**20),
            cost_estimate=pl.CostEstimate(flops=one, bytes_accessed=2**22, transcendentals=0),
        )(value)

    def exchange(pieces):
        pieces = list(pieces)
        for k in others:
            pieces[k] = swap(pieces[k], "tm", k)
        return pieces

    packed = pack(frames_in, True)
    got = exchange(packed)
    weights = (spatial, temporal.reshape(3 * z.c, z.c), q_w, k_w, v_w, o_w)
    spatial, temporal, q_w, k_w, v_w, o_w = pl.pallas_call(
        functools.partial(load_kernel, len(weights)),
        out_shape=tuple(shape(w.shape) for w in weights),
        in_specs=[pl.BlockSpec(memory_space=pl.ANY)] + [pl.BlockSpec(memory_space=pltpu.HBM)] * len(weights),
        out_specs=tuple(VMEM for _ in weights),
        scratch_shapes=[pltpu.SemaphoreType.DMA((len(weights),))],
        compiler_params=pltpu.CompilerParams(vmem_limit_bytes=16 * 2**20),
        cost_estimate=pl.CostEstimate(flops=0, bytes_accessed=16 * 2**20, transcendentals=0),
    )(packed[0], *weights)
    cot = pack(cotangent, False)
    tied = lax.optimization_barrier((*cot, *(got[k] for k in others[1:])))
    cot = exchange(tied[:n])
    for k, piece in zip(others[1:], tied[n:]):
        got[k] = piece
    line = z.block + 2 * z.f
    x, top, bottom = call(
        functools.partial(assemble_kernel, z),
        [shape((z.r, line, z.c)), shape((line, z.c)), shape((line, z.c))],
        *got,
    )
    up = lax.ppermute(bottom, "space", [(i, i + 1) for i in range(space - 1)])
    down = lax.ppermute(top, "space", [(i + 1, i) for i in range(space - 1)])
    (inner,) = call(
        functools.partial(inner_kernel, z),
        [shape((z.r, z.block, z.c), F32)],
        x,
        spatial,
        flops=9 * one * (3 * z.r - 2) // (3 * z.r),
    )
    (acts,) = call(
        functools.partial(act_kernel, z),
        [shape((z.r, z.block, 3 * z.c))],
        inner,
        up,
        down,
        spatial,
        flops=6 * one // z.r,
    )
    width = z.c // space
    keep, send = call(
        functools.partial(grad_kernel, z, width),
        [shape((z.c // 2, 3 * z.c), F32), shape((z.c // 2, 3 * z.c))],
        *cot,
        acts,
        flops=3 * one,
        scratch=[pltpu.VMEM((z.r * z.block, z.c), BF)],
    )
    other = swap(send, "space", 1)
    hidden, normed = call(
        functools.partial(norm_kernel, z),
        [shape((z.r, z.block, z.c))] * 2,
        x,
        acts,
        temporal,
        gain.reshape(1, z.c),
        flops=3 * one,
    )
    wide = z.c // n
    pieces = call(
        functools.partial(split_kernel, z),
        [shape((z.c // 2, 3 * wide), F32)] + [shape((z.c // 2, 3 * wide))] * (n - 1),
        keep,
        other,
    )
    normed, *pieces = lax.optimization_barrier((normed, *pieces))
    pieces = exchange(pieces)
    encoded = call(
        functools.partial(attend_kernel, z),
        [shape((z.r, z.piece, z.c))] * n,
        hidden,
        normed,
        q_w,
        k_w,
        v_w,
        o_w,
        flops=5 * one,
    )
    total = sum(piece.astype(F32) for piece in pieces)
    chips = space // 2
    total = total.reshape(chips, width, 3 * wide)
    sums = lax.dynamic_index_in_dim(total, here // 2, 0, False)
    total = total.astype(BF)
    for k in range(1, chips):
        mine = lax.dynamic_index_in_dim(total, here // 2 ^ k, 0, False)
        sums = sums + swap(mine, "space", 2 * k).astype(F32)
    kernel_grad = sums.reshape(width, 3, wide).transpose(1, 2, 0)
    back = exchange(encoded)
    if z.wc % 16 == 0:
        whole = write(z, 0, back[0])
        for k in reversed(others):
            whole = write(z, k, back[k], whole)
    else:
        whole = jnp.zeros((z.fl, z.r, n, z.wc, z.c), BF)
        for k in range(n):
            rows = back[k].reshape(z.r, z.fl, 1, z.wc, z.c).transpose(1, 0, 2, 3, 4)
            whole = lax.dynamic_update_slice_in_dim(whole, rows, me ^ k, 2)
    return whole.reshape(frames_in.shape), kernel_grad


def solution(mesh):
    tiles = P("tm", "space", None, None)
    return jax.shard_map(
        on_device,
        mesh=mesh,
        in_specs=(tiles,) + (P(),) * 7 + (tiles,),
        out_specs=(tiles, P(None, "tm", "space")),
        check_vma=False,
    )
```

```python
import functools

import jax
import jax.numpy as jnp
from jax import lax
from jax.experimental import pallas as pl
from jax.experimental.pallas import tpu as pltpu
from jax.sharding import PartitionSpec as P

BF = jnp.bfloat16
F32 = jnp.float32
VMEM = pl.BlockSpec(memory_space=pltpu.VMEM)


def call(kernel, outs, *args, flops=0, scratch=(), limit=16):
    moved = sum(a.size * a.dtype.itemsize for a in args)
    moved += sum(o.size * o.dtype.itemsize for o in outs)
    return pl.pallas_call(
        kernel,
        out_shape=tuple(outs),
        in_specs=[VMEM] * len(args),
        out_specs=tuple(VMEM for _ in outs),
        scratch_shapes=scratch,
        compiler_params=pltpu.CompilerParams(vmem_limit_bytes=limit * 2**20),
        cost_estimate=pl.CostEstimate(flops=flops, bytes_accessed=moved, transcendentals=0),
    )(*args)


def shape(dims, kind=BF):
    return jax.ShapeDtypeStruct(dims, kind)


def chooser(rows, cols, source):
    q = lax.broadcasted_iota(jnp.int32, (rows, cols), 0)
    m = lax.broadcasted_iota(jnp.int32, (rows, cols), 1)
    return jnp.where(source(q) == m, 1.0, 0.0).astype(BF)


def moved(matrix, rows):
    return jnp.dot(matrix, rows, preferred_element_type=F32).astype(BF)


class Sizes:
    def __init__(self, count, frames, rows, cols, chans):
        self.n, self.fl, self.r, self.w, self.c = count, frames, rows, cols, chans
        self.f = count * frames
        self.wc = cols // count
        self.block = self.f * self.wc
        self.piece = frames * self.wc
        self.main = rows * self.piece
        self.sides = 2 * rows * frames


def pack_kernel(z, halo, x_ref, *outs):
    me = lax.axis_index("tm")

    def source(q):
        k = q // z.piece
        f = q % z.piece // z.wc
        return f * z.w + (me ^ k) * z.wc + q % z.wc

    def edge(r, q):
        k = q // z.sides
        side = q % z.sides // (z.r * z.fl)
        row = q % (z.r * z.fl) // z.fl
        col = (me ^ k) * z.wc - 1 + side * (z.wc + 1)
        inside = (col >= 0) & (col < z.w) & (row == r)
        return jnp.where(inside, q % z.fl * z.w + col, -1)

    matrix = chooser(z.n * z.piece, z.fl * z.w, source)
    if halo:
        edges = [chooser(z.n * z.sides, z.fl * z.w, functools.partial(edge, r)) for r in range(z.r)]
        tails = jnp.zeros((z.n * z.sides, z.c), F32)
    for r in range(z.r):
        rows = x_ref[:, r].reshape(z.fl * z.w, z.c)
        cut = moved(matrix, rows)
        for k in range(z.n):
            outs[k][r * z.piece : (r + 1) * z.piece] = cut[k * z.piece : (k + 1) * z.piece]
        if halo:
            tails += jnp.dot(edges[r], rows, preferred_element_type=F32)
    if halo:
        tails = tails.astype(BF)
        for k in range(z.n):
            outs[k][z.main : z.main + z.sides] = tails[k * z.sides : (k + 1) * z.sides]


def gather_matrix(z, me):
    def source(q):
        s = q % z.f // z.fl
        return ((me ^ s) * z.fl + q % z.fl) * z.wc + q // z.f

    return chooser(z.block, z.block, source)


def assemble_kernel(z, *refs):
    parts, (out, top, bottom) = refs[: z.n], refs[z.n :]
    me = lax.axis_index("tm")
    matrix = gather_matrix(z, me)

    def edge(q):
        head = q // z.f
        s = q % z.f // z.fl
        return ((me ^ s) * 2 * z.r + head) * z.fl + q % z.fl

    count = z.n * z.sides
    tails = jnp.concatenate([p[z.main : z.main + z.sides] for p in parts], axis=0)
    tails = moved(chooser(count, count, edge), tails)
    last = z.f + z.block
    for r in range(z.r):
        rows = jnp.concatenate([p[r * z.piece : (r + 1) * z.piece] for p in parts], axis=0)
        rows = moved(matrix, rows)
        left = tails[r * z.f : (r + 1) * z.f]
        right = tails[(z.r + r) * z.f : (z.r + r + 1) * z.f]
        copies = [out.at[r]]
        if r == 0:
            copies.append(top)
        if r == z.r - 1:
            copies.append(bottom)
        for ref in copies:
            ref[0 : z.f] = left
            ref[z.f : last] = rows
            ref[last : last + z.f] = right


def inner_kernel(z, x_ref, w_ref, out):
    for r in range(z.r):
        total = jnp.zeros((z.block, z.c), F32)
        for di in range(3):
            if not 0 <= r + di - 1 < z.r:
                continue
            for dj in range(3):
                total += jnp.dot(
                    x_ref[r + di - 1, dj * z.f : dj * z.f + z.block],
                    w_ref[di, dj],
                    preferred_element_type=F32,
                )
        out[r] = total


def act_kernel(z, part_ref, up_ref, down_ref, w_ref, out):
    frame = lax.broadcasted_iota(jnp.int32, (z.block, z.c), 0) % z.f
    for r in range(z.r):
        total = part_ref[r]
        for edge, di, ref in ((0, 0, up_ref), (z.r - 1, 2, down_ref)):
            if r == edge:
                for dj in range(3):
                    total += jnp.dot(
                        ref[dj * z.f : dj * z.f + z.block],
                        w_ref[di, dj],
                        preferred_element_type=F32,
                    )
        act = (total / (1.0 + jnp.exp(-total))).astype(BF)
        out[r, :, 0 : z.c] = act
        wide = act.astype(F32)
        for k in (1, 2):
            late = jnp.where(frame >= k, pltpu.roll(wide, k, 0), 0.0)
            out[r, :, k * z.c : (k + 1) * z.c] = late.astype(BF)


def norm_kernel(z, x_ref, act_ref, t_ref, gain_ref, hidden_ref, normed_ref):
    gain = gain_ref[...]
    for r in range(z.r):
        temporal = jnp.dot(act_ref[r], t_ref[...], preferred_element_type=F32)
        hidden = (x_ref[r, z.f : z.f + z.block].astype(F32) + temporal).astype(BF)
        wide = hidden.astype(F32)
        mean = jnp.mean(wide * wide, axis=1, keepdims=True)
        hidden_ref[r] = hidden
        normed_ref[r] = (wide * (1.0 / jnp.sqrt(mean + 1e-06)) * gain).astype(BF)


def attend_kernel(z, hidden_ref, normed_ref, q_ref, k_ref, v_ref, o_ref, *outs):
    me = lax.axis_index("tm")
    a = lax.broadcasted_iota(jnp.int32, (z.block, z.block), 0)
    b = lax.broadcasted_iota(jnp.int32, (z.block, z.block), 1)
    allowed = (a // z.f == b // z.f) & (b % z.f <= a % z.f)
    scale = float(z.c) ** -0.5

    def source(q):
        t = ((me ^ (q // z.piece)) * z.fl) + q % z.piece // z.wc
        return q % z.wc * z.f + t

    back = chooser(z.block, z.block, source)
    held = {}

    def project(r):
        rows = normed_ref[r]
        held["q", r], held["k", r], held["v", r] = (
            jnp.dot(rows, w[...], preferred_element_type=F32).astype(BF)
            for w in (q_ref, k_ref, v_ref)
        )

    def score(r):
        held["s", r] = lax.dot_general(
            held.pop(("q", r)),
            held.pop(("k", r)),
            (((1,), (1,)), ((), ())),
            preferred_element_type=F32,
        )

    def weigh(r):
        scores = jnp.where(allowed, held.pop(("s", r)) * scale, -1e30)
        top = jnp.max(scores, axis=1, keepdims=True)
        expon = jnp.where(allowed, jnp.exp(scores - top), 0.0)
        held["t", r] = 1.0 / jnp.sum(expon, axis=1, keepdims=True)
        held["p", r] = expon.astype(BF)

    def mix(r):
        mixed = jnp.dot(held.pop(("p", r)), held.pop(("v", r)), preferred_element_type=F32)
        held["a", r] = (mixed * held.pop(("t", r))).astype(BF)

    def finish(r):
        encoded = hidden_ref[r].astype(F32) + jnp.dot(
            held.pop(("a", r)), o_ref[...], preferred_element_type=F32
        )
        held["e", r] = encoded.astype(BF)

    def spread(r):
        encoded = moved(back, held.pop(("e", r)))
        for k in range(z.n):
            outs[k][r] = encoded[k * z.piece : (k + 1) * z.piece]

    stages = (project, score, weigh, mix, finish, spread)
    for step in range(z.r + len(stages) - 1):
        for late, stage in reversed(list(enumerate(stages))):
            if 0 <= step - late < z.r:
                stage(step - late)


def grad_kernel(z, width, *refs):
    parts, (act_ref, keep, send, cot) = refs[: z.n], refs[z.n :]
    matrix = gather_matrix(z, lax.axis_index("tm"))
    mine = lax.axis_index("space") % 2 == 0
    for r in range(z.r):
        rows = jnp.concatenate([p[r * z.piece : (r + 1) * z.piece] for p in parts], axis=0)
        cot[r * z.block : (r + 1) * z.block] = moved(matrix, rows)
    flat = cot[...]
    for k in range(3):
        lanes = slice(k * z.c, (k + 1) * z.c)
        grad = lax.dot_general(
            flat,
            act_ref[:, :, lanes].reshape(z.r * z.block, z.c),
            (((0,), (0,)), ((), ())),
            preferred_element_type=F32,
        )
        for i in range(z.c // (2 * width)):
            low = grad[2 * i * width : (2 * i + 1) * width]
            high = grad[(2 * i + 1) * width : (2 * i + 2) * width]
            keep[i * width : (i + 1) * width, lanes] = jnp.where(mine, low, high)
            send[i * width : (i + 1) * width, lanes] = jnp.where(mine, high, low).astype(BF)


def split_kernel(z, keep_ref, got_ref, *outs):
    me = lax.axis_index("tm")
    wide = z.c // z.n
    for tap in range(3):
        place = slice(tap * wide, (tap + 1) * wide)
        if wide % 128 == 0:
            for k in range(z.n):
                lanes = pl.ds(pl.multiple_of(tap * z.c + (me ^ k) * wide, 128), wide)
                total = keep_ref[:, lanes] + got_ref[:, lanes].astype(F32)
                outs[k][:, place] = total.astype(outs[k].dtype)
            continue
        lanes = slice(tap * z.c, (tap + 1) * z.c)
        total = keep_ref[:, lanes] + got_ref[:, lanes].astype(F32)
        for k in range(z.n):
            cut = total[:, 0:wide]
            for i in range(1, z.n):
                cut = jnp.where((me ^ k) == i, total[:, i * wide : (i + 1) * wide], cut)
            outs[k][:, place] = cut.astype(outs[k].dtype)


def swap(value, axis, k):
    count = lax.axis_size(axis)
    return lax.ppermute(value, axis, [(i, i ^ k) for i in range(count)])


def load_kernel(count, after_ref, *refs):
    sources, places, sem = refs[:count], refs[count : 2 * count], refs[2 * count]
    copies = [
        pltpu.make_async_copy(source, place, sem.at[i])
        for i, (source, place) in enumerate(zip(sources, places))
    ]
    for copy in copies:
        copy.start()
    for copy in copies:
        copy.wait()


def on_device(frames_in, spatial, temporal, gain, q_w, k_w, v_w, o_w, cotangent):
    n = lax.axis_size("tm")
    space = lax.axis_size("space")
    z = Sizes(n, *frames_in.shape)
    me = lax.axis_index("tm")
    here = lax.axis_index("space")
    one = 2 * z.r * z.block * z.c * z.c
    others = sorted(range(1, n), key=lambda k: -k.bit_count())

    def pack(value, halo):
        rows = z.main + (z.sides if halo else 0)
        kernel = functools.partial(pack_kernel, z, halo)
        return call(kernel, [shape((rows, z.c))] * n, value, flops=one)

    def exchange(pieces):
        pieces = list(pieces)
        for k in others:
            pieces[k] = swap(pieces[k], "tm", k)
        return pieces

    packed = pack(frames_in, True)
    got = exchange(packed)
    weights = (spatial, temporal.reshape(3 * z.c, z.c), q_w, k_w, v_w, o_w)
    spatial, temporal, q_w, k_w, v_w, o_w = pl.pallas_call(
        functools.partial(load_kernel, len(weights)),
        out_shape=tuple(shape(w.shape) for w in weights),
        in_specs=[pl.BlockSpec(memory_space=pl.ANY)] + [pl.BlockSpec(memory_space=pltpu.HBM)] * len(weights),
        out_specs=tuple(VMEM for _ in weights),
        scratch_shapes=[pltpu.SemaphoreType.DMA((len(weights),))],
        compiler_params=pltpu.CompilerParams(vmem_limit_bytes=16 * 2**20),
        cost_estimate=pl.CostEstimate(flops=0, bytes_accessed=16 * 2**20, transcendentals=0),
    )(packed[0], *weights)
    cot = pack(cotangent, False)
    tied = lax.optimization_barrier((*cot, *(got[k] for k in others[1:])))
    cot = exchange(tied[:n])
    for k, piece in zip(others[1:], tied[n:]):
        got[k] = piece
    line = z.block + 2 * z.f
    x, top, bottom = call(
        functools.partial(assemble_kernel, z),
        [shape((z.r, line, z.c)), shape((line, z.c)), shape((line, z.c))],
        *got,
    )
    up = lax.ppermute(bottom, "space", [(i, i + 1) for i in range(space - 1)])
    down = lax.ppermute(top, "space", [(i + 1, i) for i in range(space - 1)])
    (inner,) = call(
        functools.partial(inner_kernel, z),
        [shape((z.r, z.block, z.c), F32)],
        x,
        spatial,
        flops=9 * one * (3 * z.r - 2) // (3 * z.r),
    )
    (acts,) = call(
        functools.partial(act_kernel, z),
        [shape((z.r, z.block, 3 * z.c))],
        inner,
        up,
        down,
        spatial,
        flops=6 * one // z.r,
    )
    width = z.c // space
    keep, send = call(
        functools.partial(grad_kernel, z, width),
        [shape((z.c // 2, 3 * z.c), F32), shape((z.c // 2, 3 * z.c))],
        *cot,
        acts,
        flops=3 * one,
        scratch=[pltpu.VMEM((z.r * z.block, z.c), BF)],
    )
    other = swap(send, "space", 1)
    hidden, normed = call(
        functools.partial(norm_kernel, z),
        [shape((z.r, z.block, z.c))] * 2,
        x,
        acts,
        temporal,
        gain.reshape(1, z.c),
        flops=3 * one,
    )
    wide = z.c // n
    pieces = call(
        functools.partial(split_kernel, z),
        [shape((z.c // 2, 3 * wide), F32)] + [shape((z.c // 2, 3 * wide))] * (n - 1),
        keep,
        other,
    )
    normed, *pieces = lax.optimization_barrier((normed, *pieces))
    pieces = exchange(pieces)
    encoded = call(
        functools.partial(attend_kernel, z),
        [shape((z.r, z.piece, z.c))] * n,
        hidden,
        normed,
        q_w,
        k_w,
        v_w,
        o_w,
        flops=5 * one,
    )
    back = exchange(encoded)
    pieces = lax.optimization_barrier((*pieces, *encoded))[:n]
    total = sum(piece.astype(F32) for piece in pieces)
    chips = space // 2
    total = total.reshape(chips, width, 3 * wide)
    sums = lax.dynamic_index_in_dim(total, here // 2, 0, False)
    total = total.astype(BF)
    for k in range(1, chips):
        mine = lax.dynamic_index_in_dim(total, here // 2 ^ k, 0, False)
        sums = sums + swap(mine, "space", 2 * k).astype(F32)
    kernel_grad = sums.reshape(width, 3, wide).transpose(1, 2, 0)
    whole = jnp.zeros((z.fl, z.r, n, z.wc, z.c), BF)
    for k in [0] + others[::-1]:
        rows = back[k].reshape(z.r, z.fl, 1, z.wc, z.c).transpose(1, 0, 2, 3, 4)
        whole = lax.dynamic_update_slice_in_dim(whole, rows, me ^ k, 2)
    return whole.reshape(frames_in.shape), kernel_grad


def solution(mesh):
    tiles = P("tm", "space", None, None)
    return jax.shard_map(
        on_device,
        mesh=mesh,
        in_specs=(tiles,) + (P(),) * 7 + (tiles,),
        out_specs=(tiles, P(None, "tm", "space")),
        check_vma=False,
    )
```

```python
import functools

import jax
import jax.numpy as jnp
from jax import lax
from jax.experimental import pallas as pl
from jax.experimental.pallas import tpu as pltpu
from jax.sharding import PartitionSpec as P

BF = jnp.bfloat16
F32 = jnp.float32
VMEM = pl.BlockSpec(memory_space=pltpu.VMEM)


def call(kernel, outs, *args, flops=0, scratch=(), limit=16):
    moved = sum(a.size * a.dtype.itemsize for a in args)
    moved += sum(o.size * o.dtype.itemsize for o in outs)
    return pl.pallas_call(
        kernel,
        out_shape=tuple(outs),
        in_specs=[VMEM] * len(args),
        out_specs=tuple(VMEM for _ in outs),
        scratch_shapes=scratch,
        compiler_params=pltpu.CompilerParams(vmem_limit_bytes=limit * 2**20),
        cost_estimate=pl.CostEstimate(flops=flops, bytes_accessed=moved, transcendentals=0),
    )(*args)


def shape(dims, kind=BF):
    return jax.ShapeDtypeStruct(dims, kind)


def chooser(rows, cols, source):
    q = lax.broadcasted_iota(jnp.int32, (rows, cols), 0)
    m = lax.broadcasted_iota(jnp.int32, (rows, cols), 1)
    return jnp.where(source(q) == m, 1.0, 0.0).astype(BF)


def moved(matrix, rows):
    return jnp.dot(matrix, rows, preferred_element_type=F32).astype(BF)


class Sizes:
    def __init__(self, count, frames, rows, cols, chans):
        self.n, self.fl, self.r, self.w, self.c = count, frames, rows, cols, chans
        self.f = count * frames
        self.wc = cols // count
        self.block = self.f * self.wc
        self.piece = frames * self.wc
        self.main = rows * self.piece
        self.sides = 2 * rows * frames


def edge_kernel(z, x_ref, after_ref, top, bottom):
    top[...] = x_ref[:, 0].reshape(z.fl * z.w, z.c)
    bottom[...] = x_ref[:, z.r - 1].reshape(z.fl * z.w, z.c)


def pack_kernel(z, x_ref, *outs):
    me = lax.axis_index("tm")

    def source(q):
        k = q // z.piece
        f = q % z.piece // z.wc
        return f * z.w + (me ^ k) * z.wc + q % z.wc

    def edge(r, q):
        k = q // z.sides
        side = q % z.sides // (z.r * z.fl)
        row = q % (z.r * z.fl) // z.fl
        col = (me ^ k) * z.wc - 1 + side * (z.wc + 1)
        inside = (col >= 0) & (col < z.w) & (row == r)
        return jnp.where(inside, q % z.fl * z.w + col, -1)

    matrix = chooser(z.n * z.piece, z.fl * z.w, source)
    tails = jnp.zeros((z.n * z.sides, z.c), F32)
    for r in range(z.r):
        rows = x_ref[:, r].reshape(z.fl * z.w, z.c)
        cut = moved(matrix, rows)
        for k in range(z.n):
            outs[k][r * z.piece : (r + 1) * z.piece] = cut[k * z.piece : (k + 1) * z.piece]
        picked = chooser(z.n * z.sides, z.fl * z.w, functools.partial(edge, r))
        tails += jnp.dot(picked, rows, preferred_element_type=F32)
    tails = tails.astype(BF)
    for k in range(z.n):
        outs[k][z.main : z.main + z.sides] = tails[k * z.sides : (k + 1) * z.sides]


def aside(z, rows):
    count = z.fl * z.w
    left = chooser(count, count, lambda q: jnp.where(q % z.w > 0, q - 1, -1))
    right = chooser(count, count, lambda q: jnp.where(q % z.w < z.w - 1, q + 1, -1))
    return moved(left, rows), rows, moved(right, rows)


def own_inner_kernel(z, x_ref, w_ref, out, beside):
    for r in range(z.r):
        for dj, rows in enumerate(aside(z, x_ref[:, r].reshape(z.fl * z.w, z.c))):
            beside[dj, r] = rows
    for r in range(z.r):
        total = jnp.zeros((z.fl * z.w, z.c), F32)
        for di in range(3):
            if 0 <= r + di - 1 < z.r:
                for dj in range(3):
                    total += jnp.dot(
                        beside[dj, r + di - 1], w_ref[di, dj], preferred_element_type=F32
                    )
        out[r] = total


def own_act_kernel(z, part_ref, up_ref, down_ref, w_ref, out, last):
    for r in range(z.r):
        total = part_ref[r]
        for edge, di, ref in ((0, 0, up_ref), (z.r - 1, 2, down_ref)):
            if r == edge:
                for dj, rows in enumerate(aside(z, ref[...])):
                    total += jnp.dot(rows, w_ref[di, dj], preferred_element_type=F32)
        act = silu(total).reshape(z.fl, z.w, z.c)
        out[:, r] = act
        last[r] = act[z.fl - 1]


def silu(total):
    return (total / (1.0 + jnp.exp(-total))).astype(BF)


def flat(value):
    return value.reshape(-1, value.shape[-1])


def outer(left, right):
    return lax.dot_general(
        flat(left), flat(right), (((0,), (0,)), ((), ())), preferred_element_type=F32
    )


def own_grad_kernel(z, act_ref, cot_ref, out):
    for k in range(3):
        out[:, k * z.c : (k + 1) * z.c] = outer(cot_ref[k:], act_ref[: z.fl - k])


def cross_kernel(z, width, part_ref, before_ref, act_ref, cot_ref, after_ref, keep, send):
    mine = lax.axis_index("space") % 2 == 0
    for k in range(3):
        lanes = slice(k * z.c, (k + 1) * z.c)
        grad = part_ref[:, lanes]
        if k == 1:
            grad += outer(cot_ref[0], before_ref[...])
        if k == 2:
            grad += outer(cot_ref[1], before_ref[...])
            grad += outer(after_ref[...], act_ref[z.fl - 2])
        for i in range(z.c // (2 * width)):
            low = grad[2 * i * width : (2 * i + 1) * width]
            high = grad[(2 * i + 1) * width : (2 * i + 2) * width]
            keep[i * width : (i + 1) * width, lanes] = jnp.where(mine, low, high)
            send[i * width : (i + 1) * width, lanes] = jnp.where(mine, high, low).astype(BF)


def gather_matrix(z, me):
    def source(q):
        s = q % z.f // z.fl
        return ((me ^ s) * z.fl + q % z.fl) * z.wc + q // z.f

    return chooser(z.block, z.block, source)


def assemble_kernel(z, *refs):
    parts, (out, top, bottom) = refs[: z.n], refs[z.n :]
    me = lax.axis_index("tm")
    matrix = gather_matrix(z, me)

    def edge(q):
        head = q // z.f
        s = q % z.f // z.fl
        return ((me ^ s) * 2 * z.r + head) * z.fl + q % z.fl

    count = z.n * z.sides
    tails = jnp.concatenate([p[z.main : z.main + z.sides] for p in parts], axis=0)
    tails = moved(chooser(count, count, edge), tails)
    last = z.f + z.block
    for r in range(z.r):
        rows = jnp.concatenate([p[r * z.piece : (r + 1) * z.piece] for p in parts], axis=0)
        rows = moved(matrix, rows)
        left = tails[r * z.f : (r + 1) * z.f]
        right = tails[(z.r + r) * z.f : (z.r + r + 1) * z.f]
        copies = [out.at[r]]
        if r == 0:
            copies.append(top)
        if r == z.r - 1:
            copies.append(bottom)
        for ref in copies:
            ref[0 : z.f] = left
            ref[z.f : last] = rows
            ref[last : last + z.f] = right


def inner_kernel(z, x_ref, w_ref, out):
    for r in range(z.r):
        total = jnp.zeros((z.block, z.c), F32)
        for di in range(3):
            if not 0 <= r + di - 1 < z.r:
                continue
            for dj in range(3):
                total += jnp.dot(
                    x_ref[r + di - 1, dj * z.f : dj * z.f + z.block],
                    w_ref[di, dj],
                    preferred_element_type=F32,
                )
        out[r] = total


def norm_kernel(
    z, part_ref, up_ref, down_ref, w_ref, x_ref, t_ref, gain_ref, hidden_ref, normed_ref
):
    frame = lax.broadcasted_iota(jnp.int32, (z.block, z.c), 0) % z.f
    held = {}

    def activate(r):
        total = part_ref[r]
        for edge, di, ref in ((0, 0, up_ref), (z.r - 1, 2, down_ref)):
            if r == edge:
                for dj in range(3):
                    total += jnp.dot(
                        ref[dj * z.f : dj * z.f + z.block],
                        w_ref[di, dj],
                        preferred_element_type=F32,
                    )
        act = silu(total)
        wide = act.astype(F32)
        held["a", r] = [act] + [
            jnp.where(frame >= k, pltpu.roll(wide, k, 0), 0.0).astype(BF) for k in (1, 2)
        ]

    def hide(r):
        temporal = sum(
            jnp.dot(late, t_ref[k], preferred_element_type=F32)
            for k, late in enumerate(held.pop(("a", r)))
        )
        hidden = (x_ref[r, z.f : z.f + z.block].astype(F32) + temporal).astype(BF)
        hidden_ref[r] = hidden
        held["h", r] = hidden

    def norm(r):
        wide = held.pop(("h", r)).astype(F32)
        mean = jnp.mean(wide * wide, axis=1, keepdims=True)
        normed_ref[r] = (wide * (1.0 / jnp.sqrt(mean + 1e-06)) * gain_ref[...]).astype(BF)

    staged(z, (activate, hide, norm))


def staged(z, stages):
    for step in range(z.r + len(stages) - 1):
        for late, stage in reversed(list(enumerate(stages))):
            if 0 <= step - late < z.r:
                stage(step - late)


def attend_kernel(z, hidden_ref, normed_ref, q_ref, k_ref, v_ref, o_ref, *outs):
    me = lax.axis_index("tm")
    a = lax.broadcasted_iota(jnp.int32, (z.block, z.block), 0)
    b = lax.broadcasted_iota(jnp.int32, (z.block, z.block), 1)
    allowed = (a // z.f == b // z.f) & (b % z.f <= a % z.f)
    scale = float(z.c) ** -0.5

    def source(q):
        t = ((me ^ (q // z.piece)) * z.fl) + q % z.piece // z.wc
        return q % z.wc * z.f + t

    back = chooser(z.block, z.block, source)
    held = {}

    def project(r):
        rows = normed_ref[r]
        held["q", r], held["k", r], held["v", r] = (
            jnp.dot(rows, w[...], preferred_element_type=F32).astype(BF)
            for w in (q_ref, k_ref, v_ref)
        )

    def score(r):
        held["s", r] = lax.dot_general(
            held.pop(("q", r)),
            held.pop(("k", r)),
            (((1,), (1,)), ((), ())),
            preferred_element_type=F32,
        )

    def weigh(r):
        scores = jnp.where(allowed, held.pop(("s", r)) * scale, -1e30)
        top = jnp.max(scores, axis=1, keepdims=True)
        expon = jnp.where(allowed, jnp.exp(scores - top), 0.0)
        held["t", r] = 1.0 / jnp.sum(expon, axis=1, keepdims=True)
        held["p", r] = expon.astype(BF)

    def mix(r):
        mixed = jnp.dot(held.pop(("p", r)), held.pop(("v", r)), preferred_element_type=F32)
        held["a", r] = (mixed * held.pop(("t", r))).astype(BF)

    def finish(r):
        encoded = hidden_ref[r].astype(F32) + jnp.dot(
            held.pop(("a", r)), o_ref[...], preferred_element_type=F32
        )
        held["e", r] = encoded.astype(BF)

    def spread(r):
        encoded = moved(back, held.pop(("e", r)))
        for k in range(z.n):
            outs[k][r] = encoded[k * z.piece : (k + 1) * z.piece]

    staged(z, (project, score, weigh, mix, finish, spread))


def split_kernel(z, keep_ref, got_ref, *outs):
    me = lax.axis_index("tm")
    wide = z.c // z.n
    for tap in range(3):
        place = slice(tap * wide, (tap + 1) * wide)
        if wide % 128 == 0:
            for k in range(z.n):
                lanes = pl.ds(pl.multiple_of(tap * z.c + (me ^ k) * wide, 128), wide)
                total = keep_ref[:, lanes] + got_ref[:, lanes].astype(F32)
                outs[k][:, place] = total.astype(outs[k].dtype)
            continue
        lanes = slice(tap * z.c, (tap + 1) * z.c)
        total = keep_ref[:, lanes] + got_ref[:, lanes].astype(F32)
        for k in range(z.n):
            cut = total[:, 0:wide]
            for i in range(1, z.n):
                cut = jnp.where((me ^ k) == i, total[:, i * wide : (i + 1) * wide], cut)
            outs[k][:, place] = cut.astype(outs[k].dtype)


def swap(value, axis, k):
    count = lax.axis_size(axis)
    return lax.ppermute(value, axis, [(i, i ^ k) for i in range(count)])


def chip_kernel(z, width, *refs):
    parts, outs, total = refs[: z.n], refs[z.n : -1], refs[-1]
    total[...] = sum(part[...].astype(F32) for part in parts)
    chip = lax.axis_index("space") // 2
    for k, out in enumerate(outs):
        rows = pl.ds(pl.multiple_of((chip ^ k) * width, width), width)
        out[...] = total[rows].astype(out.dtype)


def sum_kernel(z, *refs):
    out, wide = refs[-1], z.c // z.n
    total = sum(part[...].astype(F32) for part in refs[:-1])
    for k in range(3):
        out[k] = total[:, k * wide : (k + 1) * wide]


def join_kernel(z, *refs):
    parts, (out, whole, sem) = refs[: z.n], refs[z.n :]
    me = lax.axis_index("tm")
    copies = []
    for f in range(z.fl):
        for k in range(z.n):
            cols = pl.ds(pl.multiple_of((me ^ k) * z.wc, z.wc), z.wc)
            whole[f, :, cols] = parts[k][:, f * z.wc : (f + 1) * z.wc]
        copies.append(pltpu.make_async_copy(whole.at[f], out.at[f], sem.at[f]))
        copies[f].start()
    for copy in copies:
        copy.wait()


def joined(z, back):
    if z.wc % 16 == 0:
        return pl.pallas_call(
            functools.partial(join_kernel, z),
            out_shape=shape((z.fl, z.r, z.w, z.c)),
            in_specs=[VMEM] * z.n,
            out_specs=pl.BlockSpec(memory_space=pl.ANY),
            scratch_shapes=[
                pltpu.VMEM((z.fl, z.r, z.w, z.c), BF),
                pltpu.SemaphoreType.DMA((z.fl,)),
            ],
            compiler_params=pltpu.CompilerParams(vmem_limit_bytes=16 * 2**20),
            cost_estimate=pl.CostEstimate(
                flops=0, bytes_accessed=8 * z.n * z.main * z.c, transcendentals=0
            ),
        )(*back)
    whole = jnp.zeros((z.fl, z.r, z.n, z.wc, z.c), BF)
    for k in range(z.n):
        rows = back[k].reshape(z.r, z.fl, 1, z.wc, z.c).transpose(1, 0, 2, 3, 4)
        whole = lax.dynamic_update_slice_in_dim(whole, rows, lax.axis_index("tm") ^ k, 2)
    return whole.reshape(z.fl, z.r, z.w, z.c)


def on_device(frames_in, spatial, temporal, gain, q_w, k_w, v_w, o_w, cotangent):
    n = lax.axis_size("tm")
    space = lax.axis_size("space")
    z = Sizes(n, *frames_in.shape)
    one = 2 * z.r * z.block * z.c * z.c
    others = sorted(range(1, n), key=lambda k: -k.bit_count())
    width, wide, chips = z.c // space, z.c // n, space // 2
    up_by_one = [(i, i + 1) for i in range(space - 1)]
    down_by_one = [(i + 1, i) for i in range(space - 1)]

    def exchange(pieces):
        pieces = list(pieces)
        for k in others:
            pieces[k] = swap(pieces[k], "tm", k)
        return pieces

    edge = shape((z.fl * z.w, z.c))
    packed = call(
        functools.partial(pack_kernel, z),
        [shape((z.main + z.sides, z.c))] * n,
        frames_in,
        flops=one // 2,
    )
    top, bottom = call(
        functools.partial(edge_kernel, z), [edge, edge], frames_in, packed[0]
    )
    got = exchange(packed)
    up = lax.ppermute(bottom, "space", up_by_one)
    down = lax.ppermute(top, "space", down_by_one)
    (own,) = call(
        functools.partial(own_inner_kernel, z),
        [shape((z.r, z.fl * z.w, z.c), F32)],
        frames_in,
        spatial,
        flops=8 * one,
        scratch=[pltpu.VMEM((3, z.r, z.fl * z.w, z.c), BF)],
    )
    own_act, last = call(
        functools.partial(own_act_kernel, z),
        [shape(frames_in.shape), shape((z.r, z.w, z.c))],
        own,
        up,
        down,
        spatial,
        flops=3 * one,
    )
    before = lax.ppermute(last, "tm", [(i, i + 1) for i in range(n - 1)])
    after = lax.ppermute(cotangent[0], "tm", [(i + 1, i) for i in range(n - 1)])
    (own_grad,) = call(
        functools.partial(own_grad_kernel, z),
        [shape((z.c, 3 * z.c), F32)],
        own_act,
        cotangent,
        flops=9 * one // 4,
    )
    line = z.block + 2 * z.f
    x, top, bottom = call(
        functools.partial(assemble_kernel, z),
        [shape((z.r, line, z.c)), shape((line, z.c)), shape((line, z.c))],
        *got,
    )
    up = lax.ppermute(bottom, "space", up_by_one)
    down = lax.ppermute(top, "space", down_by_one)
    (inner,) = call(
        functools.partial(inner_kernel, z),
        [shape((z.r, z.block, z.c), F32)],
        x,
        spatial,
        flops=9 * one * (3 * z.r - 2) // (3 * z.r),
    )
    tied = lax.optimization_barrier((before, after, inner, up, down))
    before, after, inner, up, down = tied
    keep, send = call(
        functools.partial(cross_kernel, z, width),
        [shape((z.c // 2, 3 * z.c), F32), shape((z.c // 2, 3 * z.c))],
        own_grad,
        before,
        own_act,
        cotangent,
        after,
        flops=3 * one // 4,
    )
    inner, send = lax.optimization_barrier((inner, send))
    other = swap(send, "space", 1)
    hidden, normed = call(
        functools.partial(norm_kernel, z),
        [shape((z.r, z.block, z.c))] * 2,
        inner,
        up,
        down,
        spatial,
        x,
        temporal,
        gain.reshape(1, z.c),
        flops=5 * one,
    )
    pieces = call(
        functools.partial(split_kernel, z),
        [shape((z.c // 2, 3 * wide), F32)] + [shape((z.c // 2, 3 * wide))] * (n - 1),
        keep,
        other,
    )
    normed, *pieces = lax.optimization_barrier((normed, *pieces))
    pieces = exchange(pieces)
    encoded = call(
        functools.partial(attend_kernel, z),
        [shape((z.r, z.piece, z.c))] * n,
        hidden,
        normed,
        q_w,
        k_w,
        v_w,
        o_w,
        flops=5 * one,
    )
    back = exchange(encoded)
    pieces = lax.optimization_barrier((*pieces, *encoded))[:n]
    totals = call(
        functools.partial(chip_kernel, z, width),
        [shape((width, 3 * wide), F32)] + [shape((width, 3 * wide))] * (chips - 1),
        *pieces,
        scratch=[pltpu.VMEM((z.c // 2, 3 * wide), F32)],
    )
    totals = [totals[0]] + [swap(totals[k], "space", 2 * k) for k in range(1, chips)]
    (kernel_grad,) = call(
        functools.partial(sum_kernel, z), [shape((3, width, wide), F32)], *totals
    )
    return joined(z, back), kernel_grad.transpose(0, 2, 1)


def solution(mesh):
    tiles = P("tm", "space", None, None)
    return jax.shard_map(
        on_device,
        mesh=mesh,
        in_specs=(tiles,) + (P(),) * 7 + (tiles,),
        out_specs=(tiles, P(None, "tm", "space")),
        check_vma=False,
    )
```

```python
import functools

import jax
import jax.numpy as jnp
from jax import lax
from jax.experimental import pallas as pl
from jax.experimental.pallas import tpu as pltpu
from jax.sharding import PartitionSpec as P

BF = jnp.bfloat16
F32 = jnp.float32
VMEM = pl.BlockSpec(memory_space=pltpu.VMEM)


def call(kernel, outs, *args, flops=0, scratch=(), limit=16):
    moved = sum(a.size * a.dtype.itemsize for a in args)
    moved += sum(o.size * o.dtype.itemsize for o in outs)
    return pl.pallas_call(
        kernel,
        out_shape=tuple(outs),
        in_specs=[VMEM] * len(args),
        out_specs=tuple(VMEM for _ in outs),
        scratch_shapes=scratch,
        compiler_params=pltpu.CompilerParams(vmem_limit_bytes=limit * 2**20),
        cost_estimate=pl.CostEstimate(flops=flops, bytes_accessed=moved, transcendentals=0),
    )(*args)


def shape(dims, kind=BF):
    return jax.ShapeDtypeStruct(dims, kind)


def chooser(rows, cols, source):
    q = lax.broadcasted_iota(jnp.int32, (rows, cols), 0)
    m = lax.broadcasted_iota(jnp.int32, (rows, cols), 1)
    return jnp.where(source(q) == m, 1.0, 0.0).astype(BF)


def moved(matrix, rows):
    return jnp.dot(matrix, rows, preferred_element_type=F32).astype(BF)


class Sizes:
    def __init__(self, count, frames, rows, cols, chans):
        self.n, self.fl, self.r, self.w, self.c = count, frames, rows, cols, chans
        self.f = count * frames
        self.wc = cols // count
        self.block = self.f * self.wc
        self.piece = frames * self.wc
        self.main = rows * self.piece
        self.sides = 2 * rows * frames


def even(axis):
    return lax.axis_index(axis) % 2 == 0


def edge_kernel(z, x_ref, after_ref, near, far):
    top, bottom = (flat(x_ref[:, r]) for r in (0, z.r - 1))
    near[...] = jnp.where(even("space"), bottom, top)
    far[...] = jnp.where(even("space"), top, bottom)


def pack_kernel(z, x_ref, *outs):
    me = lax.axis_index("tm")

    def source(q):
        k = q // z.piece
        f = q % z.piece // z.wc
        return f * z.w + (me ^ k) * z.wc + q % z.wc

    def edge(r, q):
        k = q // z.sides
        side = q % z.sides // (z.r * z.fl)
        row = q % (z.r * z.fl) // z.fl
        col = (me ^ k) * z.wc - 1 + side * (z.wc + 1)
        inside = (col >= 0) & (col < z.w) & (row == r)
        return jnp.where(inside, q % z.fl * z.w + col, -1)

    matrix = chooser(z.n * z.piece, z.fl * z.w, source)
    tails = jnp.zeros((z.n * z.sides, z.c), F32)
    for r in range(z.r):
        rows = x_ref[:, r].reshape(z.fl * z.w, z.c)
        cut = moved(matrix, rows)
        for k in range(z.n):
            outs[k][r * z.piece : (r + 1) * z.piece] = cut[k * z.piece : (k + 1) * z.piece]
        picked = chooser(z.n * z.sides, z.fl * z.w, functools.partial(edge, r))
        tails += jnp.dot(picked, rows, preferred_element_type=F32)
    tails = tails.astype(BF)
    for k in range(z.n):
        outs[k][z.main : z.main + z.sides] = tails[k * z.sides : (k + 1) * z.sides]


def aside(z, rows):
    count = z.fl * z.w
    left = chooser(count, count, lambda q: jnp.where(q % z.w > 0, q - 1, -1))
    right = chooser(count, count, lambda q: jnp.where(q % z.w < z.w - 1, q + 1, -1))
    return moved(left, rows), rows, moved(right, rows)


def own_inner_kernel(z, x_ref, w_ref, out, beside):
    for r in range(z.r):
        for dj, rows in enumerate(aside(z, x_ref[:, r].reshape(z.fl * z.w, z.c))):
            beside[dj, r] = rows
    for r in range(z.r):
        total = jnp.zeros((z.fl * z.w, z.c), F32)
        for di in range(3):
            if 0 <= r + di - 1 < z.r:
                for dj in range(3):
                    total += jnp.dot(
                        beside[dj, r + di - 1], w_ref[di, dj], preferred_element_type=F32
                    )
        out[r] = total


def own_act_kernel(z, part_ref, near_ref, far_ref, w_ref, cot_ref, out, near, far):
    lower = even("space")
    first = even("tm")
    for r in range(z.r):
        total = part_ref[r]
        for edge, di in ((0, 0), (z.r - 1, 2)):
            if r == edge:
                rows = jnp.where(lower == (di == 2), near_ref[...], far_ref[...])
                for dj, rows in enumerate(aside(z, rows)):
                    total += jnp.dot(rows, w_ref[di, dj], preferred_element_type=F32)
        act = silu(total).reshape(z.fl, z.w, z.c)
        out[:, r] = act
        last = act[z.fl - 1]
        near[r] = jnp.where(first, last, cot_ref[0, r])
        far[r] = jnp.where(first, cot_ref[0, r], last)


def silu(total):
    return (total / (1.0 + jnp.exp(-total))).astype(BF)


def flat(value):
    return value.reshape(-1, value.shape[-1])


def outer(left, right):
    return lax.dot_general(
        flat(left), flat(right), (((0,), (0,)), ((), ())), preferred_element_type=F32
    )


def own_grad_kernel(z, act_ref, cot_ref, out):
    for k in range(3):
        out[:, k * z.c : (k + 1) * z.c] = outer(cot_ref[k:], act_ref[: z.fl - k])


def cross_kernel(z, width, part_ref, near_ref, far_ref, act_ref, cot_ref, keep, send):
    mine = even("space")
    before = jnp.where(even("tm"), far_ref[...], near_ref[...])
    after = jnp.where(even("tm"), near_ref[...], far_ref[...])
    for k in range(3):
        lanes = slice(k * z.c, (k + 1) * z.c)
        grad = part_ref[:, lanes]
        if k == 1:
            grad += outer(cot_ref[0], before)
        if k == 2:
            grad += outer(cot_ref[1], before)
            grad += outer(after, act_ref[z.fl - 2])
        for i in range(z.c // (2 * width)):
            low = grad[2 * i * width : (2 * i + 1) * width]
            high = grad[(2 * i + 1) * width : (2 * i + 2) * width]
            keep[i * width : (i + 1) * width, lanes] = jnp.where(mine, low, high)
            send[i * width : (i + 1) * width, lanes] = jnp.where(mine, high, low).astype(BF)


def gather_matrix(z, me):
    def source(q):
        s = q % z.f // z.fl
        return ((me ^ s) * z.fl + q % z.fl) * z.wc + q // z.f

    return chooser(z.block, z.block, source)


def assemble_kernel(z, *refs):
    parts, (out, near, far) = refs[: z.n], refs[z.n :]
    me = lax.axis_index("tm")
    lower = even("space")
    matrix = gather_matrix(z, me)

    def edge(q):
        head = q // z.f
        s = q % z.f // z.fl
        return ((me ^ s) * 2 * z.r + head) * z.fl + q % z.fl

    count = z.n * z.sides
    tails = jnp.concatenate([p[z.main : z.main + z.sides] for p in parts], axis=0)
    tails = moved(chooser(count, count, edge), tails)
    last = z.f + z.block
    for r in range(z.r):
        rows = jnp.concatenate([p[r * z.piece : (r + 1) * z.piece] for p in parts], axis=0)
        rows = moved(matrix, rows)
        left = tails[r * z.f : (r + 1) * z.f]
        right = tails[(z.r + r) * z.f : (z.r + r + 1) * z.f]
        out[r, 0 : z.f] = left
        out[r, z.f : last] = rows
        out[r, last : last + z.f] = right
    near[...] = jnp.where(lower, out[z.r - 1], out[0])
    far[...] = jnp.where(lower, out[0], out[z.r - 1])


def inner_kernel(z, x_ref, w_ref, out):
    for r in range(z.r):
        total = jnp.zeros((z.block, z.c), F32)
        for di in range(3):
            if not 0 <= r + di - 1 < z.r:
                continue
            for dj in range(3):
                total += jnp.dot(
                    x_ref[r + di - 1, dj * z.f : dj * z.f + z.block],
                    w_ref[di, dj],
                    preferred_element_type=F32,
                )
        out[r] = total


def norm_kernel(
    z, part_ref, near_ref, far_ref, w_ref, x_ref, t_ref, gain_ref, hidden_ref, normed_ref
):
    lower = even("space")
    frame = lax.broadcasted_iota(jnp.int32, (z.block, z.c), 0) % z.f
    held = {}

    def activate(r):
        total = part_ref[r]
        for edge, di in ((0, 0), (z.r - 1, 2)):
            if r == edge:
                rows = jnp.where(lower == (di == 2), near_ref[...], far_ref[...])
                for dj in range(3):
                    total += jnp.dot(
                        rows[dj * z.f : dj * z.f + z.block],
                        w_ref[di, dj],
                        preferred_element_type=F32,
                    )
        act = silu(total)
        wide = act.astype(F32)
        held["a", r] = [act] + [
            jnp.where(frame >= k, pltpu.roll(wide, k, 0), 0.0).astype(BF) for k in (1, 2)
        ]

    def hide(r):
        temporal = sum(
            jnp.dot(late, t_ref[k], preferred_element_type=F32)
            for k, late in enumerate(held.pop(("a", r)))
        )
        hidden = (x_ref[r, z.f : z.f + z.block].astype(F32) + temporal).astype(BF)
        hidden_ref[r] = hidden
        held["h", r] = hidden

    def norm(r):
        wide = held.pop(("h", r)).astype(F32)
        mean = jnp.mean(wide * wide, axis=1, keepdims=True)
        normed_ref[r] = (wide * (1.0 / jnp.sqrt(mean + 1e-06)) * gain_ref[...]).astype(BF)

    staged(z, (activate, hide, norm))


def staged(z, stages):
    for step in range(z.r + len(stages) - 1):
        for late, stage in reversed(list(enumerate(stages))):
            if 0 <= step - late < z.r:
                stage(step - late)


def attend_kernel(z, hidden_ref, normed_ref, q_ref, k_ref, v_ref, o_ref, *outs):
    me = lax.axis_index("tm")
    a = lax.broadcasted_iota(jnp.int32, (z.block, z.block), 0)
    b = lax.broadcasted_iota(jnp.int32, (z.block, z.block), 1)
    allowed = (a // z.f == b // z.f) & (b % z.f <= a % z.f)
    scale = float(z.c) ** -0.5

    def source(q):
        t = ((me ^ (q // z.piece)) * z.fl) + q % z.piece // z.wc
        return q % z.wc * z.f + t

    back = chooser(z.block, z.block, source)
    held = {}

    def project(r):
        rows = normed_ref[r]
        held["q", r], held["k", r], held["v", r] = (
            jnp.dot(rows, w[...], preferred_element_type=F32).astype(BF)
            for w in (q_ref, k_ref, v_ref)
        )

    def score(r):
        held["s", r] = lax.dot_general(
            held.pop(("q", r)),
            held.pop(("k", r)),
            (((1,), (1,)), ((), ())),
            preferred_element_type=F32,
        )

    def weigh(r):
        scores = jnp.where(allowed, held.pop(("s", r)) * scale, -1e30)
        top = jnp.max(scores, axis=1, keepdims=True)
        expon = jnp.where(allowed, jnp.exp(scores - top), 0.0)
        held["t", r] = 1.0 / jnp.sum(expon, axis=1, keepdims=True)
        held["p", r] = expon.astype(BF)

    def mix(r):
        mixed = jnp.dot(held.pop(("p", r)), held.pop(("v", r)), preferred_element_type=F32)
        held["a", r] = (mixed * held.pop(("t", r))).astype(BF)

    def finish(r):
        encoded = hidden_ref[r].astype(F32) + jnp.dot(
            held.pop(("a", r)), o_ref[...], preferred_element_type=F32
        )
        held["e", r] = encoded.astype(BF)

    def spread(r):
        encoded = moved(back, held.pop(("e", r)))
        for k in range(z.n):
            outs[k][r] = encoded[k * z.piece : (k + 1) * z.piece]

    staged(z, (project, score, weigh, mix, finish, spread))


def split_kernel(z, keep_ref, got_ref, *outs):
    me = lax.axis_index("tm")
    wide = z.c // z.n
    for tap in range(3):
        place = slice(tap * wide, (tap + 1) * wide)
        if wide % 128 == 0:
            for k in range(z.n):
                lanes = pl.ds(pl.multiple_of(tap * z.c + (me ^ k) * wide, 128), wide)
                total = keep_ref[:, lanes] + got_ref[:, lanes].astype(F32)
                outs[k][:, place] = total.astype(outs[k].dtype)
            continue
        lanes = slice(tap * z.c, (tap + 1) * z.c)
        total = keep_ref[:, lanes] + got_ref[:, lanes].astype(F32)
        for k in range(z.n):
            cut = total[:, 0:wide]
            for i in range(1, z.n):
                cut = jnp.where((me ^ k) == i, total[:, i * wide : (i + 1) * wide], cut)
            outs[k][:, place] = cut.astype(outs[k].dtype)


def swap(value, axis, k):
    count = lax.axis_size(axis)
    return lax.ppermute(value, axis, [(i, i ^ k) for i in range(count)])


def swap_both(near, far, axis):
    pairs = [(i, i + 1) for i in range(1, lax.axis_size(axis) - 1, 2)]
    other = lax.ppermute(far, axis, pairs + [(b, a) for a, b in pairs])
    return swap(near, axis, 1), other


def chip_kernel(z, width, *refs):
    parts, outs, total = refs[: z.n], refs[z.n : -1], refs[-1]
    total[...] = sum(part[...].astype(F32) for part in parts)
    chip = lax.axis_index("space") // 2
    for k, out in enumerate(outs):
        rows = pl.ds(pl.multiple_of((chip ^ k) * width, width), width)
        out[...] = total[rows].astype(out.dtype)


def sum_kernel(z, *refs):
    out, wide = refs[-1], z.c // z.n
    total = sum(part[...].astype(F32) for part in refs[:-1])
    for k in range(3):
        out[k] = total[:, k * wide : (k + 1) * wide]


def join_kernel(z, *refs):
    parts, (out, whole, sem) = refs[: z.n], refs[z.n :]
    me = lax.axis_index("tm")
    copies = []
    for f in range(z.fl):
        for k in range(z.n):
            cols = pl.ds(pl.multiple_of((me ^ k) * z.wc, z.wc), z.wc)
            whole[f, :, cols] = parts[k][:, f * z.wc : (f + 1) * z.wc]
        copies.append(pltpu.make_async_copy(whole.at[f], out.at[f], sem.at[f]))
        copies[f].start()
    for copy in copies:
        copy.wait()


def joined(z, back):
    if z.wc % 16 == 0:
        return pl.pallas_call(
            functools.partial(join_kernel, z),
            out_shape=shape((z.fl, z.r, z.w, z.c)),
            in_specs=[VMEM] * z.n,
            out_specs=pl.BlockSpec(memory_space=pl.ANY),
            scratch_shapes=[
                pltpu.VMEM((z.fl, z.r, z.w, z.c), BF),
                pltpu.SemaphoreType.DMA((z.fl,)),
            ],
            compiler_params=pltpu.CompilerParams(vmem_limit_bytes=16 * 2**20),
            cost_estimate=pl.CostEstimate(
                flops=0, bytes_accessed=8 * z.n * z.main * z.c, transcendentals=0
            ),
        )(*back)
    whole = jnp.zeros((z.fl, z.r, z.n, z.wc, z.c), BF)
    for k in range(z.n):
        rows = back[k].reshape(z.r, z.fl, 1, z.wc, z.c).transpose(1, 0, 2, 3, 4)
        whole = lax.dynamic_update_slice_in_dim(whole, rows, lax.axis_index("tm") ^ k, 2)
    return whole.reshape(z.fl, z.r, z.w, z.c)


def on_device(frames_in, spatial, temporal, gain, q_w, k_w, v_w, o_w, cotangent):
    n = lax.axis_size("tm")
    space = lax.axis_size("space")
    z = Sizes(n, *frames_in.shape)
    one = 2 * z.r * z.block * z.c * z.c
    others = sorted(range(1, n), key=lambda k: -k.bit_count())
    width, wide, chips = z.c // space, z.c // n, space // 2

    def exchange(pieces):
        pieces = list(pieces)
        for k in others:
            pieces[k] = swap(pieces[k], "tm", k)
        return pieces

    edge = shape((z.fl * z.w, z.c))
    packed = call(
        functools.partial(pack_kernel, z),
        [shape((z.main + z.sides, z.c))] * n,
        frames_in,
        flops=one // 2,
    )
    near, far = call(
        functools.partial(edge_kernel, z), [edge, edge], frames_in, packed[0], flops=8 * one
    )
    got = exchange(packed)
    near, far = swap_both(near, far, "space")
    (own,) = call(
        functools.partial(own_inner_kernel, z),
        [shape((z.r, z.fl * z.w, z.c), F32)],
        frames_in,
        spatial,
        flops=8 * one,
        scratch=[pltpu.VMEM((3, z.r, z.fl * z.w, z.c), BF)],
    )
    own_act, near, far = call(
        functools.partial(own_act_kernel, z),
        [shape(frames_in.shape), shape((z.r, z.w, z.c)), shape((z.r, z.w, z.c))],
        own,
        near,
        far,
        spatial,
        cotangent,
        flops=3 * one,
    )
    near, far = swap_both(near, far, "tm")
    (own_grad,) = call(
        functools.partial(own_grad_kernel, z),
        [shape((z.c, 3 * z.c), F32)],
        own_act,
        cotangent,
        flops=9 * one // 4,
    )
    line = z.block + 2 * z.f
    x, close, apart = call(
        functools.partial(assemble_kernel, z),
        [shape((z.r, line, z.c)), shape((line, z.c)), shape((line, z.c))],
        *got,
    )
    close, apart = swap_both(close, apart, "space")
    (inner,) = call(
        functools.partial(inner_kernel, z),
        [shape((z.r, z.block, z.c), F32)],
        x,
        spatial,
        flops=9 * one * (3 * z.r - 2) // (3 * z.r),
    )
    tied = lax.optimization_barrier((near, far, inner, close, apart))
    near, far, inner, close, apart = tied
    keep, send = call(
        functools.partial(cross_kernel, z, width),
        [shape((z.c // 2, 3 * z.c), F32), shape((z.c // 2, 3 * z.c))],
        own_grad,
        near,
        far,
        own_act,
        cotangent,
        flops=3 * one // 4,
    )
    inner, send = lax.optimization_barrier((inner, send))
    other = swap(send, "space", 1)
    hidden, normed = call(
        functools.partial(norm_kernel, z),
        [shape((z.r, z.block, z.c))] * 2,
        inner,
        close,
        apart,
        spatial,
        x,
        temporal,
        gain.reshape(1, z.c),
        flops=5 * one,
    )
    pieces = call(
        functools.partial(split_kernel, z),
        [shape((z.c // 2, 3 * wide), F32)] + [shape((z.c // 2, 3 * wide))] * (n - 1),
        keep,
        other,
    )
    normed, *pieces = lax.optimization_barrier((normed, *pieces))
    pieces = exchange(pieces)
    encoded = call(
        functools.partial(attend_kernel, z),
        [shape((z.r, z.piece, z.c))] * n,
        hidden,
        normed,
        q_w,
        k_w,
        v_w,
        o_w,
        flops=5 * one,
    )
    back = exchange(encoded)
    pieces = lax.optimization_barrier((*pieces, *encoded))[:n]
    totals = call(
        functools.partial(chip_kernel, z, width),
        [shape((width, 3 * wide), F32)] + [shape((width, 3 * wide))] * (chips - 1),
        *pieces,
        scratch=[pltpu.VMEM((z.c // 2, 3 * wide), F32)],
    )
    totals = [totals[0]] + [swap(totals[k], "space", 2 * k) for k in range(1, chips)]
    (kernel_grad,) = call(
        functools.partial(sum_kernel, z), [shape((3, width, wide), F32)], *totals
    )
    return joined(z, back), kernel_grad.transpose(0, 2, 1)


def solution(mesh):
    tiles = P("tm", "space", None, None)
    return jax.shard_map(
        on_device,
        mesh=mesh,
        in_specs=(tiles,) + (P(),) * 7 + (tiles,),
        out_specs=(tiles, P(None, "tm", "space")),
        check_vma=False,
    )
```

```python
import functools

import jax
import jax.numpy as jnp
from jax import lax
from jax.experimental import pallas as pl
from jax.experimental.pallas import tpu as pltpu
from jax.sharding import PartitionSpec as P

BF = jnp.bfloat16
F32 = jnp.float32
VMEM = pl.BlockSpec(memory_space=pltpu.VMEM)


def call(kernel, outs, *args, flops=0, scratch=(), limit=16):
    moved = sum(a.size * a.dtype.itemsize for a in args)
    moved += sum(o.size * o.dtype.itemsize for o in outs)
    return pl.pallas_call(
        kernel,
        out_shape=tuple(outs),
        in_specs=[VMEM] * len(args),
        out_specs=tuple(VMEM for _ in outs),
        scratch_shapes=scratch,
        compiler_params=pltpu.CompilerParams(vmem_limit_bytes=limit * 2**20),
        cost_estimate=pl.CostEstimate(flops=flops, bytes_accessed=moved, transcendentals=0),
    )(*args)


def shape(dims, kind=BF):
    return jax.ShapeDtypeStruct(dims, kind)


def chooser(rows, cols, source):
    q = lax.broadcasted_iota(jnp.int32, (rows, cols), 0)
    m = lax.broadcasted_iota(jnp.int32, (rows, cols), 1)
    return jnp.where(source(q) == m, 1.0, 0.0).astype(BF)


def moved(matrix, rows):
    return jnp.dot(matrix, rows, preferred_element_type=F32).astype(BF)


class Sizes:
    def __init__(self, count, frames, rows, cols, chans):
        self.n, self.fl, self.r, self.w, self.c = count, frames, rows, cols, chans
        self.f = count * frames
        self.wc = cols // count
        self.block = self.f * self.wc
        self.piece = frames * self.wc
        self.main = rows * self.piece
        self.sides = 2 * rows * frames


def even(axis):
    return lax.axis_index(axis) % 2 == 0


def edge_kernel(z, x_ref, after_ref, near, far):
    top, bottom = (flat(x_ref[:, r]) for r in (0, z.r - 1))
    near[...] = jnp.where(even("space"), bottom, top)
    far[...] = jnp.where(even("space"), top, bottom)


def pack_kernel(z, x_ref, *outs):
    me = lax.axis_index("tm")

    def source(q):
        k = q // z.piece
        f = q % z.piece // z.wc
        return f * z.w + (me ^ k) * z.wc + q % z.wc

    def edge(r, q):
        k = q // z.sides
        side = q % z.sides // (z.r * z.fl)
        row = q % (z.r * z.fl) // z.fl
        col = (me ^ k) * z.wc - 1 + side * (z.wc + 1)
        inside = (col >= 0) & (col < z.w) & (row == r)
        return jnp.where(inside, q % z.fl * z.w + col, -1)

    matrix = chooser(z.n * z.piece, z.fl * z.w, source)
    tails = jnp.zeros((z.n * z.sides, z.c), F32)
    for r in range(z.r):
        rows = x_ref[:, r].reshape(z.fl * z.w, z.c)
        cut = moved(matrix, rows)
        for k in range(z.n):
            outs[k][r * z.piece : (r + 1) * z.piece] = cut[k * z.piece : (k + 1) * z.piece]
        picked = chooser(z.n * z.sides, z.fl * z.w, functools.partial(edge, r))
        tails += jnp.dot(picked, rows, preferred_element_type=F32)
    tails = tails.astype(BF)
    for k in range(z.n):
        outs[k][z.main : z.main + z.sides] = tails[k * z.sides : (k + 1) * z.sides]


def aside(z, rows):
    count = z.fl * z.w
    left = chooser(count, count, lambda q: jnp.where(q % z.w > 0, q - 1, -1))
    right = chooser(count, count, lambda q: jnp.where(q % z.w < z.w - 1, q + 1, -1))
    return moved(left, rows), rows, moved(right, rows)


def own_inner_kernel(z, x_ref, w_ref, out, beside):
    for r in range(z.r):
        for dj, rows in enumerate(aside(z, x_ref[:, r].reshape(z.fl * z.w, z.c))):
            beside[dj, r] = rows
    for r in range(z.r):
        total = jnp.zeros((z.fl * z.w, z.c), F32)
        for di in range(3):
            if 0 <= r + di - 1 < z.r:
                for dj in range(3):
                    total += jnp.dot(
                        beside[dj, r + di - 1], w_ref[di, dj], preferred_element_type=F32
                    )
        out[r] = total


def own_act_kernel(z, part_ref, near_ref, far_ref, w_ref, cot_ref, out, near, far):
    lower = even("space")
    first = even("tm")
    for r in range(z.r):
        total = part_ref[r]
        for edge, di in ((0, 0), (z.r - 1, 2)):
            if r == edge:
                rows = jnp.where(lower == (di == 2), near_ref[...], far_ref[...])
                for dj, rows in enumerate(aside(z, rows)):
                    total += jnp.dot(rows, w_ref[di, dj], preferred_element_type=F32)
        act = silu(total).reshape(z.fl, z.w, z.c)
        out[:, r] = act
        last = act[z.fl - 1]
        near[r] = jnp.where(first, last, cot_ref[0, r])
        far[r] = jnp.where(first, cot_ref[0, r], last)


def silu(total):
    return (total / (1.0 + jnp.exp(-total))).astype(BF)


def flat(value):
    return value.reshape(-1, value.shape[-1])


def outer(left, right):
    return lax.dot_general(
        flat(left), flat(right), (((0,), (0,)), ((), ())), preferred_element_type=F32
    )


def own_grad_kernel(z, act_ref, cot_ref, out):
    for k in range(3):
        out[:, k * z.c : (k + 1) * z.c] = outer(cot_ref[k:], act_ref[: z.fl - k])


def cross_kernel(z, width, part_ref, near_ref, far_ref, act_ref, cot_ref, keep, send):
    mine = even("space")
    before = jnp.where(even("tm"), far_ref[...], near_ref[...])
    after = jnp.where(even("tm"), near_ref[...], far_ref[...])
    for k in range(3):
        lanes = slice(k * z.c, (k + 1) * z.c)
        grad = part_ref[:, lanes]
        if k == 1:
            grad += outer(cot_ref[0], before)
        if k == 2:
            grad += outer(cot_ref[1], before)
            grad += outer(after, act_ref[z.fl - 2])
        for i in range(z.c // (2 * width)):
            low = grad[2 * i * width : (2 * i + 1) * width]
            high = grad[(2 * i + 1) * width : (2 * i + 2) * width]
            keep[i * width : (i + 1) * width, lanes] = jnp.where(mine, low, high)
            send[i * width : (i + 1) * width, lanes] = jnp.where(mine, high, low).astype(BF)


def gather_matrix(z, me):
    def source(q):
        s = q % z.f // z.fl
        return ((me ^ s) * z.fl + q % z.fl) * z.wc + q // z.f

    return chooser(z.block, z.block, source)


def assemble_kernel(z, *refs):
    parts, (out, near, far) = refs[: z.n], refs[z.n :]
    me = lax.axis_index("tm")
    lower = even("space")
    matrix = gather_matrix(z, me)

    def edge(q):
        head = q // z.f
        s = q % z.f // z.fl
        return ((me ^ s) * 2 * z.r + head) * z.fl + q % z.fl

    count = z.n * z.sides
    tails = jnp.concatenate([p[z.main : z.main + z.sides] for p in parts], axis=0)
    tails = moved(chooser(count, count, edge), tails)
    last = z.f + z.block
    for r in range(z.r):
        rows = jnp.concatenate([p[r * z.piece : (r + 1) * z.piece] for p in parts], axis=0)
        rows = moved(matrix, rows)
        left = tails[r * z.f : (r + 1) * z.f]
        right = tails[(z.r + r) * z.f : (z.r + r + 1) * z.f]
        out[r, 0 : z.f] = left
        out[r, z.f : last] = rows
        out[r, last : last + z.f] = right
    near[...] = jnp.where(lower, out[z.r - 1], out[0])
    far[...] = jnp.where(lower, out[0], out[z.r - 1])


def conv_row(z, w_ref, three):
    total = jnp.zeros((z.block, z.c), F32)
    for di, rows in enumerate(three):
        for dj in range(3):
            total += jnp.dot(
                rows[dj * z.f : dj * z.f + z.block], w_ref[di, dj], preferred_element_type=F32
            )
    return silu(total)


def middle_kernel(z, x_ref, w_ref, out):
    for r in range(1, z.r - 1):
        out[r - 1] = conv_row(z, w_ref, [x_ref.at[r + di] for di in (-1, 0, 1)])


def border_kernel(z, x_ref, near_ref, far_ref, w_ref, out, edges):
    lower = even("space")
    edges[0] = jnp.where(lower, far_ref[...], near_ref[...])
    edges[1] = jnp.where(lower, near_ref[...], far_ref[...])
    out[0] = conv_row(z, w_ref, [edges.at[0], x_ref.at[0], x_ref.at[1]])
    out[1] = conv_row(z, w_ref, [x_ref.at[z.r - 2], x_ref.at[z.r - 1], edges.at[1]])


def staged(z, stages):
    for step in range(z.r + len(stages) - 1):
        for late, stage in reversed(list(enumerate(stages))):
            if 0 <= step - late < z.r:
                stage(step - late)


def main_kernel(
    z, middle_ref, border_ref, x_ref, t_ref, gain_ref, q_ref, k_ref, v_ref, o_ref, *outs
):
    me = lax.axis_index("tm")
    a = lax.broadcasted_iota(jnp.int32, (z.block, z.block), 0)
    b = lax.broadcasted_iota(jnp.int32, (z.block, z.block), 1)
    allowed = (a // z.f == b // z.f) & (b % z.f <= a % z.f)
    scale = float(z.c) ** -0.5

    def source(q):
        t = ((me ^ (q // z.piece)) * z.fl) + q % z.piece // z.wc
        return q % z.wc * z.f + t

    back = chooser(z.block, z.block, source)
    frame = lax.broadcasted_iota(jnp.int32, (z.block, z.c), 0) % z.f
    held = {}

    def activate(r):
        act = border_ref[r // (z.r - 1)] if r in (0, z.r - 1) else middle_ref[r - 1]
        wide = act.astype(F32)
        held["a", r] = [act] + [
            jnp.where(frame >= k, pltpu.roll(wide, k, 0), 0.0).astype(BF) for k in (1, 2)
        ]

    def hide(r):
        temporal = sum(
            jnp.dot(late, t_ref[k], preferred_element_type=F32)
            for k, late in enumerate(held.pop(("a", r)))
        )
        hidden = (x_ref[r, z.f : z.f + z.block].astype(F32) + temporal).astype(BF)
        held["h", r] = hidden

    def norm(r):
        wide = held["h", r].astype(F32)
        mean = jnp.mean(wide * wide, axis=1, keepdims=True)
        held["n", r] = (wide * (1.0 / jnp.sqrt(mean + 1e-06)) * gain_ref[...]).astype(BF)

    def project(r):
        rows = held.pop(("n", r))
        held["q", r], held["k", r], held["v", r] = (
            jnp.dot(rows, w[...], preferred_element_type=F32).astype(BF)
            for w in (q_ref, k_ref, v_ref)
        )

    def score(r):
        held["s", r] = lax.dot_general(
            held.pop(("q", r)),
            held.pop(("k", r)),
            (((1,), (1,)), ((), ())),
            preferred_element_type=F32,
        )

    def weigh(r):
        scores = jnp.where(allowed, held.pop(("s", r)) * scale, -1e30)
        top = jnp.max(scores, axis=1, keepdims=True)
        expon = jnp.where(allowed, jnp.exp(scores - top), 0.0)
        held["t", r] = 1.0 / jnp.sum(expon, axis=1, keepdims=True)
        held["p", r] = expon.astype(BF)

    def mix(r):
        mixed = jnp.dot(held.pop(("p", r)), held.pop(("v", r)), preferred_element_type=F32)
        held["a", r] = (mixed * held.pop(("t", r))).astype(BF)

    def finish(r):
        encoded = held.pop(("h", r)).astype(F32) + jnp.dot(
            held.pop(("a", r)), o_ref[...], preferred_element_type=F32
        )
        held["e", r] = encoded.astype(BF)

    def spread(r):
        encoded = moved(back, held.pop(("e", r)))
        for k in range(z.n):
            outs[k][r] = encoded[k * z.piece : (k + 1) * z.piece]

    staged(z, (activate, hide, norm, project, score, weigh, mix, finish, spread))


def split_kernel(z, keep_ref, got_ref, *outs):
    me = lax.axis_index("tm")
    wide = z.c // z.n
    for tap in range(3):
        place = slice(tap * wide, (tap + 1) * wide)
        if wide % 128 == 0:
            for k in range(z.n):
                lanes = pl.ds(pl.multiple_of(tap * z.c + (me ^ k) * wide, 128), wide)
                total = keep_ref[:, lanes] + got_ref[:, lanes].astype(F32)
                outs[k][:, place] = total.astype(outs[k].dtype)
            continue
        lanes = slice(tap * z.c, (tap + 1) * z.c)
        total = keep_ref[:, lanes] + got_ref[:, lanes].astype(F32)
        for k in range(z.n):
            cut = total[:, 0:wide]
            for i in range(1, z.n):
                cut = jnp.where((me ^ k) == i, total[:, i * wide : (i + 1) * wide], cut)
            outs[k][:, place] = cut.astype(outs[k].dtype)


def swap(value, axis, k):
    count = lax.axis_size(axis)
    return lax.ppermute(value, axis, [(i, i ^ k) for i in range(count)])


def swap_both(near, far, axis):
    pairs = [(i, i + 1) for i in range(1, lax.axis_size(axis) - 1, 2)]
    other = lax.ppermute(far, axis, pairs + [(b, a) for a, b in pairs])
    return swap(near, axis, 1), other


def chip_kernel(z, width, *refs):
    parts, outs, total = refs[: z.n], refs[z.n : -1], refs[-1]
    total[...] = sum(part[...].astype(F32) for part in parts)
    chip = lax.axis_index("space") // 2
    for k, out in enumerate(outs):
        rows = pl.ds(pl.multiple_of((chip ^ k) * width, width), width)
        out[...] = total[rows].astype(out.dtype)


def sum_kernel(z, *refs):
    out, wide = refs[-1], z.c // z.n
    total = sum(part[...].astype(F32) for part in refs[:-1])
    for k in range(3):
        out[k] = total[:, k * wide : (k + 1) * wide]


def join_kernel(z, *refs):
    parts, (out, whole, sem) = refs[: z.n], refs[z.n :]
    me = lax.axis_index("tm")
    copies = []
    for f in range(z.fl):
        for k in range(z.n):
            cols = pl.ds(pl.multiple_of((me ^ k) * z.wc, z.wc), z.wc)
            whole[f, :, cols] = parts[k][:, f * z.wc : (f + 1) * z.wc]
        copies.append(pltpu.make_async_copy(whole.at[f], out.at[f], sem.at[f]))
        copies[f].start()
    for copy in copies:
        copy.wait()


def joined(z, back):
    if z.wc % 16 == 0:
        return pl.pallas_call(
            functools.partial(join_kernel, z),
            out_shape=shape((z.fl, z.r, z.w, z.c)),
            in_specs=[VMEM] * z.n,
            out_specs=pl.BlockSpec(memory_space=pl.ANY),
            scratch_shapes=[
                pltpu.VMEM((z.fl, z.r, z.w, z.c), BF),
                pltpu.SemaphoreType.DMA((z.fl,)),
            ],
            compiler_params=pltpu.CompilerParams(vmem_limit_bytes=16 * 2**20),
            cost_estimate=pl.CostEstimate(
                flops=0, bytes_accessed=8 * z.n * z.main * z.c, transcendentals=0
            ),
        )(*back)
    whole = jnp.zeros((z.fl, z.r, z.n, z.wc, z.c), BF)
    for k in range(z.n):
        rows = back[k].reshape(z.r, z.fl, 1, z.wc, z.c).transpose(1, 0, 2, 3, 4)
        whole = lax.dynamic_update_slice_in_dim(whole, rows, lax.axis_index("tm") ^ k, 2)
    return whole.reshape(z.fl, z.r, z.w, z.c)


def on_device(frames_in, spatial, temporal, gain, q_w, k_w, v_w, o_w, cotangent):
    n = lax.axis_size("tm")
    space = lax.axis_size("space")
    z = Sizes(n, *frames_in.shape)
    one = 2 * z.r * z.block * z.c * z.c
    others = sorted(range(1, n), key=lambda k: -k.bit_count())
    width, wide, chips = z.c // space, z.c // n, space // 2

    def exchange(pieces):
        pieces = list(pieces)
        for k in others:
            pieces[k] = swap(pieces[k], "tm", k)
        return pieces

    edge = shape((z.fl * z.w, z.c))
    packed = call(
        functools.partial(pack_kernel, z),
        [shape((z.main + z.sides, z.c))] * n,
        frames_in,
        flops=one // 2,
    )
    near, far = call(
        functools.partial(edge_kernel, z), [edge, edge], frames_in, packed[0], flops=8 * one
    )
    got = exchange(packed)
    near, far = swap_both(near, far, "space")
    (own,) = call(
        functools.partial(own_inner_kernel, z),
        [shape((z.r, z.fl * z.w, z.c), F32)],
        frames_in,
        spatial,
        flops=8 * one,
        scratch=[pltpu.VMEM((3, z.r, z.fl * z.w, z.c), BF)],
    )
    own_act, near, far = call(
        functools.partial(own_act_kernel, z),
        [shape(frames_in.shape), shape((z.r, z.w, z.c)), shape((z.r, z.w, z.c))],
        own,
        near,
        far,
        spatial,
        cotangent,
        flops=3 * one,
    )
    near, far = swap_both(near, far, "tm")
    (own_grad,) = call(
        functools.partial(own_grad_kernel, z),
        [shape((z.c, 3 * z.c), F32)],
        own_act,
        cotangent,
        flops=9 * one // 4,
    )
    line = z.block + 2 * z.f
    x, close, apart = call(
        functools.partial(assemble_kernel, z),
        [shape((z.r, line, z.c)), shape((line, z.c)), shape((line, z.c))],
        *got,
    )
    close, apart = swap_both(close, apart, "space")
    (middle,) = call(
        functools.partial(middle_kernel, z),
        [shape((z.r - 2, z.block, z.c))],
        x,
        spatial,
        flops=9 * one * (z.r - 2) // z.r,
    )
    tied = lax.optimization_barrier((near, far, middle, close, apart))
    near, far, middle, close, apart = tied
    keep, send = call(
        functools.partial(cross_kernel, z, width),
        [shape((z.c // 2, 3 * z.c), F32), shape((z.c // 2, 3 * z.c))],
        own_grad,
        near,
        far,
        own_act,
        cotangent,
        flops=3 * one // 4,
    )
    other = swap(send, "space", 1)
    x, _ = lax.optimization_barrier((x, send))
    (border,) = call(
        functools.partial(border_kernel, z),
        [shape((2, z.block, z.c))],
        x,
        close,
        apart,
        spatial,
        flops=18 * one // z.r,
        scratch=[pltpu.VMEM((2, line, z.c), BF)],
    )
    other, border = lax.optimization_barrier((other, border))
    pieces = call(
        functools.partial(split_kernel, z),
        [shape((z.c // 2, 3 * wide), F32)] + [shape((z.c // 2, 3 * wide))] * (n - 1),
        keep,
        other,
    )
    border, *pieces = lax.optimization_barrier((border, *pieces))
    pieces = exchange(pieces)
    encoded = call(
        functools.partial(main_kernel, z),
        [shape((z.r, z.piece, z.c))] * n,
        middle,
        border,
        x,
        temporal,
        gain.reshape(1, z.c),
        q_w,
        k_w,
        v_w,
        o_w,
        flops=9 * one,
    )
    back = exchange(encoded)
    pieces = lax.optimization_barrier((*pieces, *encoded))[:n]
    totals = call(
        functools.partial(chip_kernel, z, width),
        [shape((width, 3 * wide), F32)] + [shape((width, 3 * wide))] * (chips - 1),
        *pieces,
        scratch=[pltpu.VMEM((z.c // 2, 3 * wide), F32)],
    )
    totals = [totals[0]] + [swap(totals[k], "space", 2 * k) for k in range(1, chips)]
    (kernel_grad,) = call(
        functools.partial(sum_kernel, z), [shape((3, width, wide), F32)], *totals
    )
    return joined(z, back), kernel_grad.transpose(0, 2, 1)


def solution(mesh):
    tiles = P("tm", "space", None, None)
    return jax.shard_map(
        on_device,
        mesh=mesh,
        in_specs=(tiles,) + (P(),) * 7 + (tiles,),
        out_specs=(tiles, P(None, "tm", "space")),
        check_vma=False,
    )
```

```python
import functools

import jax
import jax.numpy as jnp
from jax import lax
from jax.experimental import pallas as pl
from jax.experimental.pallas import tpu as pltpu
from jax.sharding import PartitionSpec as P

BF = jnp.bfloat16
F32 = jnp.float32
VMEM = pl.BlockSpec(memory_space=pltpu.VMEM)


def call(kernel, outs, *args, flops=0, scratch=(), limit=16):
    moved = sum(a.size * a.dtype.itemsize for a in args)
    moved += sum(o.size * o.dtype.itemsize for o in outs)
    return pl.pallas_call(
        kernel,
        out_shape=tuple(outs),
        in_specs=[VMEM] * len(args),
        out_specs=tuple(VMEM for _ in outs),
        scratch_shapes=scratch,
        compiler_params=pltpu.CompilerParams(vmem_limit_bytes=limit * 2**20),
        cost_estimate=pl.CostEstimate(flops=flops, bytes_accessed=moved, transcendentals=0),
    )(*args)


def shape(dims, kind=BF):
    return jax.ShapeDtypeStruct(dims, kind)


def chooser(rows, cols, source):
    q = lax.broadcasted_iota(jnp.int32, (rows, cols), 0)
    m = lax.broadcasted_iota(jnp.int32, (rows, cols), 1)
    return jnp.where(source(q) == m, 1.0, 0.0).astype(BF)


def moved(matrix, rows):
    return jnp.dot(matrix, rows, preferred_element_type=F32).astype(BF)


class Sizes:
    def __init__(self, count, frames, rows, cols, chans):
        self.n, self.fl, self.r, self.w, self.c = count, frames, rows, cols, chans
        self.f = count * frames
        self.wc = cols // count
        self.block = self.f * self.wc
        self.piece = frames * self.wc
        self.main = rows * self.piece
        self.sides = 2 * rows * frames


def even(axis):
    return lax.axis_index(axis) % 2 == 0


def edge_kernel(z, x_ref, after_ref, near, far):
    top, bottom = (flat(x_ref[:, r]) for r in (0, z.r - 1))
    near[...] = jnp.where(even("space"), bottom, top)
    far[...] = jnp.where(even("space"), top, bottom)


def pack_kernel(z, x_ref, *outs):
    me = lax.axis_index("tm")

    def source(q):
        k = q // z.piece
        f = q % z.piece // z.wc
        return f * z.w + (me ^ k) * z.wc + q % z.wc

    def edge(r, q):
        k = q // z.sides
        side = q % z.sides // (z.r * z.fl)
        row = q % (z.r * z.fl) // z.fl
        col = (me ^ k) * z.wc - 1 + side * (z.wc + 1)
        inside = (col >= 0) & (col < z.w) & (row == r)
        return jnp.where(inside, q % z.fl * z.w + col, -1)

    matrix = chooser(z.n * z.piece, z.fl * z.w, source)
    tails = jnp.zeros((z.n * z.sides, z.c), F32)
    for r in range(z.r):
        rows = x_ref[:, r].reshape(z.fl * z.w, z.c)
        cut = moved(matrix, rows)
        for k in range(z.n):
            outs[k][r * z.piece : (r + 1) * z.piece] = cut[k * z.piece : (k + 1) * z.piece]
        picked = chooser(z.n * z.sides, z.fl * z.w, functools.partial(edge, r))
        tails += jnp.dot(picked, rows, preferred_element_type=F32)
    tails = tails.astype(BF)
    for k in range(z.n):
        outs[k][z.main : z.main + z.sides] = tails[k * z.sides : (k + 1) * z.sides]


def aside(z, rows):
    count = z.fl * z.w
    left = chooser(count, count, lambda q: jnp.where(q % z.w > 0, q - 1, -1))
    right = chooser(count, count, lambda q: jnp.where(q % z.w < z.w - 1, q + 1, -1))
    return moved(left, rows), rows, moved(right, rows)


def own_inner_kernel(z, x_ref, w_ref, out, beside):
    for r in range(z.r):
        for dj, rows in enumerate(aside(z, x_ref[:, r].reshape(z.fl * z.w, z.c))):
            beside[dj, r] = rows
    for r in range(z.r):
        total = jnp.zeros((z.fl * z.w, z.c), F32)
        for di in range(3):
            if 0 <= r + di - 1 < z.r:
                for dj in range(3):
                    total += jnp.dot(
                        beside[dj, r + di - 1], w_ref[di, dj], preferred_element_type=F32
                    )
        out[r] = total


def own_act_kernel(z, part_ref, near_ref, far_ref, w_ref, cot_ref, out, near, far):
    lower = even("space")
    first = even("tm")
    for r in range(z.r):
        total = part_ref[r]
        for edge, di in ((0, 0), (z.r - 1, 2)):
            if r == edge:
                rows = jnp.where(lower == (di == 2), near_ref[...], far_ref[...])
                for dj, rows in enumerate(aside(z, rows)):
                    total += jnp.dot(rows, w_ref[di, dj], preferred_element_type=F32)
        act = silu(total).reshape(z.fl, z.w, z.c)
        out[:, r] = act
        last = act[z.fl - 1]
        near[r] = jnp.where(first, last, cot_ref[0, r])
        far[r] = jnp.where(first, cot_ref[0, r], last)


def silu(total):
    return (total / (1.0 + jnp.exp(-total))).astype(BF)


def flat(value):
    return value.reshape(-1, value.shape[-1])


def outer(left, right):
    return lax.dot_general(
        flat(left), flat(right), (((0,), (0,)), ((), ())), preferred_element_type=F32
    )


def own_grad_kernel(z, act_ref, cot_ref, out):
    for k in range(3):
        out[:, k * z.c : (k + 1) * z.c] = outer(cot_ref[k:], act_ref[: z.fl - k])


def cross_kernel(z, width, part_ref, near_ref, far_ref, act_ref, cot_ref, keep, send):
    mine = even("space")
    before = jnp.where(even("tm"), far_ref[...], near_ref[...])
    after = jnp.where(even("tm"), near_ref[...], far_ref[...])
    for k in range(3):
        lanes = slice(k * z.c, (k + 1) * z.c)
        grad = part_ref[:, lanes]
        if k == 1:
            grad += outer(cot_ref[0], before)
        if k == 2:
            grad += outer(cot_ref[1], before)
            grad += outer(after, act_ref[z.fl - 2])
        for i in range(z.c // (2 * width)):
            low = grad[2 * i * width : (2 * i + 1) * width]
            high = grad[(2 * i + 1) * width : (2 * i + 2) * width]
            keep[i * width : (i + 1) * width, lanes] = jnp.where(mine, low, high)
            send[i * width : (i + 1) * width, lanes] = jnp.where(mine, high, low).astype(BF)


def gather_matrix(z, me):
    def source(q):
        s = q % z.f // z.fl
        return ((me ^ s) * z.fl + q % z.fl) * z.wc + q // z.f

    return chooser(z.block, z.block, source)


def assemble_kernel(z, *refs):
    parts, (out, near, far) = refs[: z.n], refs[z.n :]
    me = lax.axis_index("tm")
    lower = even("space")
    matrix = gather_matrix(z, me)

    def edge(q):
        head = q // z.f
        s = q % z.f // z.fl
        return ((me ^ s) * 2 * z.r + head) * z.fl + q % z.fl

    count = z.n * z.sides
    tails = jnp.concatenate([p[z.main : z.main + z.sides] for p in parts], axis=0)
    tails = moved(chooser(count, count, edge), tails)
    last = z.f + z.block
    for r in range(z.r):
        rows = jnp.concatenate([p[r * z.piece : (r + 1) * z.piece] for p in parts], axis=0)
        rows = moved(matrix, rows)
        left = tails[r * z.f : (r + 1) * z.f]
        right = tails[(z.r + r) * z.f : (z.r + r + 1) * z.f]
        out[r, 0 : z.f] = left
        out[r, z.f : last] = rows
        out[r, last : last + z.f] = right
    near[...] = jnp.where(lower, out[z.r - 1], out[0])
    far[...] = jnp.where(lower, out[0], out[z.r - 1])


def conv_row(z, w_ref, three):
    total = jnp.zeros((z.block, z.c), F32)
    for di, rows in enumerate(three):
        for dj in range(3):
            total += jnp.dot(
                rows[dj * z.f : dj * z.f + z.block], w_ref[di, dj], preferred_element_type=F32
            )
    return silu(total)


def middle_kernel(z, x_ref, w_ref, out):
    for r in range(1, z.r - 1):
        out[r - 1] = conv_row(z, w_ref, [x_ref.at[r + di] for di in (-1, 0, 1)])


def border_kernel(z, x_ref, near_ref, far_ref, w_ref, out, edges):
    lower = even("space")
    edges[0] = jnp.where(lower, far_ref[...], near_ref[...])
    edges[1] = jnp.where(lower, near_ref[...], far_ref[...])
    out[0] = conv_row(z, w_ref, [edges.at[0], x_ref.at[0], x_ref.at[1]])
    out[1] = conv_row(z, w_ref, [x_ref.at[z.r - 2], x_ref.at[z.r - 1], edges.at[1]])


def staged(z, stages):
    for step in range(z.r + len(stages) - 1):
        for late, stage in reversed(list(enumerate(stages))):
            if 0 <= step - late < z.r:
                stage(step - late)


def main_kernel(
    z, middle_ref, border_ref, x_ref, t_ref, gain_ref, q_ref, k_ref, v_ref, o_ref, *outs
):
    me = lax.axis_index("tm")
    a = lax.broadcasted_iota(jnp.int32, (z.block, z.block), 0)
    b = lax.broadcasted_iota(jnp.int32, (z.block, z.block), 1)
    allowed = (a // z.f == b // z.f) & (b % z.f <= a % z.f)
    scale = float(z.c) ** -0.5

    def source(q):
        t = ((me ^ (q // z.piece)) * z.fl) + q % z.piece // z.wc
        return q % z.wc * z.f + t

    back = chooser(z.block, z.block, source)
    frame = lax.broadcasted_iota(jnp.int32, (z.block, z.c), 0) % z.f
    held = {}

    def activate(r):
        act = border_ref[r // (z.r - 1)] if r in (0, z.r - 1) else middle_ref[r - 1]
        wide = act.astype(F32)
        held["a", r] = [act] + [
            jnp.where(frame >= k, pltpu.roll(wide, k, 0), 0.0).astype(BF) for k in (1, 2)
        ]

    def hide(r):
        temporal = sum(
            jnp.dot(late, t_ref[k], preferred_element_type=F32)
            for k, late in enumerate(held.pop(("a", r)))
        )
        hidden = (x_ref[r, z.f : z.f + z.block].astype(F32) + temporal).astype(BF)
        held["h", r] = hidden

    def norm(r):
        wide = held["h", r].astype(F32)
        mean = jnp.mean(wide * wide, axis=1, keepdims=True)
        held["n", r] = (wide * (1.0 / jnp.sqrt(mean + 1e-06)) * gain_ref[...]).astype(BF)

    def project(r):
        rows = held.pop(("n", r))
        held["q", r], held["k", r], held["v", r] = (
            jnp.dot(rows, w[...], preferred_element_type=F32).astype(BF)
            for w in (q_ref, k_ref, v_ref)
        )

    def score(r):
        held["s", r] = lax.dot_general(
            held.pop(("q", r)),
            held.pop(("k", r)),
            (((1,), (1,)), ((), ())),
            preferred_element_type=F32,
        )

    def weigh(r):
        scores = jnp.where(allowed, held.pop(("s", r)) * scale, -1e30)
        top = jnp.max(scores, axis=1, keepdims=True)
        expon = jnp.where(allowed, jnp.exp(scores - top), 0.0)
        held["t", r] = 1.0 / jnp.sum(expon, axis=1, keepdims=True)
        held["p", r] = expon.astype(BF)

    def mix(r):
        mixed = jnp.dot(held.pop(("p", r)), held.pop(("v", r)), preferred_element_type=F32)
        held["a", r] = (mixed * held.pop(("t", r))).astype(BF)

    def finish(r):
        encoded = held.pop(("h", r)).astype(F32) + jnp.dot(
            held.pop(("a", r)), o_ref[...], preferred_element_type=F32
        )
        held["e", r] = encoded.astype(BF)

    def spread(r):
        encoded = moved(back, held.pop(("e", r)))
        for k in range(z.n):
            outs[k][r] = encoded[k * z.piece : (k + 1) * z.piece]

    staged(z, (activate, hide, norm, project, score, weigh, mix, finish, spread))


def split_kernel(z, keep_ref, got_ref, *outs):
    me = lax.axis_index("tm")
    wide = z.c // z.n
    for tap in range(3):
        place = slice(tap * wide, (tap + 1) * wide)
        if wide % 128 == 0:
            for k in range(z.n):
                lanes = pl.ds(pl.multiple_of(tap * z.c + (me ^ k) * wide, 128), wide)
                total = keep_ref[:, lanes] + got_ref[:, lanes].astype(F32)
                outs[k][:, place] = total.astype(outs[k].dtype)
            continue
        lanes = slice(tap * z.c, (tap + 1) * z.c)
        total = keep_ref[:, lanes] + got_ref[:, lanes].astype(F32)
        for k in range(z.n):
            cut = total[:, 0:wide]
            for i in range(1, z.n):
                cut = jnp.where((me ^ k) == i, total[:, i * wide : (i + 1) * wide], cut)
            outs[k][:, place] = cut.astype(outs[k].dtype)


def swap(value, axis, k):
    count = lax.axis_size(axis)
    return lax.ppermute(value, axis, [(i, i ^ k) for i in range(count)])


def swap_both(near, far, axis):
    pairs = [(i, i + 1) for i in range(1, lax.axis_size(axis) - 1, 2)]
    other = lax.ppermute(far, axis, pairs + [(b, a) for a, b in pairs])
    return swap(near, axis, 1), other


def chip_kernel(z, width, *refs):
    parts, outs, total = refs[: z.n], refs[z.n : -1], refs[-1]
    total[...] = sum(part[...].astype(F32) for part in parts)
    chip = lax.axis_index("space") // 2
    for k, out in enumerate(outs):
        rows = pl.ds(pl.multiple_of((chip ^ k) * width, width), width)
        out[...] = total[rows].astype(out.dtype)


def sum_kernel(z, *refs):
    out, wide = refs[-1], z.c // z.n
    total = sum(part[...].astype(F32) for part in refs[:-1])
    for k in range(3):
        out[k] = total[:, k * wide : (k + 1) * wide]


def join_kernel(z, *refs):
    parts, (out, whole, sem) = refs[: z.n], refs[z.n :]
    me = lax.axis_index("tm")
    copies = []
    for f in range(z.fl):
        for k in range(z.n):
            cols = pl.ds(pl.multiple_of((me ^ k) * z.wc, z.wc), z.wc)
            whole[f, :, cols] = parts[k][:, f * z.wc : (f + 1) * z.wc]
        copies.append(pltpu.make_async_copy(whole.at[f], out.at[f], sem.at[f]))
        copies[f].start()
    for copy in copies:
        copy.wait()


def joined(z, back):
    if z.wc % 16 == 0:
        return pl.pallas_call(
            functools.partial(join_kernel, z),
            out_shape=shape((z.fl, z.r, z.w, z.c)),
            in_specs=[VMEM] * z.n,
            out_specs=pl.BlockSpec(memory_space=pl.ANY),
            scratch_shapes=[
                pltpu.VMEM((z.fl, z.r, z.w, z.c), BF),
                pltpu.SemaphoreType.DMA((z.fl,)),
            ],
            compiler_params=pltpu.CompilerParams(vmem_limit_bytes=16 * 2**20),
            cost_estimate=pl.CostEstimate(
                flops=0, bytes_accessed=8 * z.n * z.main * z.c, transcendentals=0
            ),
        )(*back)
    whole = jnp.zeros((z.fl, z.r, z.n, z.wc, z.c), BF)
    for k in range(z.n):
        rows = back[k].reshape(z.r, z.fl, 1, z.wc, z.c).transpose(1, 0, 2, 3, 4)
        whole = lax.dynamic_update_slice_in_dim(whole, rows, lax.axis_index("tm") ^ k, 2)
    return whole.reshape(z.fl, z.r, z.w, z.c)


def on_device(frames_in, spatial, temporal, gain, q_w, k_w, v_w, o_w, cotangent):
    n = lax.axis_size("tm")
    space = lax.axis_size("space")
    z = Sizes(n, *frames_in.shape)
    one = 2 * z.r * z.block * z.c * z.c
    others = sorted(range(1, n), key=lambda k: -k.bit_count())
    width, wide, chips = z.c // space, z.c // n, space // 2

    def exchange(pieces):
        pieces = list(pieces)
        for k in others:
            pieces[k] = swap(pieces[k], "tm", k)
        return pieces

    edge = shape((z.fl * z.w, z.c))
    packed = call(
        functools.partial(pack_kernel, z),
        [shape((z.main + z.sides, z.c))] * n,
        frames_in,
        flops=one // 2,
    )
    near, far = call(
        functools.partial(edge_kernel, z), [edge, edge], frames_in, packed[0], flops=8 * one
    )
    got = exchange(packed)
    near, far = swap_both(near, far, "space")
    (own,) = call(
        functools.partial(own_inner_kernel, z),
        [shape((z.r, z.fl * z.w, z.c), F32)],
        frames_in,
        spatial,
        flops=8 * one,
        scratch=[pltpu.VMEM((3, z.r, z.fl * z.w, z.c), BF)],
    )
    own_act, near, far = call(
        functools.partial(own_act_kernel, z),
        [shape(frames_in.shape), shape((z.r, z.w, z.c)), shape((z.r, z.w, z.c))],
        own,
        near,
        far,
        spatial,
        cotangent,
        flops=3 * one,
    )
    near, far = swap_both(near, far, "tm")
    (own_grad,) = call(
        functools.partial(own_grad_kernel, z),
        [shape((z.c, 3 * z.c), F32)],
        own_act,
        cotangent,
        flops=9 * one // 4,
    )
    line = z.block + 2 * z.f
    own_grad, *got = lax.optimization_barrier((own_grad, *got))
    x, close, apart = call(
        functools.partial(assemble_kernel, z),
        [shape((z.r, line, z.c)), shape((line, z.c)), shape((line, z.c))],
        *got,
    )
    close, apart = swap_both(close, apart, "space")
    (middle,) = call(
        functools.partial(middle_kernel, z),
        [shape((z.r - 2, z.block, z.c))],
        x,
        spatial,
        flops=9 * one * (z.r - 2) // z.r,
    )
    near, far, middle = lax.optimization_barrier((near, far, middle))
    keep, send = call(
        functools.partial(cross_kernel, z, width),
        [shape((z.c // 2, 3 * z.c), F32), shape((z.c // 2, 3 * z.c))],
        own_grad,
        near,
        far,
        own_act,
        cotangent,
        flops=3 * one // 4,
    )
    other = swap(send, "space", 1)
    pieces = call(
        functools.partial(split_kernel, z),
        [shape((z.c // 2, 3 * wide), F32)] + [shape((z.c // 2, 3 * wide))] * (n - 1),
        keep,
        other,
    )
    x, *pieces = lax.optimization_barrier((x, *pieces))
    pieces = exchange(pieces)
    (border,) = call(
        functools.partial(border_kernel, z),
        [shape((2, z.block, z.c))],
        x,
        close,
        apart,
        spatial,
        flops=18 * one // z.r,
        scratch=[pltpu.VMEM((2, line, z.c), BF)],
    )
    encoded = call(
        functools.partial(main_kernel, z),
        [shape((z.r, z.piece, z.c))] * n,
        middle,
        border,
        x,
        temporal,
        gain.reshape(1, z.c),
        q_w,
        k_w,
        v_w,
        o_w,
        flops=9 * one,
    )
    back = exchange(encoded)
    pieces = lax.optimization_barrier((*pieces, *encoded))[:n]
    totals = call(
        functools.partial(chip_kernel, z, width),
        [shape((width, 3 * wide), F32)] + [shape((width, 3 * wide))] * (chips - 1),
        *pieces,
        scratch=[pltpu.VMEM((z.c // 2, 3 * wide), F32)],
    )
    totals = [totals[0]] + [swap(totals[k], "space", 2 * k) for k in range(1, chips)]
    (kernel_grad,) = call(
        functools.partial(sum_kernel, z), [shape((3, width, wide), F32)], *totals
    )
    return joined(z, back), kernel_grad.transpose(0, 2, 1)


def solution(mesh):
    tiles = P("tm", "space", None, None)
    return jax.shard_map(
        on_device,
        mesh=mesh,
        in_specs=(tiles,) + (P(),) * 7 + (tiles,),
        out_specs=(tiles, P(None, "tm", "space")),
        check_vma=False,
    )
```

```python
import functools

import jax
import jax.numpy as jnp
from jax import lax
from jax.experimental import pallas as pl
from jax.experimental.pallas import tpu as pltpu
from jax.sharding import PartitionSpec as P

BF = jnp.bfloat16
F32 = jnp.float32
VMEM = pl.BlockSpec(memory_space=pltpu.VMEM)


def call(kernel, outs, *args, flops=0, scratch=(), limit=16):
    moved = sum(a.size * a.dtype.itemsize for a in args)
    moved += sum(o.size * o.dtype.itemsize for o in outs)
    return pl.pallas_call(
        kernel,
        out_shape=tuple(outs),
        in_specs=[VMEM] * len(args),
        out_specs=tuple(VMEM for _ in outs),
        scratch_shapes=scratch,
        compiler_params=pltpu.CompilerParams(vmem_limit_bytes=limit * 2**20),
        cost_estimate=pl.CostEstimate(flops=flops, bytes_accessed=moved, transcendentals=0),
    )(*args)


def shape(dims, kind=BF):
    return jax.ShapeDtypeStruct(dims, kind)


def chooser(rows, cols, source):
    q = lax.broadcasted_iota(jnp.int32, (rows, cols), 0)
    m = lax.broadcasted_iota(jnp.int32, (rows, cols), 1)
    return jnp.where(source(q) == m, 1.0, 0.0).astype(BF)


def moved(matrix, rows):
    return jnp.dot(matrix, rows, preferred_element_type=F32).astype(BF)


class Sizes:
    def __init__(self, count, frames, rows, cols, chans):
        self.n, self.fl, self.r, self.w, self.c = count, frames, rows, cols, chans
        self.f = count * frames
        self.wc = cols // count
        self.block = self.f * self.wc
        self.piece = frames * self.wc
        self.main = rows * self.piece
        self.sides = 2 * rows * frames


def even(axis):
    return lax.axis_index(axis) % 2 == 0


def edge_kernel(z, x_ref, after_ref, near, far):
    top, bottom = (flat(x_ref[:, r]) for r in (0, z.r - 1))
    near[...] = jnp.where(even("space"), bottom, top)
    far[...] = jnp.where(even("space"), top, bottom)


def pack_kernel(z, x_ref, *outs):
    me = lax.axis_index("tm")

    def source(q):
        k = q // z.piece
        f = q % z.piece // z.wc
        return f * z.w + (me ^ k) * z.wc + q % z.wc

    def edge(r, q):
        k = q // z.sides
        side = q % z.sides // (z.r * z.fl)
        row = q % (z.r * z.fl) // z.fl
        col = (me ^ k) * z.wc - 1 + side * (z.wc + 1)
        inside = (col >= 0) & (col < z.w) & (row == r)
        return jnp.where(inside, q % z.fl * z.w + col, -1)

    matrix = chooser(z.n * z.piece, z.fl * z.w, source)
    tails = jnp.zeros((z.n * z.sides, z.c), F32)
    for r in range(z.r):
        rows = x_ref[:, r].reshape(z.fl * z.w, z.c)
        cut = moved(matrix, rows)
        for k in range(z.n):
            outs[k][r * z.piece : (r + 1) * z.piece] = cut[k * z.piece : (k + 1) * z.piece]
        picked = chooser(z.n * z.sides, z.fl * z.w, functools.partial(edge, r))
        tails += jnp.dot(picked, rows, preferred_element_type=F32)
    tails = tails.astype(BF)
    for k in range(z.n):
        outs[k][z.main : z.main + z.sides] = tails[k * z.sides : (k + 1) * z.sides]


def aside(z, rows):
    count = z.fl * z.w
    left = chooser(count, count, lambda q: jnp.where(q % z.w > 0, q - 1, -1))
    right = chooser(count, count, lambda q: jnp.where(q % z.w < z.w - 1, q + 1, -1))
    return moved(left, rows), rows, moved(right, rows)


def own_inner_kernel(z, x_ref, w_ref, out, beside):
    for r in range(z.r):
        for dj, rows in enumerate(aside(z, x_ref[:, r].reshape(z.fl * z.w, z.c))):
            beside[dj, r] = rows
    for r in range(z.r):
        total = jnp.zeros((z.fl * z.w, z.c), F32)
        for di in range(3):
            if 0 <= r + di - 1 < z.r:
                for dj in range(3):
                    total += jnp.dot(
                        beside[dj, r + di - 1], w_ref[di, dj], preferred_element_type=F32
                    )
        out[r] = total


def own_act_kernel(z, part_ref, near_ref, far_ref, w_ref, cot_ref, out, far, near):
    lower = even("space")
    first = even("tm")
    for r in range(z.r):
        total = part_ref[r]
        for edge, di in ((0, 0), (z.r - 1, 2)):
            if r == edge:
                rows = jnp.where(lower == (di == 2), near_ref[...], far_ref[...])
                for dj, rows in enumerate(aside(z, rows)):
                    total += jnp.dot(rows, w_ref[di, dj], preferred_element_type=F32)
        act = silu(total).reshape(z.fl, z.w, z.c)
        out[:, r] = act
        last = act[z.fl - 1]
        near[r] = jnp.where(first, last, cot_ref[0, r])
        far[r] = jnp.where(first, cot_ref[0, r], last)


def silu(total):
    return (total / (1.0 + jnp.exp(-total))).astype(BF)


def flat(value):
    return value.reshape(-1, value.shape[-1])


def outer(left, right):
    return lax.dot_general(
        flat(left), flat(right), (((0,), (0,)), ((), ())), preferred_element_type=F32
    )


def own_grad_kernel(z, act_ref, cot_ref, out):
    for k in range(3):
        out[:, k * z.c : (k + 1) * z.c] = outer(cot_ref[k:], act_ref[: z.fl - k])


def cross_kernel(z, width, part_ref, far_ref, near_ref, act_ref, cot_ref, keep, send):
    mine = even("space")
    before = jnp.where(even("tm"), far_ref[...], near_ref[...])
    after = jnp.where(even("tm"), near_ref[...], far_ref[...])
    for k in range(3):
        lanes = slice(k * z.c, (k + 1) * z.c)
        grad = part_ref[:, lanes]
        if k == 1:
            grad += outer(cot_ref[0], before)
        if k == 2:
            grad += outer(cot_ref[1], before)
            grad += outer(after, act_ref[z.fl - 2])
        for i in range(z.c // (2 * width)):
            low = grad[2 * i * width : (2 * i + 1) * width]
            high = grad[(2 * i + 1) * width : (2 * i + 2) * width]
            keep[i * width : (i + 1) * width, lanes] = jnp.where(mine, low, high)
            send[i * width : (i + 1) * width, lanes] = jnp.where(mine, high, low).astype(BF)


def gather_matrix(z, me):
    def source(q):
        s = q % z.f // z.fl
        return ((me ^ s) * z.fl + q % z.fl) * z.wc + q // z.f

    return chooser(z.block, z.block, source)


def assemble_kernel(z, *refs):
    parts, (out, near, far) = refs[: z.n], refs[z.n :]
    me = lax.axis_index("tm")
    lower = even("space")
    matrix = gather_matrix(z, me)

    def edge(q):
        head = q // z.f
        s = q % z.f // z.fl
        return ((me ^ s) * 2 * z.r + head) * z.fl + q % z.fl

    count = z.n * z.sides
    tails = jnp.concatenate([p[z.main : z.main + z.sides] for p in parts], axis=0)
    tails = moved(chooser(count, count, edge), tails)
    last = z.f + z.block
    for r in range(z.r):
        rows = jnp.concatenate([p[r * z.piece : (r + 1) * z.piece] for p in parts], axis=0)
        rows = moved(matrix, rows)
        left = tails[r * z.f : (r + 1) * z.f]
        right = tails[(z.r + r) * z.f : (z.r + r + 1) * z.f]
        out[r, 0 : z.f] = left
        out[r, z.f : last] = rows
        out[r, last : last + z.f] = right
    near[...] = jnp.where(lower, out[z.r - 1], out[0])
    far[...] = jnp.where(lower, out[0], out[z.r - 1])


def conv_row(z, w_ref, three):
    total = jnp.zeros((z.block, z.c), F32)
    for di, rows in enumerate(three):
        for dj in range(3):
            total += jnp.dot(
                rows[dj * z.f : dj * z.f + z.block], w_ref[di, dj], preferred_element_type=F32
            )
    return silu(total)


def middle_kernel(z, x_ref, w_ref, out):
    for r in range(1, z.r - 1):
        out[r - 1] = conv_row(z, w_ref, [x_ref.at[r + di] for di in (-1, 0, 1)])


def border_kernel(z, x_ref, near_ref, far_ref, w_ref, out, edges):
    lower = even("space")
    edges[0] = jnp.where(lower, far_ref[...], near_ref[...])
    edges[1] = jnp.where(lower, near_ref[...], far_ref[...])
    out[0] = conv_row(z, w_ref, [edges.at[0], x_ref.at[0], x_ref.at[1]])
    out[1] = conv_row(z, w_ref, [x_ref.at[z.r - 2], x_ref.at[z.r - 1], edges.at[1]])


def staged(z, stages):
    for step in range(z.r + len(stages) - 1):
        for late, stage in reversed(list(enumerate(stages))):
            if 0 <= step - late < z.r:
                stage(step - late)


def main_kernel(
    z, middle_ref, border_ref, x_ref, t_ref, gain_ref, q_ref, k_ref, v_ref, o_ref, *outs
):
    me = lax.axis_index("tm")
    a = lax.broadcasted_iota(jnp.int32, (z.block, z.block), 0)
    b = lax.broadcasted_iota(jnp.int32, (z.block, z.block), 1)
    allowed = (a // z.f == b // z.f) & (b % z.f <= a % z.f)
    scale = float(z.c) ** -0.5

    def source(q):
        t = ((me ^ (q // z.piece)) * z.fl) + q % z.piece // z.wc
        return q % z.wc * z.f + t

    back = chooser(z.block, z.block, source)
    frame = lax.broadcasted_iota(jnp.int32, (z.block, z.c), 0) % z.f
    held = {}

    def activate(r):
        act = border_ref[r // (z.r - 1)] if r in (0, z.r - 1) else middle_ref[r - 1]
        wide = act.astype(F32)
        held["a", r] = [act] + [
            jnp.where(frame >= k, pltpu.roll(wide, k, 0), 0.0).astype(BF) for k in (1, 2)
        ]

    def hide(r):
        temporal = sum(
            jnp.dot(late, t_ref[k], preferred_element_type=F32)
            for k, late in enumerate(held.pop(("a", r)))
        )
        hidden = (x_ref[r, z.f : z.f + z.block].astype(F32) + temporal).astype(BF)
        held["h", r] = hidden

    def norm(r):
        wide = held["h", r].astype(F32)
        mean = jnp.mean(wide * wide, axis=1, keepdims=True)
        held["n", r] = (wide * (1.0 / jnp.sqrt(mean + 1e-06)) * gain_ref[...]).astype(BF)

    def project(r):
        rows = held.pop(("n", r))
        held["q", r], held["k", r], held["v", r] = (
            jnp.dot(rows, w[...], preferred_element_type=F32).astype(BF)
            for w in (q_ref, k_ref, v_ref)
        )

    def score(r):
        held["s", r] = lax.dot_general(
            held.pop(("q", r)),
            held.pop(("k", r)),
            (((1,), (1,)), ((), ())),
            preferred_element_type=F32,
        )

    def weigh(r):
        scores = jnp.where(allowed, held.pop(("s", r)) * scale, -1e30)
        top = jnp.max(scores, axis=1, keepdims=True)
        expon = jnp.where(allowed, jnp.exp(scores - top), 0.0)
        held["t", r] = 1.0 / jnp.sum(expon, axis=1, keepdims=True)
        held["p", r] = expon.astype(BF)

    def mix(r):
        mixed = jnp.dot(held.pop(("p", r)), held.pop(("v", r)), preferred_element_type=F32)
        held["a", r] = (mixed * held.pop(("t", r))).astype(BF)

    def finish(r):
        encoded = held.pop(("h", r)).astype(F32) + jnp.dot(
            held.pop(("a", r)), o_ref[...], preferred_element_type=F32
        )
        held["e", r] = encoded.astype(BF)

    def spread(r):
        encoded = moved(back, held.pop(("e", r)))
        for k in range(z.n):
            outs[k][r] = encoded[k * z.piece : (k + 1) * z.piece]

    staged(z, (activate, hide, norm, project, score, weigh, mix, finish, spread))


def split_kernel(z, keep_ref, got_ref, *outs):
    me = lax.axis_index("tm")
    wide = z.c // z.n
    for tap in range(3):
        place = slice(tap * wide, (tap + 1) * wide)
        if wide % 128 == 0:
            for k in range(z.n):
                lanes = pl.ds(pl.multiple_of(tap * z.c + (me ^ k) * wide, 128), wide)
                total = keep_ref[:, lanes] + got_ref[:, lanes].astype(F32)
                outs[k][:, place] = total.astype(outs[k].dtype)
            continue
        lanes = slice(tap * z.c, (tap + 1) * z.c)
        total = keep_ref[:, lanes] + got_ref[:, lanes].astype(F32)
        for k in range(z.n):
            cut = total[:, 0:wide]
            for i in range(1, z.n):
                cut = jnp.where((me ^ k) == i, total[:, i * wide : (i + 1) * wide], cut)
            outs[k][:, place] = cut.astype(outs[k].dtype)


def swap(value, axis, k):
    count = lax.axis_size(axis)
    return lax.ppermute(value, axis, [(i, i ^ k) for i in range(count)])


def swap_both(near, far, axis):
    pairs = [(i, i + 1) for i in range(1, lax.axis_size(axis) - 1, 2)]
    far = lax.ppermute(far, axis, pairs + [(b, a) for a, b in pairs])
    return swap(near, axis, 1), far


def halve_kernel(z, width, bit, *refs):
    parts, (keep, send) = refs[:-2], refs[-2:]
    total = sum(part[...].astype(F32) for part in parts)
    lower = lax.axis_index("space") // (2 << bit) % 2 == 0
    for i in range(keep.shape[0] // width):
        low = total[2 * i * width : (2 * i + 1) * width]
        high = total[(2 * i + 1) * width : (2 * i + 2) * width]
        rows = slice(i * width, (i + 1) * width)
        keep[rows] = jnp.where(lower, low, high)
        send[rows] = jnp.where(lower, high, low).astype(BF)


def sum_kernel(z, *refs):
    out, wide = refs[-1], z.c // z.n
    total = sum(part[...].astype(F32) for part in refs[:-1])
    for k in range(3):
        out[k] = total[:, k * wide : (k + 1) * wide]


def join_kernel(z, *refs):
    parts, (out, whole, sem) = refs[: z.n], refs[z.n :]
    me = lax.axis_index("tm")
    copies = []
    for f in range(z.fl):
        for k in range(z.n):
            cols = pl.ds(pl.multiple_of((me ^ k) * z.wc, z.wc), z.wc)
            whole[f, :, cols] = parts[k][:, f * z.wc : (f + 1) * z.wc]
        copies.append(pltpu.make_async_copy(whole.at[f], out.at[f], sem.at[f]))
        copies[f].start()
    for copy in copies:
        copy.wait()


def joined(z, back):
    if z.wc % 16 == 0:
        return pl.pallas_call(
            functools.partial(join_kernel, z),
            out_shape=shape((z.fl, z.r, z.w, z.c)),
            in_specs=[VMEM] * z.n,
            out_specs=pl.BlockSpec(memory_space=pl.ANY),
            scratch_shapes=[
                pltpu.VMEM((z.fl, z.r, z.w, z.c), BF),
                pltpu.SemaphoreType.DMA((z.fl,)),
            ],
            compiler_params=pltpu.CompilerParams(vmem_limit_bytes=16 * 2**20),
            cost_estimate=pl.CostEstimate(
                flops=0, bytes_accessed=8 * z.n * z.main * z.c, transcendentals=0
            ),
        )(*back)
    whole = jnp.zeros((z.fl, z.r, z.n, z.wc, z.c), BF)
    for k in range(z.n):
        rows = back[k].reshape(z.r, z.fl, 1, z.wc, z.c).transpose(1, 0, 2, 3, 4)
        whole = lax.dynamic_update_slice_in_dim(whole, rows, lax.axis_index("tm") ^ k, 2)
    return whole.reshape(z.fl, z.r, z.w, z.c)


def on_device(frames_in, spatial, temporal, gain, q_w, k_w, v_w, o_w, cotangent):
    n = lax.axis_size("tm")
    space = lax.axis_size("space")
    z = Sizes(n, *frames_in.shape)
    one = 2 * z.r * z.block * z.c * z.c
    others = sorted(range(1, n), key=lambda k: -k.bit_count())
    width, wide = z.c // space, z.c // n

    def exchange(pieces):
        pieces = list(pieces)
        for k in others:
            pieces[k] = swap(pieces[k], "tm", k)
        return pieces

    edge = shape((z.fl * z.w, z.c))
    packed = call(
        functools.partial(pack_kernel, z),
        [shape((z.main + z.sides, z.c))] * n,
        frames_in,
        flops=one // 2,
    )
    near, far = call(
        functools.partial(edge_kernel, z), [edge, edge], frames_in, packed[0], flops=8 * one
    )
    got = exchange(packed)
    near, far = swap_both(near, far, "space")
    (own,) = call(
        functools.partial(own_inner_kernel, z),
        [shape((z.r, z.fl * z.w, z.c), F32)],
        frames_in,
        spatial,
        flops=8 * one,
        scratch=[pltpu.VMEM((3, z.r, z.fl * z.w, z.c), BF)],
    )
    own_act, far, near = call(
        functools.partial(own_act_kernel, z),
        [shape(frames_in.shape), shape((z.r, z.w, z.c)), shape((z.r, z.w, z.c))],
        own,
        near,
        far,
        spatial,
        cotangent,
        flops=3 * one,
    )
    near, far = swap_both(near, far, "tm")
    (own_grad,) = call(
        functools.partial(own_grad_kernel, z),
        [shape((z.c, 3 * z.c), F32)],
        own_act,
        cotangent,
        flops=9 * one // 4,
    )
    line = z.block + 2 * z.f
    x, close, apart = call(
        functools.partial(assemble_kernel, z),
        [shape((z.r, line, z.c)), shape((line, z.c)), shape((line, z.c))],
        *got,
    )
    close, apart = swap_both(close, apart, "space")
    (middle,) = call(
        functools.partial(middle_kernel, z),
        [shape((z.r - 2, z.block, z.c))],
        x,
        spatial,
        flops=9 * one * (z.r - 2) // z.r,
    )
    tied = lax.optimization_barrier((far, near, middle, close, apart))
    far, near, middle, close, apart = tied
    keep, send = call(
        functools.partial(cross_kernel, z, width),
        [shape((z.c // 2, 3 * z.c), F32), shape((z.c // 2, 3 * z.c))],
        own_grad,
        far,
        near,
        own_act,
        cotangent,
        flops=3 * one // 4,
    )
    other = swap(send, "space", 1)
    x, _ = lax.optimization_barrier((x, send))
    (border,) = call(
        functools.partial(border_kernel, z),
        [shape((2, z.block, z.c))],
        x,
        close,
        apart,
        spatial,
        flops=18 * one // z.r,
        scratch=[pltpu.VMEM((2, line, z.c), BF)],
    )
    other, border = lax.optimization_barrier((other, border))
    pieces = call(
        functools.partial(split_kernel, z),
        [shape((z.c // 2, 3 * wide), F32)] + [shape((z.c // 2, 3 * wide))] * (n - 1),
        keep,
        other,
    )
    border, *pieces = lax.optimization_barrier((border, *pieces))
    pieces = exchange(pieces)
    encoded = call(
        functools.partial(main_kernel, z),
        [shape((z.r, z.piece, z.c))] * n,
        middle,
        border,
        x,
        temporal,
        gain.reshape(1, z.c),
        q_w,
        k_w,
        v_w,
        o_w,
        flops=9 * one,
    )
    back = exchange(encoded)
    pieces = lax.optimization_barrier((*pieces, *encoded))[:n]
    bit = 0
    while 2 << bit < space:
        half = (pieces[0].shape[0] // 2, 3 * wide)
        keep, send = call(
            functools.partial(halve_kernel, z, width, bit), [shape(half, F32), shape(half)], *pieces
        )
        pieces = (keep, swap(send, "space", 2 << bit))
        bit += 1
    (kernel_grad,) = call(
        functools.partial(sum_kernel, z), [shape((3, width, wide), F32)], *pieces
    )
    return joined(z, back), kernel_grad.transpose(0, 2, 1)


def solution(mesh):
    tiles = P("tm", "space", None, None)
    return jax.shard_map(
        on_device,
        mesh=mesh,
        in_specs=(tiles,) + (P(),) * 7 + (tiles,),
        out_specs=(tiles, P(None, "tm", "space")),
        check_vma=False,
    )
```

```python
import functools

import jax
import jax.numpy as jnp
from jax import lax
from jax.experimental import pallas as pl
from jax.experimental.pallas import tpu as pltpu
from jax.sharding import PartitionSpec as P

BF = jnp.bfloat16
F32 = jnp.float32
VMEM = pl.BlockSpec(memory_space=pltpu.VMEM)


def call(kernel, outs, *args, flops=0, scratch=(), limit=16):
    moved = sum(a.size * a.dtype.itemsize for a in args)
    moved += sum(o.size * o.dtype.itemsize for o in outs)
    return pl.pallas_call(
        kernel,
        out_shape=tuple(outs),
        in_specs=[VMEM] * len(args),
        out_specs=tuple(VMEM for _ in outs),
        scratch_shapes=scratch,
        compiler_params=pltpu.CompilerParams(vmem_limit_bytes=limit * 2**20),
        cost_estimate=pl.CostEstimate(flops=flops, bytes_accessed=moved, transcendentals=0),
    )(*args)


def shape(dims, kind=BF):
    return jax.ShapeDtypeStruct(dims, kind)


def chooser(rows, cols, source):
    q = lax.broadcasted_iota(jnp.int32, (rows, cols), 0)
    m = lax.broadcasted_iota(jnp.int32, (rows, cols), 1)
    return jnp.where(source(q) == m, 1.0, 0.0).astype(BF)


def moved(matrix, rows):
    return jnp.dot(matrix, rows, preferred_element_type=F32).astype(BF)


class Sizes:
    def __init__(self, count, frames, rows, cols, chans):
        self.n, self.fl, self.r, self.w, self.c = count, frames, rows, cols, chans
        self.f = count * frames
        self.wc = cols // count
        self.block = self.f * self.wc
        self.piece = frames * self.wc
        self.main = rows * self.piece
        self.sides = 2 * rows * frames


def even(axis):
    return lax.axis_index(axis) % 2 == 0


def edge_kernel(z, x_ref, after_ref, near, far):
    top, bottom = (flat(x_ref[:, r]) for r in (0, z.r - 1))
    near[...] = jnp.where(even("space"), bottom, top)
    far[...] = jnp.where(even("space"), top, bottom)


def pack_kernel(z, x_ref, *outs):
    me = lax.axis_index("tm")

    def source(q):
        k = q // z.piece
        f = q % z.piece // z.wc
        return f * z.w + (me ^ k) * z.wc + q % z.wc

    def edge(r, q):
        k = q // z.sides
        side = q % z.sides // (z.r * z.fl)
        row = q % (z.r * z.fl) // z.fl
        col = (me ^ k) * z.wc - 1 + side * (z.wc + 1)
        inside = (col >= 0) & (col < z.w) & (row == r)
        return jnp.where(inside, q % z.fl * z.w + col, -1)

    matrix = chooser(z.n * z.piece, z.fl * z.w, source)
    tails = jnp.zeros((z.n * z.sides, z.c), F32)
    for r in range(z.r):
        rows = x_ref[:, r].reshape(z.fl * z.w, z.c)
        cut = moved(matrix, rows)
        for k in range(z.n):
            outs[k][r * z.piece : (r + 1) * z.piece] = cut[k * z.piece : (k + 1) * z.piece]
        picked = chooser(z.n * z.sides, z.fl * z.w, functools.partial(edge, r))
        tails += jnp.dot(picked, rows, preferred_element_type=F32)
    tails = tails.astype(BF)
    for k in range(z.n):
        outs[k][z.main : z.main + z.sides] = tails[k * z.sides : (k + 1) * z.sides]


def aside(z, rows):
    count = z.fl * z.w
    left = chooser(count, count, lambda q: jnp.where(q % z.w > 0, q - 1, -1))
    right = chooser(count, count, lambda q: jnp.where(q % z.w < z.w - 1, q + 1, -1))
    return moved(left, rows), rows, moved(right, rows)


def own_inner_kernel(z, x_ref, w_ref, out, beside):
    for r in range(z.r):
        for dj, rows in enumerate(aside(z, x_ref[:, r].reshape(z.fl * z.w, z.c))):
            beside[dj, r] = rows
    for r in range(z.r):
        low, high = max(0, 1 - r), min(3, z.r + 1 - r)
        pieces = [beside[dj, r + di - 1] for di in range(low, high) for dj in range(3)]
        out[r] = taps(pieces, w_ref[low:high])


def own_act_kernel(z, part_ref, near_ref, far_ref, w_ref, cot_ref, out, near, far):
    lower = even("space")
    first = even("tm")
    for r in range(z.r):
        total = part_ref[r]
        for edge, di in ((0, 0), (z.r - 1, 2)):
            if r == edge:
                rows = jnp.where(lower == (di == 2), near_ref[...], far_ref[...])
                total += taps(aside(z, rows), w_ref[di])
        act = silu(total).reshape(z.fl, z.w, z.c)
        out[:, r] = act
        last = act[z.fl - 1]
        near[r] = jnp.where(first, last, cot_ref[0, r])
        far[r] = jnp.where(first, cot_ref[0, r], last)


def silu(total):
    return (total / (1.0 + jnp.exp(-total))).astype(BF)


def flat(value):
    return value.reshape(-1, value.shape[-1])


def outer(left, right):
    return lax.dot_general(
        flat(left), flat(right), (((0,), (0,)), ((), ())), preferred_element_type=F32
    )


def own_grad_kernel(z, act_ref, cot_ref, out):
    for k in range(3):
        out[:, k * z.c : (k + 1) * z.c] = outer(cot_ref[k:], act_ref[: z.fl - k])


def cross_kernel(z, width, part_ref, near_ref, far_ref, act_ref, cot_ref, keep, send):
    mine = even("space")
    before = jnp.where(even("tm"), far_ref[...], near_ref[...])
    after = jnp.where(even("tm"), near_ref[...], far_ref[...])
    for k in range(3):
        lanes = slice(k * z.c, (k + 1) * z.c)
        grad = part_ref[:, lanes]
        if k == 1:
            grad += outer(cot_ref[0], before)
        if k == 2:
            grad += outer(cot_ref[1], before)
            grad += outer(after, act_ref[z.fl - 2])
        for i in range(z.c // (2 * width)):
            low = grad[2 * i * width : (2 * i + 1) * width]
            high = grad[(2 * i + 1) * width : (2 * i + 2) * width]
            keep[i * width : (i + 1) * width, lanes] = jnp.where(mine, low, high)
            send[i * width : (i + 1) * width, lanes] = jnp.where(mine, high, low).astype(BF)


def gather_matrix(z, me):
    def source(q):
        s = q % z.f // z.fl
        return ((me ^ s) * z.fl + q % z.fl) * z.wc + q // z.f

    return chooser(z.block, z.block, source)


def assemble_kernel(z, *refs):
    parts, (out, near, far) = refs[: z.n], refs[z.n :]
    me = lax.axis_index("tm")
    lower = even("space")
    matrix = gather_matrix(z, me)

    def edge(q):
        head = q // z.f
        s = q % z.f // z.fl
        return ((me ^ s) * 2 * z.r + head) * z.fl + q % z.fl

    count = z.n * z.sides
    tails = jnp.concatenate([p[z.main : z.main + z.sides] for p in parts], axis=0)
    tails = moved(chooser(count, count, edge), tails)
    last = z.f + z.block
    for r in range(z.r):
        rows = jnp.concatenate([p[r * z.piece : (r + 1) * z.piece] for p in parts], axis=0)
        rows = moved(matrix, rows)
        left = tails[r * z.f : (r + 1) * z.f]
        right = tails[(z.r + r) * z.f : (z.r + r + 1) * z.f]
        out[r, 0 : z.f] = left
        out[r, z.f : last] = rows
        out[r, last : last + z.f] = right
    near[...] = jnp.where(lower, out[z.r - 1], out[0])
    far[...] = jnp.where(lower, out[0], out[z.r - 1])


def taps(pieces, weights):
    rows = jnp.concatenate(pieces, axis=1)
    return jnp.dot(rows, flat(weights), preferred_element_type=F32)


def conv_row(z, w_ref, three):
    return silu(taps([rows[dj * z.f : dj * z.f + z.block] for rows in three for dj in range(3)], w_ref[...]))


def middle_kernel(z, x_ref, w_ref, out):
    for r in range(1, z.r - 1):
        out[r - 1] = conv_row(z, w_ref, [x_ref.at[r + di] for di in (-1, 0, 1)])


def border_kernel(z, x_ref, near_ref, far_ref, w_ref, out, edges):
    lower = even("space")
    edges[0] = jnp.where(lower, far_ref[...], near_ref[...])
    edges[1] = jnp.where(lower, near_ref[...], far_ref[...])
    out[0] = conv_row(z, w_ref, [edges.at[0], x_ref.at[0], x_ref.at[1]])
    out[1] = conv_row(z, w_ref, [x_ref.at[z.r - 2], x_ref.at[z.r - 1], edges.at[1]])


def staged(z, stages):
    for step in range(z.r + len(stages) - 1):
        for late, stage in reversed(list(enumerate(stages))):
            if 0 <= step - late < z.r:
                stage(step - late)


def main_kernel(
    z, middle_ref, border_ref, x_ref, t_ref, gain_ref, q_ref, k_ref, v_ref, o_ref, *outs
):
    me = lax.axis_index("tm")
    a = lax.broadcasted_iota(jnp.int32, (z.block, z.block), 0)
    b = lax.broadcasted_iota(jnp.int32, (z.block, z.block), 1)
    allowed = (a // z.f == b // z.f) & (b % z.f <= a % z.f)
    scale = float(z.c) ** -0.5

    def source(q):
        t = ((me ^ (q // z.piece)) * z.fl) + q % z.piece // z.wc
        return q % z.wc * z.f + t

    back = chooser(z.block, z.block, source)
    frame = lax.broadcasted_iota(jnp.int32, (z.block, z.c), 0) % z.f
    held = {}

    def activate(r):
        act = border_ref[r // (z.r - 1)] if r in (0, z.r - 1) else middle_ref[r - 1]
        wide = act.astype(F32)
        held["a", r] = [act] + [
            jnp.where(frame >= k, pltpu.roll(wide, k, 0), 0.0).astype(BF) for k in (1, 2)
        ]

    def hide(r):
        temporal = taps(held.pop(("a", r)), t_ref[...])
        hidden = (x_ref[r, z.f : z.f + z.block].astype(F32) + temporal).astype(BF)
        held["h", r] = hidden

    def norm(r):
        wide = held["h", r].astype(F32)
        mean = jnp.mean(wide * wide, axis=1, keepdims=True)
        held["n", r] = (wide * (1.0 / jnp.sqrt(mean + 1e-06)) * gain_ref[...]).astype(BF)

    def project(r):
        rows = held.pop(("n", r))
        held["q", r], held["k", r], held["v", r] = (
            jnp.dot(rows, w[...], preferred_element_type=F32).astype(BF)
            for w in (q_ref, k_ref, v_ref)
        )

    def score(r):
        held["s", r] = lax.dot_general(
            held.pop(("q", r)),
            held.pop(("k", r)),
            (((1,), (1,)), ((), ())),
            preferred_element_type=F32,
        )

    def weigh(r):
        scores = jnp.where(allowed, held.pop(("s", r)) * scale, -1e30)
        top = jnp.max(scores, axis=1, keepdims=True)
        expon = jnp.where(allowed, jnp.exp(scores - top), 0.0)
        held["t", r] = 1.0 / jnp.sum(expon, axis=1, keepdims=True)
        held["p", r] = expon.astype(BF)

    def mix(r):
        mixed = jnp.dot(held.pop(("p", r)), held.pop(("v", r)), preferred_element_type=F32)
        held["a", r] = (mixed * held.pop(("t", r))).astype(BF)

    def finish(r):
        encoded = held.pop(("h", r)).astype(F32) + jnp.dot(
            held.pop(("a", r)), o_ref[...], preferred_element_type=F32
        )
        held["e", r] = encoded.astype(BF)

    def spread(r):
        encoded = moved(back, held.pop(("e", r)))
        for k in range(z.n):
            outs[k][r] = encoded[k * z.piece : (k + 1) * z.piece]

    staged(z, (activate, hide, norm, project, score, weigh, mix, finish, spread))


def split_kernel(z, keep_ref, got_ref, *outs):
    me = lax.axis_index("tm")
    wide = z.c // z.n
    for tap in range(3):
        place = slice(tap * wide, (tap + 1) * wide)
        if wide % 128 == 0:
            for k in range(z.n):
                lanes = pl.ds(pl.multiple_of(tap * z.c + (me ^ k) * wide, 128), wide)
                total = keep_ref[:, lanes] + got_ref[:, lanes].astype(F32)
                outs[k][:, place] = total.astype(outs[k].dtype)
            continue
        lanes = slice(tap * z.c, (tap + 1) * z.c)
        total = keep_ref[:, lanes] + got_ref[:, lanes].astype(F32)
        for k in range(z.n):
            cut = total[:, 0:wide]
            for i in range(1, z.n):
                cut = jnp.where((me ^ k) == i, total[:, i * wide : (i + 1) * wide], cut)
            outs[k][:, place] = cut.astype(outs[k].dtype)


def swap(value, axis, k):
    count = lax.axis_size(axis)
    return lax.ppermute(value, axis, [(i, i ^ k) for i in range(count)])


def swap_both(near, far, axis):
    pairs = [(i, i + 1) for i in range(1, lax.axis_size(axis) - 1, 2)]
    far = lax.ppermute(far, axis, pairs + [(b, a) for a, b in pairs])
    return swap(near, axis, 1), far


def halve_kernel(z, width, bit, *refs):
    parts, (keep, send) = refs[:-2], refs[-2:]
    total = sum(part[...].astype(F32) for part in parts)
    lower = lax.axis_index("space") // (2 << bit) % 2 == 0
    for i in range(keep.shape[0] // width):
        low = total[2 * i * width : (2 * i + 1) * width]
        high = total[(2 * i + 1) * width : (2 * i + 2) * width]
        rows = slice(i * width, (i + 1) * width)
        keep[rows] = jnp.where(lower, low, high)
        send[rows] = jnp.where(lower, high, low).astype(BF)


def sum_kernel(z, *refs):
    out, wide = refs[-1], z.c // z.n
    total = sum(part[...].astype(F32) for part in refs[:-1])
    for k in range(3):
        out[k] = total[:, k * wide : (k + 1) * wide]


def join_kernel(z, *refs):
    parts, (out, whole, sem) = refs[: z.n], refs[z.n :]
    me = lax.axis_index("tm")
    copies = []
    for f in range(z.fl):
        for k in range(z.n):
            cols = pl.ds(pl.multiple_of((me ^ k) * z.wc, z.wc), z.wc)
            whole[f, :, cols] = parts[k][:, f * z.wc : (f + 1) * z.wc]
        copies.append(pltpu.make_async_copy(whole.at[f], out.at[f], sem.at[f]))
        copies[f].start()
    for copy in copies:
        copy.wait()


def joined(z, back):
    if z.wc % 16 == 0:
        return pl.pallas_call(
            functools.partial(join_kernel, z),
            out_shape=shape((z.fl, z.r, z.w, z.c)),
            in_specs=[VMEM] * z.n,
            out_specs=pl.BlockSpec(memory_space=pl.ANY),
            scratch_shapes=[
                pltpu.VMEM((z.fl, z.r, z.w, z.c), BF),
                pltpu.SemaphoreType.DMA((z.fl,)),
            ],
            compiler_params=pltpu.CompilerParams(vmem_limit_bytes=16 * 2**20),
            cost_estimate=pl.CostEstimate(
                flops=0, bytes_accessed=8 * z.n * z.main * z.c, transcendentals=0
            ),
        )(*back)
    whole = jnp.zeros((z.fl, z.r, z.n, z.wc, z.c), BF)
    for k in range(z.n):
        rows = back[k].reshape(z.r, z.fl, 1, z.wc, z.c).transpose(1, 0, 2, 3, 4)
        whole = lax.dynamic_update_slice_in_dim(whole, rows, lax.axis_index("tm") ^ k, 2)
    return whole.reshape(z.fl, z.r, z.w, z.c)


def on_device(frames_in, spatial, temporal, gain, q_w, k_w, v_w, o_w, cotangent):
    n = lax.axis_size("tm")
    space = lax.axis_size("space")
    z = Sizes(n, *frames_in.shape)
    one = 2 * z.r * z.block * z.c * z.c
    others = sorted(range(1, n), key=lambda k: -k.bit_count())
    width, wide = z.c // space, z.c // n

    def exchange(pieces):
        pieces = list(pieces)
        for k in others:
            pieces[k] = swap(pieces[k], "tm", k)
        return pieces

    edge = shape((z.fl * z.w, z.c))
    packed = call(
        functools.partial(pack_kernel, z),
        [shape((z.main + z.sides, z.c))] * n,
        frames_in,
        flops=one // 2,
    )
    near, far = call(
        functools.partial(edge_kernel, z), [edge, edge], frames_in, packed[0], flops=8 * one
    )
    got = exchange(packed)
    near, far = swap_both(near, far, "space")
    (own,) = call(
        functools.partial(own_inner_kernel, z),
        [shape((z.r, z.fl * z.w, z.c), F32)],
        frames_in,
        spatial,
        flops=8 * one,
        scratch=[pltpu.VMEM((3, z.r, z.fl * z.w, z.c), BF)],
    )
    own_act, near, far = call(
        functools.partial(own_act_kernel, z),
        [shape(frames_in.shape), shape((z.r, z.w, z.c)), shape((z.r, z.w, z.c))],
        own,
        near,
        far,
        spatial,
        cotangent,
        flops=3 * one,
    )
    near, far = swap_both(near, far, "tm")
    (own_grad,) = call(
        functools.partial(own_grad_kernel, z),
        [shape((z.c, 3 * z.c), F32)],
        own_act,
        cotangent,
        flops=9 * one // 4,
    )
    line = z.block + 2 * z.f
    x, close, apart = call(
        functools.partial(assemble_kernel, z),
        [shape((z.r, line, z.c)), shape((line, z.c)), shape((line, z.c))],
        *got,
    )
    close, apart = swap_both(close, apart, "space")
    (middle,) = call(
        functools.partial(middle_kernel, z),
        [shape((z.r - 2, z.block, z.c))],
        x,
        spatial,
        flops=9 * one * (z.r - 2) // z.r,
    )
    tied = lax.optimization_barrier((near, far, middle, close, apart))
    near, far, middle, close, apart = tied
    keep, send = call(
        functools.partial(cross_kernel, z, width),
        [shape((z.c // 2, 3 * z.c), F32), shape((z.c // 2, 3 * z.c))],
        own_grad,
        near,
        far,
        own_act,
        cotangent,
        flops=3 * one // 4,
    )
    other = swap(send, "space", 1)
    x, _ = lax.optimization_barrier((x, send))
    (border,) = call(
        functools.partial(border_kernel, z),
        [shape((2, z.block, z.c))],
        x,
        close,
        apart,
        spatial,
        flops=18 * one // z.r,
        scratch=[pltpu.VMEM((2, line, z.c), BF)],
    )
    other, border = lax.optimization_barrier((other, border))
    pieces = call(
        functools.partial(split_kernel, z),
        [shape((z.c // 2, 3 * wide), F32)] + [shape((z.c // 2, 3 * wide))] * (n - 1),
        keep,
        other,
    )
    border, *pieces = lax.optimization_barrier((border, *pieces))
    pieces = exchange(pieces)
    encoded = call(
        functools.partial(main_kernel, z),
        [shape((z.r, z.piece, z.c))] * n,
        middle,
        border,
        x,
        temporal,
        gain.reshape(1, z.c),
        q_w,
        k_w,
        v_w,
        o_w,
        flops=9 * one,
    )
    back = exchange(encoded)
    pieces = lax.optimization_barrier((*pieces, *encoded))[:n]
    bit = 0
    while 2 << bit < space:
        half = (pieces[0].shape[0] // 2, 3 * wide)
        keep, send = call(
            functools.partial(halve_kernel, z, width, bit), [shape(half, F32), shape(half)], *pieces
        )
        pieces = (keep, swap(send, "space", 2 << bit))
        bit += 1
    (kernel_grad,) = call(
        functools.partial(sum_kernel, z), [shape((3, width, wide), F32)], *pieces
    )
    return joined(z, back), kernel_grad.transpose(0, 2, 1)


def solution(mesh):
    tiles = P("tm", "space", None, None)
    return jax.shard_map(
        on_device,
        mesh=mesh,
        in_specs=(tiles,) + (P(),) * 7 + (tiles,),
        out_specs=(tiles, P(None, "tm", "space")),
        check_vma=False,
    )
```

```python
import functools

import jax
import jax.numpy as jnp
from jax import lax
from jax.experimental import pallas as pl
from jax.experimental.pallas import tpu as pltpu
from jax.sharding import PartitionSpec as P

BF = jnp.bfloat16
F32 = jnp.float32
VMEM = pl.BlockSpec(memory_space=pltpu.VMEM)


def call(kernel, outs, *args, flops=0, scratch=(), limit=16):
    moved = sum(a.size * a.dtype.itemsize for a in args)
    moved += sum(o.size * o.dtype.itemsize for o in outs)
    return pl.pallas_call(
        kernel,
        out_shape=tuple(outs),
        in_specs=[VMEM] * len(args),
        out_specs=tuple(VMEM for _ in outs),
        scratch_shapes=scratch,
        compiler_params=pltpu.CompilerParams(vmem_limit_bytes=limit * 2**20),
        cost_estimate=pl.CostEstimate(flops=flops, bytes_accessed=moved, transcendentals=0),
    )(*args)


def shape(dims, kind=BF):
    return jax.ShapeDtypeStruct(dims, kind)


def chooser(rows, cols, source):
    q = lax.broadcasted_iota(jnp.int32, (rows, cols), 0)
    m = lax.broadcasted_iota(jnp.int32, (rows, cols), 1)
    return jnp.where(source(q) == m, 1.0, 0.0).astype(BF)


def moved(matrix, rows):
    return jnp.dot(matrix, rows, preferred_element_type=F32).astype(BF)


class Sizes:
    def __init__(self, count, frames, rows, cols, chans):
        self.n, self.fl, self.r, self.w, self.c = count, frames, rows, cols, chans
        self.f = count * frames
        self.wc = cols // count
        self.block = self.f * self.wc
        self.piece = frames * self.wc
        self.main = rows * self.piece
        self.sides = 2 * rows * frames


def even(axis):
    return lax.axis_index(axis) % 2 == 0


def edge_kernel(z, x_ref, after_ref, near, far):
    top, bottom = (flat(x_ref[:, r]) for r in (0, z.r - 1))
    near[...] = jnp.where(even("space"), bottom, top)
    far[...] = jnp.where(even("space"), top, bottom)


def pack_kernel(z, x_ref, *outs):
    me = lax.axis_index("tm")

    def source(q):
        k = q // z.piece
        f = q % z.piece // z.wc
        return f * z.w + (me ^ k) * z.wc + q % z.wc

    def edge(r, q):
        k = q // z.sides
        side = q % z.sides // (z.r * z.fl)
        row = q % (z.r * z.fl) // z.fl
        col = (me ^ k) * z.wc - 1 + side * (z.wc + 1)
        inside = (col >= 0) & (col < z.w) & (row == r)
        return jnp.where(inside, q % z.fl * z.w + col, -1)

    matrix = chooser(z.n * z.piece, z.fl * z.w, source)
    tails = jnp.zeros((z.n * z.sides, z.c), F32)
    for r in range(z.r):
        rows = x_ref[:, r].reshape(z.fl * z.w, z.c)
        cut = moved(matrix, rows)
        for k in range(z.n):
            outs[k][r * z.piece : (r + 1) * z.piece] = cut[k * z.piece : (k + 1) * z.piece]
        picked = chooser(z.n * z.sides, z.fl * z.w, functools.partial(edge, r))
        tails += jnp.dot(picked, rows, preferred_element_type=F32)
    tails = tails.astype(BF)
    for k in range(z.n):
        outs[k][z.main : z.main + z.sides] = tails[k * z.sides : (k + 1) * z.sides]


def aside(z, rows):
    count = z.fl * z.w
    left = chooser(count, count, lambda q: jnp.where(q % z.w > 0, q - 1, -1))
    right = chooser(count, count, lambda q: jnp.where(q % z.w < z.w - 1, q + 1, -1))
    return moved(left, rows), rows, moved(right, rows)


def own_inner_kernel(z, x_ref, w_ref, out, beside):
    for r in range(z.r):
        for dj, rows in enumerate(aside(z, x_ref[:, r].reshape(z.fl * z.w, z.c))):
            beside[dj, r] = rows
    for r in range(z.r):
        low, high = max(0, 1 - r), min(3, z.r + 1 - r)
        pieces = [beside[dj, r + di - 1] for di in range(low, high) for dj in range(3)]
        out[r] = taps(pieces, w_ref[low:high])


def own_act_kernel(z, part_ref, near_ref, far_ref, w_ref, out):
    lower = even("space")
    for r in range(z.r):
        total = part_ref[r]
        for edge, di in ((0, 0), (z.r - 1, 2)):
            if r == edge:
                rows = jnp.where(lower == (di == 2), near_ref[...], far_ref[...])
                total += taps(aside(z, rows), w_ref[di])
        out[:, r] = silu(total).reshape(z.fl, z.w, z.c)


def silu(total):
    return (total / (1.0 + jnp.exp(-total))).astype(BF)


def flat(value):
    return value.reshape(-1, value.shape[-1])


def outer(left, right):
    return lax.dot_general(
        flat(left), flat(right), (((0,), (0,)), ((), ())), preferred_element_type=F32
    )


def own_grad_kernel(z, act_ref, cot_ref, out):
    for k in range(3):
        out[:, k * z.c : (k + 1) * z.c] = outer(cot_ref[k:], act_ref[: z.fl - k])


def head_kernel(z, cot_ref, after_ref, keep, send):
    me = lax.axis_index("tm")

    def source(q):
        k = q // (2 * z.wc)
        return q % (2 * z.wc) // z.wc * z.w + (me ^ k) * z.wc + q % z.wc

    matrix = chooser(2 * z.w, 2 * z.w, source)
    for r in range(z.r):
        cut = moved(matrix, flat(cot_ref[0:2, r]))
        for k in range(z.n):
            out = (keep, send)[k % 2]
            out[k // 2, r] = cut[2 * z.wc * k : 2 * z.wc * (k + 1)]


def relay_kernel(picks, *refs):
    for i, (array, place) in enumerate(picks):
        refs[-1][i] = refs[array][place]


def cross_kernel(z, width, picks, part_ref, middle_ref, border_ref, *refs):
    heads, (keep, send, cot, late) = refs[:-4], refs[-4:]
    me = lax.axis_index("tm")
    count = 2 * z.n * z.wc

    def head(q):
        s = q % (2 * z.n) // 2
        return ((me ^ s) * 2 + q % 2) * z.wc + q // (2 * z.n)

    def earlier(k, q):
        s = q % (2 * z.n) // 2
        return jnp.where((s > 0) & (q % 2 < k), q // (2 * z.n) * z.f + s * z.fl + q % 2 - k, -1)

    first = chooser(count, count, head)
    backs = [chooser(count, z.block, functools.partial(earlier, k)) for k in (1, 2)]
    for r in range(z.r):
        rows = slice(r * count, (r + 1) * count)
        pieces = [heads[array][place, r] for array, place in picks]
        cot[rows] = moved(first, jnp.concatenate(pieces, axis=0))
        act = border_ref[r // (z.r - 1)] if r in (0, z.r - 1) else middle_ref[r - 1]
        for k in (1, 2):
            late[rows, (k - 1) * z.c : k * z.c] = moved(backs[k - 1], act)
    added = outer(cot[...], late[...])
    mine = even("space")
    for k in range(3):
        lanes = slice(k * z.c, (k + 1) * z.c)
        grad = part_ref[:, lanes]
        if k:
            grad += added[:, (k - 1) * z.c : k * z.c]
        for i in range(z.c // (2 * width)):
            low = grad[2 * i * width : (2 * i + 1) * width]
            high = grad[(2 * i + 1) * width : (2 * i + 2) * width]
            keep[i * width : (i + 1) * width, lanes] = jnp.where(mine, low, high)
            send[i * width : (i + 1) * width, lanes] = jnp.where(mine, high, low).astype(BF)


def gather_matrix(z, me):
    def source(q):
        s = q % z.f // z.fl
        return ((me ^ s) * z.fl + q % z.fl) * z.wc + q // z.f

    return chooser(z.block, z.block, source)


def assemble_kernel(z, *refs):
    parts, (out, near, far) = refs[: z.n], refs[z.n :]
    me = lax.axis_index("tm")
    lower = even("space")
    matrix = gather_matrix(z, me)

    def edge(q):
        head = q // z.f
        s = q % z.f // z.fl
        return ((me ^ s) * 2 * z.r + head) * z.fl + q % z.fl

    count = z.n * z.sides
    tails = jnp.concatenate([p[z.main : z.main + z.sides] for p in parts], axis=0)
    tails = moved(chooser(count, count, edge), tails)
    last = z.f + z.block
    for r in range(z.r):
        rows = jnp.concatenate([p[r * z.piece : (r + 1) * z.piece] for p in parts], axis=0)
        rows = moved(matrix, rows)
        left = tails[r * z.f : (r + 1) * z.f]
        right = tails[(z.r + r) * z.f : (z.r + r + 1) * z.f]
        out[r, 0 : z.f] = left
        out[r, z.f : last] = rows
        out[r, last : last + z.f] = right
    near[...] = jnp.where(lower, out[z.r - 1], out[0])
    far[...] = jnp.where(lower, out[0], out[z.r - 1])


def taps(pieces, weights):
    rows = jnp.concatenate(pieces, axis=1)
    return jnp.dot(rows, flat(weights), preferred_element_type=F32)


def conv_row(z, w_ref, three):
    return silu(taps([rows[dj * z.f : dj * z.f + z.block] for rows in three for dj in range(3)], w_ref[...]))


def middle_kernel(z, x_ref, w_ref, out):
    for r in range(1, z.r - 1):
        out[r - 1] = conv_row(z, w_ref, [x_ref.at[r + di] for di in (-1, 0, 1)])


def border_kernel(z, x_ref, near_ref, far_ref, w_ref, out, edges):
    lower = even("space")
    edges[0] = jnp.where(lower, far_ref[...], near_ref[...])
    edges[1] = jnp.where(lower, near_ref[...], far_ref[...])
    out[0] = conv_row(z, w_ref, [edges.at[0], x_ref.at[0], x_ref.at[1]])
    out[1] = conv_row(z, w_ref, [x_ref.at[z.r - 2], x_ref.at[z.r - 1], edges.at[1]])


def staged(z, stages):
    for step in range(z.r + len(stages) - 1):
        for late, stage in reversed(list(enumerate(stages))):
            if 0 <= step - late < z.r:
                stage(step - late)


def norm_kernel(
    z, middle_ref, border_ref, x_ref, t_ref, gain_ref, hidden_ref, normed_ref
):
    frame = lax.broadcasted_iota(jnp.int32, (z.block, z.c), 0) % z.f
    held = {}

    def activate(r):
        act = border_ref[r // (z.r - 1)] if r in (0, z.r - 1) else middle_ref[r - 1]
        wide = act.astype(F32)
        held["a", r] = [act] + [
            jnp.where(frame >= k, pltpu.roll(wide, k, 0), 0.0).astype(BF) for k in (1, 2)
        ]

    def hide(r):
        temporal = taps(held.pop(("a", r)), t_ref[...])
        hidden = (x_ref[r, z.f : z.f + z.block].astype(F32) + temporal).astype(BF)
        hidden_ref[r] = hidden
        held["h", r] = hidden

    def norm(r):
        wide = held.pop(("h", r)).astype(F32)
        mean = jnp.mean(wide * wide, axis=1, keepdims=True)
        normed_ref[r] = (wide * (1.0 / jnp.sqrt(mean + 1e-06)) * gain_ref[...]).astype(BF)

    staged(z, (activate, hide, norm))


def attend_kernel(z, hidden_ref, normed_ref, q_ref, k_ref, v_ref, o_ref, *outs):
    me = lax.axis_index("tm")
    a = lax.broadcasted_iota(jnp.int32, (z.block, z.block), 0)
    b = lax.broadcasted_iota(jnp.int32, (z.block, z.block), 1)
    allowed = (a // z.f == b // z.f) & (b % z.f <= a % z.f)
    scale = float(z.c) ** -0.5

    def source(q):
        t = ((me ^ (q // z.piece)) * z.fl) + q % z.piece // z.wc
        return q % z.wc * z.f + t

    back = chooser(z.block, z.block, source)
    held = {}

    def project(r):
        rows = normed_ref[r]
        held["q", r], held["k", r], held["v", r] = (
            jnp.dot(rows, w[...], preferred_element_type=F32).astype(BF)
            for w in (q_ref, k_ref, v_ref)
        )

    def score(r):
        held["s", r] = lax.dot_general(
            held.pop(("q", r)),
            held.pop(("k", r)),
            (((1,), (1,)), ((), ())),
            preferred_element_type=F32,
        )

    def weigh(r):
        scores = jnp.where(allowed, held.pop(("s", r)) * scale, -1e30)
        top = jnp.max(scores, axis=1, keepdims=True)
        expon = jnp.where(allowed, jnp.exp(scores - top), 0.0)
        held["t", r] = 1.0 / jnp.sum(expon, axis=1, keepdims=True)
        held["p", r] = expon.astype(BF)

    def mix(r):
        mixed = jnp.dot(held.pop(("p", r)), held.pop(("v", r)), preferred_element_type=F32)
        held["a", r] = (mixed * held.pop(("t", r))).astype(BF)

    def finish(r):
        encoded = hidden_ref[r].astype(F32) + jnp.dot(
            held.pop(("a", r)), o_ref[...], preferred_element_type=F32
        )
        held["e", r] = encoded.astype(BF)

    def spread(r):
        encoded = moved(back, held.pop(("e", r)))
        for k in range(z.n):
            outs[k][r] = encoded[k * z.piece : (k + 1) * z.piece]

    staged(z, (project, score, weigh, mix, finish, spread))


def split_kernel(z, keep_ref, got_ref, *outs):
    me = lax.axis_index("tm")
    wide = z.c // z.n
    for tap in range(3):
        place = slice(tap * wide, (tap + 1) * wide)
        if wide % 128 == 0:
            for k in range(z.n):
                lanes = pl.ds(pl.multiple_of(tap * z.c + (me ^ k) * wide, 128), wide)
                total = keep_ref[:, lanes] + got_ref[:, lanes].astype(F32)
                outs[k][:, place] = total.astype(outs[k].dtype)
            continue
        lanes = slice(tap * z.c, (tap + 1) * z.c)
        total = keep_ref[:, lanes] + got_ref[:, lanes].astype(F32)
        for k in range(z.n):
            cut = total[:, 0:wide]
            for i in range(1, z.n):
                cut = jnp.where((me ^ k) == i, total[:, i * wide : (i + 1) * wide], cut)
            outs[k][:, place] = cut.astype(outs[k].dtype)


def swap(value, axis, k):
    count = lax.axis_size(axis)
    return lax.ppermute(value, axis, [(i, i ^ k) for i in range(count)])


def swap_both(near, far, axis):
    pairs = [(i, i + 1) for i in range(1, lax.axis_size(axis) - 1, 2)]
    far = lax.ppermute(far, axis, pairs + [(b, a) for a, b in pairs])
    return swap(near, axis, 1), far


def halve_kernel(z, width, bit, *refs):
    parts, (keep, send) = refs[:-2], refs[-2:]
    total = sum(part[...].astype(F32) for part in parts)
    lower = lax.axis_index("space") // (2 << bit) % 2 == 0
    for i in range(keep.shape[0] // width):
        low = total[2 * i * width : (2 * i + 1) * width]
        high = total[(2 * i + 1) * width : (2 * i + 2) * width]
        rows = slice(i * width, (i + 1) * width)
        keep[rows] = jnp.where(lower, low, high)
        send[rows] = jnp.where(lower, high, low).astype(BF)


def sum_kernel(z, *refs):
    out, wide = refs[-1], z.c // z.n
    total = sum(part[...].astype(F32) for part in refs[:-1])
    for k in range(3):
        out[k] = total[:, k * wide : (k + 1) * wide]


def join_kernel(z, *refs):
    parts, (out, whole, sem) = refs[: z.n], refs[z.n :]
    me = lax.axis_index("tm")
    copies = []
    for f in range(z.fl):
        for k in range(z.n):
            cols = pl.ds(pl.multiple_of((me ^ k) * z.wc, z.wc), z.wc)
            whole[f, :, cols] = parts[k][:, f * z.wc : (f + 1) * z.wc]
        copies.append(pltpu.make_async_copy(whole.at[f], out.at[f], sem.at[f]))
        copies[f].start()
    for copy in copies:
        copy.wait()


def joined(z, back):
    if z.wc % 16 == 0:
        return pl.pallas_call(
            functools.partial(join_kernel, z),
            out_shape=shape((z.fl, z.r, z.w, z.c)),
            in_specs=[VMEM] * z.n,
            out_specs=pl.BlockSpec(memory_space=pl.ANY),
            scratch_shapes=[
                pltpu.VMEM((z.fl, z.r, z.w, z.c), BF),
                pltpu.SemaphoreType.DMA((z.fl,)),
            ],
            compiler_params=pltpu.CompilerParams(vmem_limit_bytes=16 * 2**20),
            cost_estimate=pl.CostEstimate(
                flops=0, bytes_accessed=8 * z.n * z.main * z.c, transcendentals=0
            ),
        )(*back)
    whole = jnp.zeros((z.fl, z.r, z.n, z.wc, z.c), BF)
    for k in range(z.n):
        rows = back[k].reshape(z.r, z.fl, 1, z.wc, z.c).transpose(1, 0, 2, 3, 4)
        whole = lax.dynamic_update_slice_in_dim(whole, rows, lax.axis_index("tm") ^ k, 2)
    return whole.reshape(z.fl, z.r, z.w, z.c)


def on_device(frames_in, spatial, temporal, gain, q_w, k_w, v_w, o_w, cotangent):
    n = lax.axis_size("tm")
    space = lax.axis_size("space")
    z = Sizes(n, *frames_in.shape)
    one = 2 * z.r * z.block * z.c * z.c
    others = sorted(range(1, n), key=lambda k: -k.bit_count())
    width, wide = z.c // space, z.c // n

    def exchange(pieces):
        pieces = list(pieces)
        for k in others:
            pieces[k] = swap(pieces[k], "tm", k)
        return pieces

    edge = shape((z.fl * z.w, z.c))
    packed = call(
        functools.partial(pack_kernel, z),
        [shape((z.main + z.sides, z.c))] * n,
        frames_in,
        flops=one // 2,
    )
    near, far = call(
        functools.partial(edge_kernel, z), [edge, edge], frames_in, packed[0], flops=8 * one
    )
    got = exchange(packed)
    near, far = swap_both(near, far, "space")
    (own,) = call(
        functools.partial(own_inner_kernel, z),
        [shape((z.r, z.fl * z.w, z.c), F32)],
        frames_in,
        spatial,
        flops=8 * one,
        scratch=[pltpu.VMEM((3, z.r, z.fl * z.w, z.c), BF)],
    )
    (own_act,) = call(
        functools.partial(own_act_kernel, z),
        [shape(frames_in.shape)],
        own,
        near,
        far,
        spatial,
        flops=3 * one,
    )
    kept, sent = call(
        functools.partial(head_kernel, z),
        [shape((n // 2, z.r, 2 * z.wc, z.c))] * 2,
        cotangent,
        own_act,
    )
    arrays = [kept, swap(sent, "tm", 1)]
    heads = [(0, i, 2 * i, 0) for i in range(n // 2)] + [(1, i, 2 * i, 1) for i in range(n // 2)]
    bit = 2
    while bit < n:
        picks = [head for head in heads if head[2] & bit]
        (relayed,) = call(
            functools.partial(relay_kernel, [head[:2] for head in picks]),
            [shape((len(picks),) + kept.shape[1:])],
            *arrays,
        )
        moves = [(len(arrays), i, k ^ bit, s ^ bit) for i, (_, _, k, s) in enumerate(picks)]
        heads = [head for head in heads if not head[2] & bit] + moves
        arrays.append(swap(relayed, "tm", bit))
        bit *= 2
    heads = [head[:2] for head in sorted(heads, key=lambda head: head[3])]
    (own_grad,) = call(
        functools.partial(own_grad_kernel, z),
        [shape((z.c, 3 * z.c), F32)],
        own_act,
        cotangent,
        flops=9 * one // 4,
    )
    line = z.block + 2 * z.f
    own_grad, *got = lax.optimization_barrier((own_grad, *got))
    x, close, apart = call(
        functools.partial(assemble_kernel, z),
        [shape((z.r, line, z.c)), shape((line, z.c)), shape((line, z.c))],
        *got,
    )
    close, apart = swap_both(close, apart, "space")
    (middle,) = call(
        functools.partial(middle_kernel, z),
        [shape((z.r - 2, z.block, z.c))],
        x,
        spatial,
        flops=9 * one * (z.r - 2) // z.r,
    )
    (border,) = call(
        functools.partial(border_kernel, z),
        [shape((2, z.block, z.c))],
        x,
        close,
        apart,
        spatial,
        flops=18 * one // z.r,
        scratch=[pltpu.VMEM((2, line, z.c), BF)],
    )
    count = 2 * n * z.wc * z.r
    keep, send = call(
        functools.partial(cross_kernel, z, width, heads),
        [shape((z.c // 2, 3 * z.c), F32), shape((z.c // 2, 3 * z.c))],
        own_grad,
        middle,
        border,
        *arrays,
        flops=2 * one,
        scratch=[pltpu.VMEM((count, z.c), BF), pltpu.VMEM((count, 2 * z.c), BF)],
    )
    other = swap(send, "space", 1)
    border, _ = lax.optimization_barrier((border, send))
    hidden, normed = call(
        functools.partial(norm_kernel, z),
        [shape((z.r, z.block, z.c))] * 2,
        middle,
        border,
        x,
        temporal,
        gain.reshape(1, z.c),
        flops=3 * one,
    )
    pieces = call(
        functools.partial(split_kernel, z),
        [shape((z.c // 2, 3 * wide), F32)] + [shape((z.c // 2, 3 * wide))] * (n - 1),
        keep,
        other,
    )
    normed, *pieces = lax.optimization_barrier((normed, *pieces))
    pieces = exchange(pieces)
    encoded = call(
        functools.partial(attend_kernel, z),
        [shape((z.r, z.piece, z.c))] * n,
        hidden,
        normed,
        q_w,
        k_w,
        v_w,
        o_w,
        flops=5 * one,
    )
    back = exchange(encoded)
    pieces = lax.optimization_barrier((*pieces, *encoded))[:n]
    bit = 0
    while 2 << bit < space:
        half = (pieces[0].shape[0] // 2, 3 * wide)
        keep, send = call(
            functools.partial(halve_kernel, z, width, bit), [shape(half, F32), shape(half)], *pieces
        )
        pieces = (keep, swap(send, "space", 2 << bit))
        bit += 1
    (kernel_grad,) = call(
        functools.partial(sum_kernel, z), [shape((3, width, wide), F32)], *pieces
    )
    kernel_grad, *back = lax.optimization_barrier((kernel_grad, *back))
    return joined(z, back), kernel_grad.transpose(0, 2, 1)


def solution(mesh):
    tiles = P("tm", "space", None, None)
    return jax.shard_map(
        on_device,
        mesh=mesh,
        in_specs=(tiles,) + (P(),) * 7 + (tiles,),
        out_specs=(tiles, P(None, "tm", "space")),
        check_vma=False,
    )
```

```python
import functools

import jax
import jax.numpy as jnp
from jax import lax
from jax.experimental import pallas as pl
from jax.experimental.pallas import tpu as pltpu
from jax.sharding import PartitionSpec as P

BF = jnp.bfloat16
F32 = jnp.float32
VMEM = pl.BlockSpec(memory_space=pltpu.VMEM)


def call(kernel, outs, *args, flops=0, scratch=(), limit=16):
    moved = sum(a.size * a.dtype.itemsize for a in args)
    moved += sum(o.size * o.dtype.itemsize for o in outs)
    return pl.pallas_call(
        kernel,
        out_shape=tuple(outs),
        in_specs=[VMEM] * len(args),
        out_specs=tuple(VMEM for _ in outs),
        scratch_shapes=scratch,
        compiler_params=pltpu.CompilerParams(vmem_limit_bytes=limit * 2**20),
        cost_estimate=pl.CostEstimate(flops=flops, bytes_accessed=moved, transcendentals=0),
    )(*args)


def shape(dims, kind=BF):
    return jax.ShapeDtypeStruct(dims, kind)


def chooser(rows, cols, source):
    q = lax.broadcasted_iota(jnp.int32, (rows, cols), 0)
    m = lax.broadcasted_iota(jnp.int32, (rows, cols), 1)
    return jnp.where(source(q) == m, 1.0, 0.0).astype(BF)


def moved(matrix, rows):
    return jnp.dot(matrix, rows, preferred_element_type=F32).astype(BF)


class Sizes:
    def __init__(self, count, frames, rows, cols, chans):
        self.n, self.fl, self.r, self.w, self.c = count, frames, rows, cols, chans
        self.f = count * frames
        self.wc = cols // count
        self.block = self.f * self.wc
        self.piece = frames * self.wc
        self.main = rows * self.piece
        self.sides = 2 * rows * frames


def even(axis):
    return lax.axis_index(axis) % 2 == 0


def edge_kernel(z, x_ref, after_ref, near, far):
    top, bottom = (flat(x_ref[:, r]) for r in (0, z.r - 1))
    near[...] = jnp.where(even("space"), bottom, top)
    far[...] = jnp.where(even("space"), top, bottom)


def pack_kernel(z, x_ref, *outs):
    me = lax.axis_index("tm")

    def source(q):
        k = q // z.piece
        f = q % z.piece // z.wc
        return f * z.w + (me ^ k) * z.wc + q % z.wc

    def edge(r, q):
        k = q // z.sides
        side = q % z.sides // (z.r * z.fl)
        row = q % (z.r * z.fl) // z.fl
        col = (me ^ k) * z.wc - 1 + side * (z.wc + 1)
        inside = (col >= 0) & (col < z.w) & (row == r)
        return jnp.where(inside, q % z.fl * z.w + col, -1)

    matrix = chooser(z.n * z.piece, z.fl * z.w, source)
    tails = jnp.zeros((z.n * z.sides, z.c), F32)
    for r in range(z.r):
        rows = x_ref[:, r].reshape(z.fl * z.w, z.c)
        cut = moved(matrix, rows)
        for k in range(z.n):
            outs[k][r * z.piece : (r + 1) * z.piece] = cut[k * z.piece : (k + 1) * z.piece]
        picked = chooser(z.n * z.sides, z.fl * z.w, functools.partial(edge, r))
        tails += jnp.dot(picked, rows, preferred_element_type=F32)
    tails = tails.astype(BF)
    for k in range(z.n):
        outs[k][z.main : z.main + z.sides] = tails[k * z.sides : (k + 1) * z.sides]


def aside(z, rows):
    count = z.fl * z.w
    left = chooser(count, count, lambda q: jnp.where(q % z.w > 0, q - 1, -1))
    right = chooser(count, count, lambda q: jnp.where(q % z.w < z.w - 1, q + 1, -1))
    return moved(left, rows), rows, moved(right, rows)


def own_inner_kernel(z, x_ref, w_ref, out, beside):
    for r in range(z.r):
        for dj, rows in enumerate(aside(z, x_ref[:, r].reshape(z.fl * z.w, z.c))):
            beside[dj, r] = rows
    for r in range(z.r):
        low, high = max(0, 1 - r), min(3, z.r + 1 - r)
        pieces = [beside[dj, r + di - 1] for di in range(low, high) for dj in range(3)]
        out[r] = taps(pieces, w_ref[low:high])


def own_act_kernel(z, part_ref, near_ref, far_ref, w_ref, cot_ref, out, near, far):
    lower = even("space")
    first = even("tm")
    for r in range(z.r):
        total = part_ref[r]
        for edge, di in ((0, 0), (z.r - 1, 2)):
            if r == edge:
                rows = jnp.where(lower == (di == 2), near_ref[...], far_ref[...])
                total += taps(aside(z, rows), w_ref[di])
        act = silu(total).reshape(z.fl, z.w, z.c)
        out[:, r] = act
        last = act[z.fl - 1]
        near[r] = jnp.where(first, last, cot_ref[0, r])
        far[r] = jnp.where(first, cot_ref[0, r], last)


def silu(total):
    return (total / (1.0 + jnp.exp(-total))).astype(BF)


def flat(value):
    return value.reshape(-1, value.shape[-1])


def outer(left, right):
    return lax.dot_general(
        flat(left), flat(right), (((0,), (0,)), ((), ())), preferred_element_type=F32
    )


def own_grad_kernel(z, act_ref, cot_ref, out):
    for k in range(3):
        out[:, k * z.c : (k + 1) * z.c] = outer(cot_ref[k:], act_ref[: z.fl - k])


def cross_kernel(z, width, part_ref, near_ref, far_ref, act_ref, cot_ref, keep, send):
    mine = even("space")
    before = jnp.where(even("tm"), far_ref[...], near_ref[...])
    after = jnp.where(even("tm"), near_ref[...], far_ref[...])
    for k in range(3):
        lanes = slice(k * z.c, (k + 1) * z.c)
        grad = part_ref[:, lanes]
        if k == 1:
            grad += outer(cot_ref[0], before)
        if k == 2:
            grad += outer(cot_ref[1], before)
            grad += outer(after, act_ref[z.fl - 2])
        for i in range(z.c // (2 * width)):
            low = grad[2 * i * width : (2 * i + 1) * width]
            high = grad[(2 * i + 1) * width : (2 * i + 2) * width]
            keep[i * width : (i + 1) * width, lanes] = jnp.where(mine, low, high)
            send[i * width : (i + 1) * width, lanes] = jnp.where(mine, high, low).astype(BF)


def gather_matrix(z, me):
    def source(q):
        s = q % z.f // z.fl
        return ((me ^ s) * z.fl + q % z.fl) * z.wc + q // z.f

    return chooser(z.block, z.block, source)


def assemble_kernel(z, *refs):
    parts, (out, near, far) = refs[: z.n], refs[z.n :]
    me = lax.axis_index("tm")
    lower = even("space")
    matrix = gather_matrix(z, me)

    def edge(q):
        head = q // z.f
        s = q % z.f // z.fl
        return ((me ^ s) * 2 * z.r + head) * z.fl + q % z.fl

    count = z.n * z.sides
    tails = jnp.concatenate([p[z.main : z.main + z.sides] for p in parts], axis=0)
    tails = moved(chooser(count, count, edge), tails)
    last = z.f + z.block
    for r in range(z.r):
        rows = jnp.concatenate([p[r * z.piece : (r + 1) * z.piece] for p in parts], axis=0)
        rows = moved(matrix, rows)
        left = tails[r * z.f : (r + 1) * z.f]
        right = tails[(z.r + r) * z.f : (z.r + r + 1) * z.f]
        out[r, 0 : z.f] = left
        out[r, z.f : last] = rows
        out[r, last : last + z.f] = right
    near[...] = jnp.where(lower, out[z.r - 1], out[0])
    far[...] = jnp.where(lower, out[0], out[z.r - 1])


def taps(pieces, weights):
    rows = jnp.concatenate(pieces, axis=1)
    return jnp.dot(rows, flat(weights), preferred_element_type=F32)


def conv_row(z, w_ref, three):
    return silu(taps([rows[dj * z.f : dj * z.f + z.block] for rows in three for dj in range(3)], w_ref[...]))


def middle_kernel(z, x_ref, w_ref, out):
    for r in range(1, z.r - 1):
        out[r - 1] = conv_row(z, w_ref, [x_ref.at[r + di] for di in (-1, 0, 1)])


def border_kernel(z, x_ref, near_ref, far_ref, w_ref, out, edges):
    lower = even("space")
    edges[0] = jnp.where(lower, far_ref[...], near_ref[...])
    edges[1] = jnp.where(lower, near_ref[...], far_ref[...])
    out[0] = conv_row(z, w_ref, [edges.at[0], x_ref.at[0], x_ref.at[1]])
    out[1] = conv_row(z, w_ref, [x_ref.at[z.r - 2], x_ref.at[z.r - 1], edges.at[1]])


def staged(count, stages):
    for step in range(count + len(stages) - 1):
        for late, stage in reversed(list(enumerate(stages))):
            if 0 <= step - late < count:
                stage(step - late)


def main_kernel(
    z, places, act_ref, x_ref, t_ref, gain_ref, q_ref, k_ref, v_ref, o_ref, *outs
):
    me = lax.axis_index("tm")
    a = lax.broadcasted_iota(jnp.int32, (z.block, z.block), 0)
    b = lax.broadcasted_iota(jnp.int32, (z.block, z.block), 1)
    allowed = (a // z.f == b // z.f) & (b % z.f <= a % z.f)
    scale = float(z.c) ** -0.5

    def source(q):
        t = ((me ^ (q // z.piece)) * z.fl) + q % z.piece // z.wc
        return q % z.wc * z.f + t

    back = chooser(z.block, z.block, source)
    frame = lax.broadcasted_iota(jnp.int32, (z.block, z.c), 0) % z.f
    held = {}

    def activate(r):
        act = act_ref[r]
        wide = act.astype(F32)
        held["a", r] = [act] + [
            jnp.where(frame >= k, pltpu.roll(wide, k, 0), 0.0).astype(BF) for k in (1, 2)
        ]

    def hide(r):
        temporal = taps(held.pop(("a", r)), t_ref[...])
        hidden = (x_ref[places[r], z.f : z.f + z.block].astype(F32) + temporal).astype(BF)
        held["h", r] = hidden

    def norm(r):
        wide = held["h", r].astype(F32)
        mean = jnp.mean(wide * wide, axis=1, keepdims=True)
        held["n", r] = (wide * (1.0 / jnp.sqrt(mean + 1e-06)) * gain_ref[...]).astype(BF)

    def project(r):
        rows = held.pop(("n", r))
        held["q", r], held["k", r], held["v", r] = (
            jnp.dot(rows, w[...], preferred_element_type=F32).astype(BF)
            for w in (q_ref, k_ref, v_ref)
        )

    def score(r):
        held["s", r] = lax.dot_general(
            held.pop(("q", r)),
            held.pop(("k", r)),
            (((1,), (1,)), ((), ())),
            preferred_element_type=F32,
        )

    def weigh(r):
        scores = jnp.where(allowed, held.pop(("s", r)) * scale, -1e30)
        top = jnp.max(scores, axis=1, keepdims=True)
        expon = jnp.where(allowed, jnp.exp(scores - top), 0.0)
        held["t", r] = 1.0 / jnp.sum(expon, axis=1, keepdims=True)
        held["p", r] = expon.astype(BF)

    def mix(r):
        mixed = jnp.dot(held.pop(("p", r)), held.pop(("v", r)), preferred_element_type=F32)
        held["a", r] = (mixed * held.pop(("t", r))).astype(BF)

    def finish(r):
        encoded = held.pop(("h", r)).astype(F32) + jnp.dot(
            held.pop(("a", r)), o_ref[...], preferred_element_type=F32
        )
        held["e", r] = encoded.astype(BF)

    def spread(r):
        encoded = moved(back, held.pop(("e", r)))
        for k in range(z.n):
            outs[k][r] = encoded[k * z.piece : (k + 1) * z.piece]

    staged(len(places), (activate, hide, norm, project, score, weigh, mix, finish, spread))


def split_kernel(z, keep_ref, got_ref, *outs):
    me = lax.axis_index("tm")
    wide = z.c // z.n
    for tap in range(3):
        place = slice(tap * wide, (tap + 1) * wide)
        if wide % 128 == 0:
            for k in range(z.n):
                lanes = pl.ds(pl.multiple_of(tap * z.c + (me ^ k) * wide, 128), wide)
                total = keep_ref[:, lanes] + got_ref[:, lanes].astype(F32)
                outs[k][:, place] = total.astype(outs[k].dtype)
            continue
        lanes = slice(tap * z.c, (tap + 1) * z.c)
        total = keep_ref[:, lanes] + got_ref[:, lanes].astype(F32)
        for k in range(z.n):
            cut = total[:, 0:wide]
            for i in range(1, z.n):
                cut = jnp.where((me ^ k) == i, total[:, i * wide : (i + 1) * wide], cut)
            outs[k][:, place] = cut.astype(outs[k].dtype)


def swap(value, axis, k):
    count = lax.axis_size(axis)
    return lax.ppermute(value, axis, [(i, i ^ k) for i in range(count)])


def swap_both(near, far, axis):
    pairs = [(i, i + 1) for i in range(1, lax.axis_size(axis) - 1, 2)]
    far = lax.ppermute(far, axis, pairs + [(b, a) for a, b in pairs])
    return swap(near, axis, 1), far


def halve_kernel(z, width, bit, *refs):
    parts, (keep, send) = refs[:-2], refs[-2:]
    total = sum(part[...].astype(F32) for part in parts)
    lower = lax.axis_index("space") // (2 << bit) % 2 == 0
    for i in range(keep.shape[0] // width):
        low = total[2 * i * width : (2 * i + 1) * width]
        high = total[(2 * i + 1) * width : (2 * i + 2) * width]
        rows = slice(i * width, (i + 1) * width)
        keep[rows] = jnp.where(lower, low, high)
        send[rows] = jnp.where(lower, high, low).astype(BF)


def sum_kernel(z, *refs):
    out, wide = refs[-1], z.c // z.n
    total = sum(part[...].astype(F32) for part in refs[:-1])
    for k in range(3):
        out[k] = total[:, k * wide : (k + 1) * wide]


def join_kernel(z, *refs):
    inside, border, (out, whole, sem) = refs[: z.n], refs[z.n : 2 * z.n], refs[2 * z.n :]
    me = lax.axis_index("tm")
    copies = []
    for f in range(z.fl):
        for k in range(z.n):
            cols = pl.ds(pl.multiple_of((me ^ k) * z.wc, z.wc), z.wc)
            rows = slice(f * z.wc, (f + 1) * z.wc)
            whole[f, 0, cols] = border[k][0, rows]
            whole[f, 1 : z.r - 1, cols] = inside[k][:, rows]
            whole[f, z.r - 1, cols] = border[k][1, rows]
        copies.append(pltpu.make_async_copy(whole.at[f], out.at[f], sem.at[f]))
        copies[f].start()
    for copy in copies:
        copy.wait()


def joined(z, inside, border):
    if z.wc % 16 == 0:
        return pl.pallas_call(
            functools.partial(join_kernel, z),
            out_shape=shape((z.fl, z.r, z.w, z.c)),
            in_specs=[VMEM] * (2 * z.n),
            out_specs=pl.BlockSpec(memory_space=pl.ANY),
            scratch_shapes=[
                pltpu.VMEM((z.fl, z.r, z.w, z.c), BF),
                pltpu.SemaphoreType.DMA((z.fl,)),
            ],
            compiler_params=pltpu.CompilerParams(vmem_limit_bytes=16 * 2**20),
            cost_estimate=pl.CostEstimate(
                flops=2**34, bytes_accessed=8 * z.n * z.main * z.c, transcendentals=0
            ),
        )(*inside, *border)
    whole = jnp.zeros((z.fl, z.r, z.n, z.wc, z.c), BF)
    for k in range(z.n):
        back = jnp.concatenate([border[k][:1], inside[k], border[k][1:]], axis=0)
        rows = back.reshape(z.r, z.fl, 1, z.wc, z.c).transpose(1, 0, 2, 3, 4)
        whole = lax.dynamic_update_slice_in_dim(whole, rows, lax.axis_index("tm") ^ k, 2)
    return whole.reshape(z.fl, z.r, z.w, z.c)


def on_device(frames_in, spatial, temporal, gain, q_w, k_w, v_w, o_w, cotangent):
    n = lax.axis_size("tm")
    space = lax.axis_size("space")
    z = Sizes(n, *frames_in.shape)
    one = 2 * z.r * z.block * z.c * z.c
    others = sorted(range(1, n), key=lambda k: -k.bit_count())
    width, wide = z.c // space, z.c // n

    def exchange(pieces):
        pieces = list(pieces)
        for k in others:
            pieces[k] = swap(pieces[k], "tm", k)
        return pieces

    edge = shape((z.fl * z.w, z.c))
    packed = call(
        functools.partial(pack_kernel, z),
        [shape((z.main + z.sides, z.c))] * n,
        frames_in,
        flops=one // 2,
    )
    near, far = call(
        functools.partial(edge_kernel, z), [edge, edge], frames_in, packed[0], flops=8 * one
    )
    got = exchange(packed)
    near, far = swap_both(near, far, "space")
    (own,) = call(
        functools.partial(own_inner_kernel, z),
        [shape((z.r, z.fl * z.w, z.c), F32)],
        frames_in,
        spatial,
        flops=8 * one,
        scratch=[pltpu.VMEM((3, z.r, z.fl * z.w, z.c), BF)],
    )
    own_act, near, far = call(
        functools.partial(own_act_kernel, z),
        [shape(frames_in.shape), shape((z.r, z.w, z.c)), shape((z.r, z.w, z.c))],
        own,
        near,
        far,
        spatial,
        cotangent,
        flops=3 * one,
    )
    near, far = swap_both(near, far, "tm")
    (own_grad,) = call(
        functools.partial(own_grad_kernel, z),
        [shape((z.c, 3 * z.c), F32)],
        own_act,
        cotangent,
        flops=9 * one // 4,
    )
    line = z.block + 2 * z.f
    x, close, apart = call(
        functools.partial(assemble_kernel, z),
        [shape((z.r, line, z.c)), shape((line, z.c)), shape((line, z.c))],
        *got,
    )
    close, apart = swap_both(close, apart, "space")
    (middle,) = call(
        functools.partial(middle_kernel, z),
        [shape((z.r - 2, z.block, z.c))],
        x,
        spatial,
        flops=9 * one * (z.r - 2) // z.r,
    )

    def attend(act, x, places):
        return call(
            functools.partial(main_kernel, z, places),
            [shape((len(places), z.piece, z.c))] * n,
            act,
            x,
            temporal.reshape(3 * z.c, z.c),
            gain.reshape(1, z.c),
            q_w,
            k_w,
            v_w,
            o_w,
            flops=9 * one * len(places) // z.r,
        )

    encoded = attend(middle, x, list(range(1, z.r - 1)))
    inside = exchange(encoded)
    tied = lax.optimization_barrier((near, far, encoded[0], close, apart))
    near, far, _, close, apart = tied
    keep, send = call(
        functools.partial(cross_kernel, z, width),
        [shape((z.c // 2, 3 * z.c), F32), shape((z.c // 2, 3 * z.c))],
        own_grad,
        near,
        far,
        own_act,
        cotangent,
        flops=3 * one // 4,
    )
    other = swap(send, "space", 1)
    x, _ = lax.optimization_barrier((x, send))
    (border,) = call(
        functools.partial(border_kernel, z),
        [shape((2, z.block, z.c))],
        x,
        close,
        apart,
        spatial,
        flops=18 * one // z.r,
        scratch=[pltpu.VMEM((2, line, z.c), BF)],
    )
    other, border = lax.optimization_barrier((other, border))
    pieces = call(
        functools.partial(split_kernel, z),
        [shape((z.c // 2, 3 * wide), F32)] + [shape((z.c // 2, 3 * wide))] * (n - 1),
        keep,
        other,
    )
    tied = lax.optimization_barrier((border, *pieces, *inside))
    border, inside = tied[0], tied[1 + n :]
    pieces = exchange(pieces)
    encoded = attend(border, x, [0, z.r - 1])
    back = exchange(encoded)
    pieces = lax.optimization_barrier((*pieces, *encoded))[:n]
    bit = 0
    while 2 << bit < space:
        half = (pieces[0].shape[0] // 2, 3 * wide)
        keep, send = call(
            functools.partial(halve_kernel, z, width, bit), [shape(half, F32), shape(half)], *pieces
        )
        pieces = (keep, swap(send, "space", 2 << bit))
        bit += 1
    (kernel_grad,) = call(
        functools.partial(sum_kernel, z), [shape((3, width, wide), F32)], *pieces
    )
    return joined(z, inside, back), kernel_grad.transpose(0, 2, 1)


def solution(mesh):
    tiles = P("tm", "space", None, None)
    return jax.shard_map(
        on_device,
        mesh=mesh,
        in_specs=(tiles,) + (P(),) * 7 + (tiles,),
        out_specs=(tiles, P(None, "tm", "space")),
        check_vma=False,
    )
```

```python
import functools

import jax
import jax.numpy as jnp
from jax import lax
from jax.experimental import pallas as pl
from jax.experimental.pallas import tpu as pltpu
from jax.sharding import PartitionSpec as P

BF = jnp.bfloat16
F32 = jnp.float32
VMEM = pl.BlockSpec(memory_space=pltpu.VMEM)


def call(kernel, outs, *args, flops=0, scratch=(), limit=16):
    moved = sum(a.size * a.dtype.itemsize for a in args)
    moved += sum(o.size * o.dtype.itemsize for o in outs)
    return pl.pallas_call(
        kernel,
        out_shape=tuple(outs),
        in_specs=[VMEM] * len(args),
        out_specs=tuple(VMEM for _ in outs),
        scratch_shapes=scratch,
        compiler_params=pltpu.CompilerParams(vmem_limit_bytes=limit * 2**20),
        cost_estimate=pl.CostEstimate(flops=flops, bytes_accessed=moved, transcendentals=0),
    )(*args)


def shape(dims, kind=BF):
    return jax.ShapeDtypeStruct(dims, kind)


def chooser(rows, cols, source):
    q = lax.broadcasted_iota(jnp.int32, (rows, cols), 0)
    m = lax.broadcasted_iota(jnp.int32, (rows, cols), 1)
    return jnp.where(source(q) == m, 1.0, 0.0).astype(BF)


def moved(matrix, rows):
    return jnp.dot(matrix, rows, preferred_element_type=F32).astype(BF)


class Sizes:
    def __init__(self, count, frames, rows, cols, chans):
        self.n, self.fl, self.r, self.w, self.c = count, frames, rows, cols, chans
        self.f = count * frames
        self.wc = cols // count
        self.block = self.f * self.wc
        self.piece = frames * self.wc
        self.main = rows * self.piece
        self.sides = 2 * rows * frames


def even(axis):
    return lax.axis_index(axis) % 2 == 0


def edge_kernel(z, x_ref, after_ref, near, far):
    top, bottom = (flat(x_ref[:, r]) for r in (0, z.r - 1))
    near[...] = jnp.where(even("space"), bottom, top)
    far[...] = jnp.where(even("space"), top, bottom)


def pack_kernel(z, x_ref, *outs):
    me = lax.axis_index("tm")

    def source(q):
        k = q // z.piece
        f = q % z.piece // z.wc
        return f * z.w + (me ^ k) * z.wc + q % z.wc

    def edge(r, q):
        k = q // z.sides
        side = q % z.sides // (z.r * z.fl)
        row = q % (z.r * z.fl) // z.fl
        col = (me ^ k) * z.wc - 1 + side * (z.wc + 1)
        inside = (col >= 0) & (col < z.w) & (row == r)
        return jnp.where(inside, q % z.fl * z.w + col, -1)

    matrix = chooser(z.n * z.piece, z.fl * z.w, source)
    tails = jnp.zeros((z.n * z.sides, z.c), F32)
    for r in range(z.r):
        rows = x_ref[:, r].reshape(z.fl * z.w, z.c)
        cut = moved(matrix, rows)
        for k in range(z.n):
            outs[k][r * z.piece : (r + 1) * z.piece] = cut[k * z.piece : (k + 1) * z.piece]
        picked = chooser(z.n * z.sides, z.fl * z.w, functools.partial(edge, r))
        tails += jnp.dot(picked, rows, preferred_element_type=F32)
    tails = tails.astype(BF)
    for k in range(z.n):
        outs[k][z.main : z.main + z.sides] = tails[k * z.sides : (k + 1) * z.sides]


def aside(z, rows):
    count = z.fl * z.w
    left = chooser(count, count, lambda q: jnp.where(q % z.w > 0, q - 1, -1))
    right = chooser(count, count, lambda q: jnp.where(q % z.w < z.w - 1, q + 1, -1))
    return moved(left, rows), rows, moved(right, rows)


def own_inner_kernel(z, x_ref, w_ref, out, beside):
    for r in range(z.r):
        for dj, rows in enumerate(aside(z, x_ref[:, r].reshape(z.fl * z.w, z.c))):
            beside[dj, r] = rows
    for r in range(z.r):
        low, high = max(0, 1 - r), min(3, z.r + 1 - r)
        pieces = [beside[dj, r + di - 1] for di in range(low, high) for dj in range(3)]
        out[r] = taps(pieces, w_ref[low:high])


def own_act_kernel(z, part_ref, near_ref, far_ref, w_ref, cot_ref, out, near, far):
    lower = even("space")
    first = even("tm")
    for r in range(z.r):
        total = part_ref[r]
        for edge, di in ((0, 0), (z.r - 1, 2)):
            if r == edge:
                rows = jnp.where(lower == (di == 2), near_ref[...], far_ref[...])
                total += taps(aside(z, rows), w_ref[di])
        act = silu(total).reshape(z.fl, z.w, z.c)
        out[:, r] = act
        last = act[z.fl - 1]
        near[r] = jnp.where(first, last, cot_ref[0, r])
        far[r] = jnp.where(first, cot_ref[0, r], last)


def silu(total):
    return (total / (1.0 + jnp.exp(-total))).astype(BF)


def flat(value):
    return value.reshape(-1, value.shape[-1])


def outer(left, right):
    return lax.dot_general(
        flat(left), flat(right), (((0,), (0,)), ((), ())), preferred_element_type=F32
    )


def own_grad_kernel(z, act_ref, cot_ref, out):
    for k in range(3):
        out[:, k * z.c : (k + 1) * z.c] = outer(cot_ref[k:], act_ref[: z.fl - k])


def cross_kernel(z, width, part_ref, near_ref, far_ref, act_ref, cot_ref, keep, send):
    mine = even("space")
    before = jnp.where(even("tm"), far_ref[...], near_ref[...])
    after = jnp.where(even("tm"), near_ref[...], far_ref[...])
    for k in range(3):
        lanes = slice(k * z.c, (k + 1) * z.c)
        grad = part_ref[:, lanes]
        if k == 1:
            grad += outer(cot_ref[0], before)
        if k == 2:
            grad += outer(cot_ref[1], before)
            grad += outer(after, act_ref[z.fl - 2])
        for i in range(z.c // (2 * width)):
            low = grad[2 * i * width : (2 * i + 1) * width]
            high = grad[(2 * i + 1) * width : (2 * i + 2) * width]
            keep[i * width : (i + 1) * width, lanes] = jnp.where(mine, low, high)
            send[i * width : (i + 1) * width, lanes] = jnp.where(mine, high, low).astype(BF)


def gather_matrix(z, me):
    def source(q):
        s = q % z.f // z.fl
        return ((me ^ s) * z.fl + q % z.fl) * z.wc + q // z.f

    return chooser(z.block, z.block, source)


def assemble_kernel(z, *refs):
    parts, (out, near, far) = refs[: z.n], refs[z.n :]
    me = lax.axis_index("tm")
    lower = even("space")
    matrix = gather_matrix(z, me)

    def edge(q):
        head = q // z.f
        s = q % z.f // z.fl
        return ((me ^ s) * 2 * z.r + head) * z.fl + q % z.fl

    count = z.n * z.sides
    tails = jnp.concatenate([p[z.main : z.main + z.sides] for p in parts], axis=0)
    tails = moved(chooser(count, count, edge), tails)
    last = z.f + z.block
    for r in range(z.r):
        rows = jnp.concatenate([p[r * z.piece : (r + 1) * z.piece] for p in parts], axis=0)
        rows = moved(matrix, rows)
        left = tails[r * z.f : (r + 1) * z.f]
        right = tails[(z.r + r) * z.f : (z.r + r + 1) * z.f]
        out[r, 0 : z.f] = left
        out[r, z.f : last] = rows
        out[r, last : last + z.f] = right
    near[...] = jnp.where(lower, out[z.r - 1], out[0])
    far[...] = jnp.where(lower, out[0], out[z.r - 1])


def taps(pieces, weights):
    rows = jnp.concatenate(pieces, axis=1)
    return jnp.dot(rows, flat(weights), preferred_element_type=F32)


def conv_row(z, w_ref, three):
    return silu(taps([rows[dj * z.f : dj * z.f + z.block] for rows in three for dj in range(3)], w_ref[...]))


def middle_kernel(z, x_ref, w_ref, out):
    for r in range(1, z.r - 1):
        out[r - 1] = conv_row(z, w_ref, [x_ref.at[r + di] for di in (-1, 0, 1)])


def border_kernel(z, x_ref, near_ref, far_ref, w_ref, out, edges):
    lower = even("space")
    edges[0] = jnp.where(lower, far_ref[...], near_ref[...])
    edges[1] = jnp.where(lower, near_ref[...], far_ref[...])
    out[0] = conv_row(z, w_ref, [edges.at[0], x_ref.at[0], x_ref.at[1]])
    out[1] = conv_row(z, w_ref, [x_ref.at[z.r - 2], x_ref.at[z.r - 1], edges.at[1]])


def staged(z, stages):
    for step in range(z.r + len(stages) - 1):
        for late, stage in reversed(list(enumerate(stages))):
            if 0 <= step - late < z.r:
                stage(step - late)


def main_kernel(
    z, middle_ref, border_ref, x_ref, t_ref, gain_ref, q_ref, k_ref, v_ref, o_ref, *outs
):
    me = lax.axis_index("tm")
    a = lax.broadcasted_iota(jnp.int32, (z.block, z.block), 0)
    b = lax.broadcasted_iota(jnp.int32, (z.block, z.block), 1)
    allowed = (a // z.f == b // z.f) & (b % z.f <= a % z.f)
    scale = float(z.c) ** -0.5

    def source(q):
        t = ((me ^ (q // z.piece)) * z.fl) + q % z.piece // z.wc
        return q % z.wc * z.f + t

    back = chooser(z.block, z.block, source)
    frame = lax.broadcasted_iota(jnp.int32, (z.block, z.c), 0) % z.f
    held = {}

    def activate(r):
        act = border_ref[r // (z.r - 1)] if r in (0, z.r - 1) else middle_ref[r - 1]
        wide = act.astype(F32)
        held["a", r] = [act] + [
            jnp.where(frame >= k, pltpu.roll(wide, k, 0), 0.0).astype(BF) for k in (1, 2)
        ]

    def hide(r):
        temporal = taps(held.pop(("a", r)), t_ref[...])
        hidden = (x_ref[r, z.f : z.f + z.block].astype(F32) + temporal).astype(BF)
        held["h", r] = hidden

    def norm(r):
        wide = held["h", r].astype(F32)
        mean = jnp.mean(wide * wide, axis=1, keepdims=True)
        held["n", r] = (wide * (1.0 / jnp.sqrt(mean + 1e-06)) * gain_ref[...]).astype(BF)

    def project(r):
        rows = held.pop(("n", r))
        held["q", r], held["k", r], held["v", r] = (
            jnp.dot(rows, w[...], preferred_element_type=F32).astype(BF)
            for w in (q_ref, k_ref, v_ref)
        )

    def score(r):
        held["s", r] = lax.dot_general(
            held.pop(("q", r)),
            held.pop(("k", r)),
            (((1,), (1,)), ((), ())),
            preferred_element_type=F32,
        )

    def weigh(r):
        scores = jnp.where(allowed, held.pop(("s", r)) * scale, -1e30)
        top = jnp.max(scores, axis=1, keepdims=True)
        expon = jnp.where(allowed, jnp.exp(scores - top), 0.0)
        held["t", r] = 1.0 / jnp.sum(expon, axis=1, keepdims=True)
        held["p", r] = expon.astype(BF)

    def mix(r):
        mixed = jnp.dot(held.pop(("p", r)), held.pop(("v", r)), preferred_element_type=F32)
        held["a", r] = (mixed * held.pop(("t", r))).astype(BF)

    def finish(r):
        encoded = held.pop(("h", r)).astype(F32) + jnp.dot(
            held.pop(("a", r)), o_ref[...], preferred_element_type=F32
        )
        held["e", r] = encoded.astype(BF)

    def spread(r):
        encoded = moved(back, held.pop(("e", r)))
        for k in range(z.n):
            outs[k][r] = encoded[k * z.piece : (k + 1) * z.piece]

    staged(z, (activate, hide, norm, project, score, weigh, mix, finish, spread))


def split_kernel(z, keep_ref, got_ref, *outs):
    me = lax.axis_index("tm")
    wide = z.c // z.n
    for tap in range(3):
        place = slice(tap * wide, (tap + 1) * wide)
        if wide % 128 == 0:
            for k in range(z.n):
                lanes = pl.ds(pl.multiple_of(tap * z.c + (me ^ k) * wide, 128), wide)
                total = keep_ref[:, lanes] + got_ref[:, lanes].astype(F32)
                outs[k][:, place] = total.astype(outs[k].dtype)
            continue
        lanes = slice(tap * z.c, (tap + 1) * z.c)
        total = keep_ref[:, lanes] + got_ref[:, lanes].astype(F32)
        for k in range(z.n):
            cut = total[:, 0:wide]
            for i in range(1, z.n):
                cut = jnp.where((me ^ k) == i, total[:, i * wide : (i + 1) * wide], cut)
            outs[k][:, place] = cut.astype(outs[k].dtype)


def swap(value, axis, k):
    count = lax.axis_size(axis)
    return lax.ppermute(value, axis, [(i, i ^ k) for i in range(count)])


def swap_both(near, far, axis):
    pairs = [(i, i + 1) for i in range(1, lax.axis_size(axis) - 1, 2)]
    far = lax.ppermute(far, axis, pairs + [(b, a) for a, b in pairs])
    return swap(near, axis, 1), far


def halve_kernel(z, width, bit, *refs):
    parts, (keep, send) = refs[:-2], refs[-2:]
    total = sum(part[...].astype(F32) for part in parts)
    lower = lax.axis_index("space") // (2 << bit) % 2 == 0
    for i in range(keep.shape[0] // width):
        low = total[2 * i * width : (2 * i + 1) * width]
        high = total[(2 * i + 1) * width : (2 * i + 2) * width]
        rows = slice(i * width, (i + 1) * width)
        keep[rows] = jnp.where(lower, low, high)
        send[rows] = jnp.where(lower, high, low).astype(BF)


def add_up(z, kept_ref, got_ref, out):
    wide = z.c // z.n
    total = kept_ref[...] + got_ref[...].astype(F32)
    for k in range(3):
        out[k] = total[:, k * wide : (k + 1) * wide]


def join_kernel(z, kept_ref, got_ref, *refs):
    parts, (out, grad, whole, sem) = refs[: z.n], refs[z.n :]
    me = lax.axis_index("tm")
    copies = []
    for f in range(z.fl):
        for k in range(z.n):
            cols = pl.ds(pl.multiple_of((me ^ k) * z.wc, z.wc), z.wc)
            whole[f, :, cols] = parts[k][:, f * z.wc : (f + 1) * z.wc]
        copies.append(pltpu.make_async_copy(whole.at[f], out.at[f], sem.at[f]))
        copies[f].start()
    add_up(z, kept_ref, got_ref, grad)
    for copy in copies:
        copy.wait()


def joined(z, back, kept, got):
    grad = shape((3, kept.shape[0], z.c // z.n), F32)
    if z.wc % 16 == 0:
        return pl.pallas_call(
            functools.partial(join_kernel, z),
            out_shape=(shape((z.fl, z.r, z.w, z.c)), grad),
            in_specs=[VMEM] * (2 + z.n),
            out_specs=(pl.BlockSpec(memory_space=pl.ANY), VMEM),
            scratch_shapes=[
                pltpu.VMEM((z.fl, z.r, z.w, z.c), BF),
                pltpu.SemaphoreType.DMA((z.fl,)),
            ],
            compiler_params=pltpu.CompilerParams(vmem_limit_bytes=16 * 2**20),
            cost_estimate=pl.CostEstimate(
                flops=0, bytes_accessed=8 * z.n * z.main * z.c, transcendentals=0
            ),
        )(kept, got, *back)
    whole = jnp.zeros((z.fl, z.r, z.n, z.wc, z.c), BF)
    for k in range(z.n):
        rows = back[k].reshape(z.r, z.fl, 1, z.wc, z.c).transpose(1, 0, 2, 3, 4)
        whole = lax.dynamic_update_slice_in_dim(whole, rows, lax.axis_index("tm") ^ k, 2)
    (grad,) = call(functools.partial(add_up, z), [grad], kept, got)
    return whole.reshape(z.fl, z.r, z.w, z.c), grad


def on_device(frames_in, spatial, temporal, gain, q_w, k_w, v_w, o_w, cotangent):
    n = lax.axis_size("tm")
    space = lax.axis_size("space")
    z = Sizes(n, *frames_in.shape)
    one = 2 * z.r * z.block * z.c * z.c
    others = sorted(range(1, n), key=lambda k: -k.bit_count())
    width, wide = z.c // space, z.c // n

    def exchange(pieces):
        pieces = list(pieces)
        for k in others:
            pieces[k] = swap(pieces[k], "tm", k)
        return pieces

    edge = shape((z.fl * z.w, z.c))
    packed = call(
        functools.partial(pack_kernel, z),
        [shape((z.main + z.sides, z.c))] * n,
        frames_in,
        flops=one // 2,
    )
    near, far = call(
        functools.partial(edge_kernel, z), [edge, edge], frames_in, packed[0], flops=8 * one
    )
    got = exchange(packed)
    near, far = swap_both(near, far, "space")
    (own,) = call(
        functools.partial(own_inner_kernel, z),
        [shape((z.r, z.fl * z.w, z.c), F32)],
        frames_in,
        spatial,
        flops=8 * one,
        scratch=[pltpu.VMEM((3, z.r, z.fl * z.w, z.c), BF)],
    )
    own_act, near, far = call(
        functools.partial(own_act_kernel, z),
        [shape(frames_in.shape), shape((z.r, z.w, z.c)), shape((z.r, z.w, z.c))],
        own,
        near,
        far,
        spatial,
        cotangent,
        flops=3 * one,
    )
    near, far = swap_both(near, far, "tm")
    (own_grad,) = call(
        functools.partial(own_grad_kernel, z),
        [shape((z.c, 3 * z.c), F32)],
        own_act,
        cotangent,
        flops=9 * one // 4,
    )
    line = z.block + 2 * z.f
    x, close, apart = call(
        functools.partial(assemble_kernel, z),
        [shape((z.r, line, z.c)), shape((line, z.c)), shape((line, z.c))],
        *got,
    )
    close, apart = swap_both(close, apart, "space")
    (middle,) = call(
        functools.partial(middle_kernel, z),
        [shape((z.r - 2, z.block, z.c))],
        x,
        spatial,
        flops=9 * one * (z.r - 2) // z.r,
    )
    tied = lax.optimization_barrier((near, far, middle, close, apart))
    near, far, middle, close, apart = tied
    keep, send = call(
        functools.partial(cross_kernel, z, width),
        [shape((z.c // 2, 3 * z.c), F32), shape((z.c // 2, 3 * z.c))],
        own_grad,
        near,
        far,
        own_act,
        cotangent,
        flops=3 * one // 4,
    )
    other = swap(send, "space", 1)
    x, _ = lax.optimization_barrier((x, send))
    (border,) = call(
        functools.partial(border_kernel, z),
        [shape((2, z.block, z.c))],
        x,
        close,
        apart,
        spatial,
        flops=18 * one // z.r,
        scratch=[pltpu.VMEM((2, line, z.c), BF)],
    )
    other, border = lax.optimization_barrier((other, border))
    pieces = call(
        functools.partial(split_kernel, z),
        [shape((z.c // 2, 3 * wide), F32)] + [shape((z.c // 2, 3 * wide))] * (n - 1),
        keep,
        other,
    )
    border, *pieces = lax.optimization_barrier((border, *pieces))
    pieces = exchange(pieces)
    encoded = call(
        functools.partial(main_kernel, z),
        [shape((z.r, z.piece, z.c))] * n,
        middle,
        border,
        x,
        temporal,
        gain.reshape(1, z.c),
        q_w,
        k_w,
        v_w,
        o_w,
        flops=9 * one,
    )
    back = exchange(encoded)
    pieces = lax.optimization_barrier((*pieces, *encoded))[:n]
    bit = 0
    while 2 << bit < space:
        half = (pieces[0].shape[0] // 2, 3 * wide)
        keep, send = call(
            functools.partial(halve_kernel, z, width, bit), [shape(half, F32), shape(half)], *pieces
        )
        pieces = (keep, swap(send, "space", 2 << bit))
        bit += 1
    encoded, kernel_grad = joined(z, back, *pieces)
    return encoded, kernel_grad.transpose(0, 2, 1)


def solution(mesh):
    tiles = P("tm", "space", None, None)
    return jax.shard_map(
        on_device,
        mesh=mesh,
        in_specs=(tiles,) + (P(),) * 7 + (tiles,),
        out_specs=(tiles, P(None, "tm", "space")),
        check_vma=False,
    )
```

```python
import functools

import jax
import jax.numpy as jnp
from jax import lax
from jax.experimental import pallas as pl
from jax.experimental.pallas import tpu as pltpu
from jax.sharding import PartitionSpec as P

BF = jnp.bfloat16
F32 = jnp.float32
VMEM = pl.BlockSpec(memory_space=pltpu.VMEM)


def call(kernel, outs, *args, flops=0, scratch=(), limit=16):
    moved = sum(a.size * a.dtype.itemsize for a in args)
    moved += sum(o.size * o.dtype.itemsize for o in outs)
    return pl.pallas_call(
        kernel,
        out_shape=tuple(outs),
        in_specs=[VMEM] * len(args),
        out_specs=tuple(VMEM for _ in outs),
        scratch_shapes=scratch,
        compiler_params=pltpu.CompilerParams(vmem_limit_bytes=limit * 2**20),
        cost_estimate=pl.CostEstimate(flops=flops, bytes_accessed=moved, transcendentals=0),
    )(*args)


def shape(dims, kind=BF):
    return jax.ShapeDtypeStruct(dims, kind)


def chooser(rows, cols, source):
    q = lax.broadcasted_iota(jnp.int32, (rows, cols), 0)
    m = lax.broadcasted_iota(jnp.int32, (rows, cols), 1)
    return jnp.where(source(q) == m, 1.0, 0.0).astype(BF)


def moved(matrix, rows):
    return jnp.dot(matrix, rows, preferred_element_type=F32).astype(BF)


class Sizes:
    def __init__(self, count, frames, rows, cols, chans):
        self.n, self.fl, self.r, self.w, self.c = count, frames, rows, cols, chans
        self.f = count * frames
        self.wc = cols // count
        self.block = self.f * self.wc
        self.piece = frames * self.wc
        self.main = rows * self.piece
        self.sides = 2 * rows * frames
        self.order = sorted(range(count), key=lambda k: -k.bit_count())

    def ordered(self, pieces):
        return [pieces[k] for k in self.order]

    def by_partner(self, pieces):
        return [pieces[self.order.index(k)] for k in range(self.n)]


def even(axis):
    return lax.axis_index(axis) % 2 == 0


def edge_kernel(z, x_ref, after_ref, near, far):
    top, bottom = (flat(x_ref[:, r]) for r in (0, z.r - 1))
    near[...] = jnp.where(even("space"), bottom, top)
    far[...] = jnp.where(even("space"), top, bottom)


def pack_kernel(z, x_ref, *outs):
    me = lax.axis_index("tm")

    def source(q):
        k = q // z.piece
        f = q % z.piece // z.wc
        return f * z.w + (me ^ k) * z.wc + q % z.wc

    def edge(r, q):
        k = q // z.sides
        side = q % z.sides // (z.r * z.fl)
        row = q % (z.r * z.fl) // z.fl
        col = (me ^ k) * z.wc - 1 + side * (z.wc + 1)
        inside = (col >= 0) & (col < z.w) & (row == r)
        return jnp.where(inside, q % z.fl * z.w + col, -1)

    matrix = chooser(z.n * z.piece, z.fl * z.w, source)
    tails = jnp.zeros((z.n * z.sides, z.c), F32)
    for r in range(z.r):
        rows = x_ref[:, r].reshape(z.fl * z.w, z.c)
        cut = moved(matrix, rows)
        for k in range(z.n):
            outs[k][r * z.piece : (r + 1) * z.piece] = cut[k * z.piece : (k + 1) * z.piece]
        picked = chooser(z.n * z.sides, z.fl * z.w, functools.partial(edge, r))
        tails += jnp.dot(picked, rows, preferred_element_type=F32)
    tails = tails.astype(BF)
    for k in range(z.n):
        outs[k][z.main : z.main + z.sides] = tails[k * z.sides : (k + 1) * z.sides]


def aside(z, rows):
    count = z.fl * z.w
    left = chooser(count, count, lambda q: jnp.where(q % z.w > 0, q - 1, -1))
    right = chooser(count, count, lambda q: jnp.where(q % z.w < z.w - 1, q + 1, -1))
    return moved(left, rows), rows, moved(right, rows)


def own_inner_kernel(z, x_ref, w_ref, out, beside):
    for r in range(z.r):
        for dj, rows in enumerate(aside(z, x_ref[:, r].reshape(z.fl * z.w, z.c))):
            beside[dj, r] = rows
    for r in range(z.r):
        low, high = max(0, 1 - r), min(3, z.r + 1 - r)
        pieces = [beside[dj, r + di - 1] for di in range(low, high) for dj in range(3)]
        out[r] = taps(pieces, w_ref[low:high])


def own_act_kernel(z, part_ref, near_ref, far_ref, w_ref, cot_ref, out, near, far):
    lower = even("space")
    first = even("tm")
    for r in range(z.r):
        total = part_ref[r]
        for edge, di in ((0, 0), (z.r - 1, 2)):
            if r == edge:
                rows = jnp.where(lower == (di == 2), near_ref[...], far_ref[...])
                total += taps(aside(z, rows), w_ref[di])
        act = silu(total).reshape(z.fl, z.w, z.c)
        out[:, r] = act
        last = act[z.fl - 1]
        near[r] = jnp.where(first, last, cot_ref[0, r])
        far[r] = jnp.where(first, cot_ref[0, r], last)


def silu(total):
    return (total / (1.0 + jnp.exp(-total))).astype(BF)


def flat(value):
    return value.reshape(-1, value.shape[-1])


def outer(left, right):
    return lax.dot_general(
        flat(left), flat(right), (((0,), (0,)), ((), ())), preferred_element_type=F32
    )


def own_grad_kernel(z, act_ref, cot_ref, out):
    for k in range(3):
        out[:, k * z.c : (k + 1) * z.c] = outer(cot_ref[k:], act_ref[: z.fl - k])


def cross_kernel(z, width, part_ref, near_ref, far_ref, act_ref, cot_ref, keep, send):
    mine = even("space")
    before = jnp.where(even("tm"), far_ref[...], near_ref[...])
    after = jnp.where(even("tm"), near_ref[...], far_ref[...])
    for k in range(3):
        lanes = slice(k * z.c, (k + 1) * z.c)
        grad = part_ref[:, lanes]
        if k == 1:
            grad += outer(cot_ref[0], before)
        if k == 2:
            grad += outer(cot_ref[1], before)
            grad += outer(after, act_ref[z.fl - 2])
        for i in range(z.c // (2 * width)):
            low = grad[2 * i * width : (2 * i + 1) * width]
            high = grad[(2 * i + 1) * width : (2 * i + 2) * width]
            keep[i * width : (i + 1) * width, lanes] = jnp.where(mine, low, high)
            send[i * width : (i + 1) * width, lanes] = jnp.where(mine, high, low).astype(BF)


def gather_matrix(z, me):
    def source(q):
        s = q % z.f // z.fl
        return ((me ^ s) * z.fl + q % z.fl) * z.wc + q // z.f

    return chooser(z.block, z.block, source)


def assemble_kernel(z, *refs):
    parts, (out, near, far) = z.by_partner(refs[: z.n]), refs[z.n :]
    me = lax.axis_index("tm")
    lower = even("space")
    matrix = gather_matrix(z, me)

    def edge(q):
        head = q // z.f
        s = q % z.f // z.fl
        return ((me ^ s) * 2 * z.r + head) * z.fl + q % z.fl

    count = z.n * z.sides
    tails = jnp.concatenate([p[z.main : z.main + z.sides] for p in parts], axis=0)
    tails = moved(chooser(count, count, edge), tails)
    last = z.f + z.block
    for r in range(z.r):
        rows = jnp.concatenate([p[r * z.piece : (r + 1) * z.piece] for p in parts], axis=0)
        rows = moved(matrix, rows)
        left = tails[r * z.f : (r + 1) * z.f]
        right = tails[(z.r + r) * z.f : (z.r + r + 1) * z.f]
        out[r, 0 : z.f] = left
        out[r, z.f : last] = rows
        out[r, last : last + z.f] = right
    near[...] = jnp.where(lower, out[z.r - 1], out[0])
    far[...] = jnp.where(lower, out[0], out[z.r - 1])


def taps(pieces, weights):
    rows = jnp.concatenate(pieces, axis=1)
    return jnp.dot(rows, flat(weights), preferred_element_type=F32)


def conv_row(z, w_ref, three):
    return silu(taps([rows[dj * z.f : dj * z.f + z.block] for rows in three for dj in range(3)], w_ref[...]))


def middle_kernel(z, x_ref, w_ref, out):
    for r in range(1, z.r - 1):
        out[r - 1] = conv_row(z, w_ref, [x_ref.at[r + di] for di in (-1, 0, 1)])


def border_kernel(z, x_ref, near_ref, far_ref, w_ref, out, edges):
    lower = even("space")
    edges[0] = jnp.where(lower, far_ref[...], near_ref[...])
    edges[1] = jnp.where(lower, near_ref[...], far_ref[...])
    out[0] = conv_row(z, w_ref, [edges.at[0], x_ref.at[0], x_ref.at[1]])
    out[1] = conv_row(z, w_ref, [x_ref.at[z.r - 2], x_ref.at[z.r - 1], edges.at[1]])


def staged(z, stages):
    for step in range(z.r + len(stages) - 1):
        for late, stage in reversed(list(enumerate(stages))):
            if 0 <= step - late < z.r:
                stage(step - late)


def main_kernel(
    z, middle_ref, border_ref, x_ref, t_ref, gain_ref, q_ref, k_ref, v_ref, o_ref, *outs
):
    me = lax.axis_index("tm")
    a = lax.broadcasted_iota(jnp.int32, (z.block, z.block), 0)
    b = lax.broadcasted_iota(jnp.int32, (z.block, z.block), 1)
    allowed = (a // z.f == b // z.f) & (b % z.f <= a % z.f)
    scale = float(z.c) ** -0.5

    def source(q):
        t = ((me ^ (q // z.piece)) * z.fl) + q % z.piece // z.wc
        return q % z.wc * z.f + t

    back = chooser(z.block, z.block, source)
    frame = lax.broadcasted_iota(jnp.int32, (z.block, z.c), 0) % z.f
    held = {}

    def activate(r):
        act = border_ref[r // (z.r - 1)] if r in (0, z.r - 1) else middle_ref[r - 1]
        wide = act.astype(F32)
        held["a", r] = [act] + [
            jnp.where(frame >= k, pltpu.roll(wide, k, 0), 0.0).astype(BF) for k in (1, 2)
        ]

    def hide(r):
        temporal = taps(held.pop(("a", r)), t_ref[...])
        hidden = (x_ref[r, z.f : z.f + z.block].astype(F32) + temporal).astype(BF)
        held["h", r] = hidden

    def norm(r):
        wide = held["h", r].astype(F32)
        mean = jnp.mean(wide * wide, axis=1, keepdims=True)
        held["n", r] = (wide * (1.0 / jnp.sqrt(mean + 1e-06)) * gain_ref[...]).astype(BF)

    def project(r):
        rows = held.pop(("n", r))
        held["q", r], held["k", r], held["v", r] = (
            jnp.dot(rows, w[...], preferred_element_type=F32).astype(BF)
            for w in (q_ref, k_ref, v_ref)
        )

    def score(r):
        held["s", r] = lax.dot_general(
            held.pop(("q", r)),
            held.pop(("k", r)),
            (((1,), (1,)), ((), ())),
            preferred_element_type=F32,
        )

    def weigh(r):
        scores = jnp.where(allowed, held.pop(("s", r)) * scale, -1e30)
        top = jnp.max(scores, axis=1, keepdims=True)
        expon = jnp.where(allowed, jnp.exp(scores - top), 0.0)
        held["t", r] = 1.0 / jnp.sum(expon, axis=1, keepdims=True)
        held["p", r] = expon.astype(BF)

    def mix(r):
        mixed = jnp.dot(held.pop(("p", r)), held.pop(("v", r)), preferred_element_type=F32)
        held["a", r] = (mixed * held.pop(("t", r))).astype(BF)

    def finish(r):
        encoded = held.pop(("h", r)).astype(F32) + jnp.dot(
            held.pop(("a", r)), o_ref[...], preferred_element_type=F32
        )
        held["e", r] = encoded.astype(BF)

    def spread(r):
        encoded = moved(back, held.pop(("e", r)))
        for out, k in zip(outs, z.order):
            out[r] = encoded[k * z.piece : (k + 1) * z.piece]

    staged(z, (activate, hide, norm, project, score, weigh, mix, finish, spread))


def split_kernel(z, keep_ref, got_ref, *outs):
    me = lax.axis_index("tm")
    wide = z.c // z.n
    for tap in range(3):
        place = slice(tap * wide, (tap + 1) * wide)
        if wide % 128 == 0:
            for k in range(z.n):
                lanes = pl.ds(pl.multiple_of(tap * z.c + (me ^ k) * wide, 128), wide)
                total = keep_ref[:, lanes] + got_ref[:, lanes].astype(F32)
                outs[k][:, place] = total.astype(outs[k].dtype)
            continue
        lanes = slice(tap * z.c, (tap + 1) * z.c)
        total = keep_ref[:, lanes] + got_ref[:, lanes].astype(F32)
        for k in range(z.n):
            cut = total[:, 0:wide]
            for i in range(1, z.n):
                cut = jnp.where((me ^ k) == i, total[:, i * wide : (i + 1) * wide], cut)
            outs[k][:, place] = cut.astype(outs[k].dtype)


def swap(value, axis, k):
    count = lax.axis_size(axis)
    return lax.ppermute(value, axis, [(i, i ^ k) for i in range(count)])


def swap_both(near, far, axis):
    pairs = [(i, i + 1) for i in range(1, lax.axis_size(axis) - 1, 2)]
    far = lax.ppermute(far, axis, pairs + [(b, a) for a, b in pairs])
    return swap(near, axis, 1), far


def halve_kernel(z, width, bit, *refs):
    parts, (keep, send) = refs[:-2], refs[-2:]
    total = sum(part[...].astype(F32) for part in parts)
    lower = lax.axis_index("space") // (2 << bit) % 2 == 0
    for i in range(keep.shape[0] // width):
        low = total[2 * i * width : (2 * i + 1) * width]
        high = total[(2 * i + 1) * width : (2 * i + 2) * width]
        rows = slice(i * width, (i + 1) * width)
        keep[rows] = jnp.where(lower, low, high)
        send[rows] = jnp.where(lower, high, low).astype(BF)


def add_up(z, kept_ref, got_ref, out):
    wide = z.c // z.n
    total = kept_ref[...] + got_ref[...].astype(F32)
    for k in range(3):
        out[k] = total[:, k * wide : (k + 1) * wide]


def join_kernel(z, kept_ref, got_ref, *refs):
    parts, (out, grad, whole, total, sem) = z.by_partner(refs[: z.n]), refs[z.n :]
    me = lax.axis_index("tm")
    add_up(z, kept_ref, got_ref, total)
    copies = [pltpu.make_async_copy(total, grad, sem.at[z.fl])]
    copies[0].start()
    for f in range(z.fl):
        for k in range(z.n):
            cols = pl.ds(pl.multiple_of((me ^ k) * z.wc, z.wc), z.wc)
            whole[f, :, cols] = parts[k][:, f * z.wc : (f + 1) * z.wc]
        copies.append(pltpu.make_async_copy(whole.at[f], out.at[f], sem.at[f]))
        copies[-1].start()
    for copy in copies:
        copy.wait()


def joined(z, back, kept, got):
    grad = shape((3, kept.shape[0], z.c // z.n), F32)
    if z.wc % 16 == 0:
        return pl.pallas_call(
            functools.partial(join_kernel, z),
            out_shape=(shape((z.fl, z.r, z.w, z.c)), grad),
            in_specs=[VMEM] * (2 + z.n),
            out_specs=(pl.BlockSpec(memory_space=pl.ANY),) * 2,
            scratch_shapes=[
                pltpu.VMEM((z.fl, z.r, z.w, z.c), BF),
                pltpu.VMEM(grad.shape, F32),
                pltpu.SemaphoreType.DMA((z.fl + 1,)),
            ],
            compiler_params=pltpu.CompilerParams(vmem_limit_bytes=16 * 2**20),
            cost_estimate=pl.CostEstimate(
                flops=0, bytes_accessed=8 * z.n * z.main * z.c, transcendentals=0
            ),
        )(kept, got, *z.ordered(back))
    whole = jnp.zeros((z.fl, z.r, z.n, z.wc, z.c), BF)
    for k in range(z.n):
        rows = back[k].reshape(z.r, z.fl, 1, z.wc, z.c).transpose(1, 0, 2, 3, 4)
        whole = lax.dynamic_update_slice_in_dim(whole, rows, lax.axis_index("tm") ^ k, 2)
    (grad,) = call(functools.partial(add_up, z), [grad], kept, got)
    return whole.reshape(z.fl, z.r, z.w, z.c), grad


def on_device(frames_in, spatial, temporal, gain, q_w, k_w, v_w, o_w, cotangent):
    n = lax.axis_size("tm")
    space = lax.axis_size("space")
    z = Sizes(n, *frames_in.shape)
    one = 2 * z.r * z.block * z.c * z.c
    width, wide = z.c // space, z.c // n

    def exchange(pieces):
        pieces = list(pieces)
        for k in z.order[:-1]:
            pieces[k] = swap(pieces[k], "tm", k)
        return pieces

    edge = shape((z.fl * z.w, z.c))
    packed = call(
        functools.partial(pack_kernel, z),
        [shape((z.main + z.sides, z.c))] * n,
        frames_in,
        flops=one // 2,
    )
    near, far = call(
        functools.partial(edge_kernel, z), [edge, edge], frames_in, packed[0], flops=8 * one
    )
    got = exchange(packed)
    near, far = swap_both(near, far, "space")
    (own,) = call(
        functools.partial(own_inner_kernel, z),
        [shape((z.r, z.fl * z.w, z.c), F32)],
        frames_in,
        spatial,
        flops=8 * one,
        scratch=[pltpu.VMEM((3, z.r, z.fl * z.w, z.c), BF)],
    )
    own_act, near, far = call(
        functools.partial(own_act_kernel, z),
        [shape(frames_in.shape), shape((z.r, z.w, z.c)), shape((z.r, z.w, z.c))],
        own,
        near,
        far,
        spatial,
        cotangent,
        flops=3 * one,
    )
    near, far = swap_both(near, far, "tm")
    (own_grad,) = call(
        functools.partial(own_grad_kernel, z),
        [shape((z.c, 3 * z.c), F32)],
        own_act,
        cotangent,
        flops=9 * one // 4,
    )
    line = z.block + 2 * z.f
    x, close, apart = call(
        functools.partial(assemble_kernel, z),
        [shape((z.r, line, z.c)), shape((line, z.c)), shape((line, z.c))],
        *z.ordered(got),
    )
    close, apart = swap_both(close, apart, "space")
    (middle,) = call(
        functools.partial(middle_kernel, z),
        [shape((z.r - 2, z.block, z.c))],
        x,
        spatial,
        flops=9 * one * (z.r - 2) // z.r,
    )
    tied = lax.optimization_barrier((near, far, middle, close, apart))
    near, far, middle, close, apart = tied
    keep, send = call(
        functools.partial(cross_kernel, z, width),
        [shape((z.c // 2, 3 * z.c), F32), shape((z.c // 2, 3 * z.c))],
        own_grad,
        near,
        far,
        own_act,
        cotangent,
        flops=3 * one // 4,
    )
    other = swap(send, "space", 1)
    x, _ = lax.optimization_barrier((x, send))
    (border,) = call(
        functools.partial(border_kernel, z),
        [shape((2, z.block, z.c))],
        x,
        close,
        apart,
        spatial,
        flops=18 * one // z.r,
        scratch=[pltpu.VMEM((2, line, z.c), BF)],
    )
    other, border = lax.optimization_barrier((other, border))
    pieces = call(
        functools.partial(split_kernel, z),
        [shape((z.c // 2, 3 * wide), F32)] + [shape((z.c // 2, 3 * wide))] * (n - 1),
        keep,
        other,
    )
    border, *pieces = lax.optimization_barrier((border, *pieces))
    pieces = exchange(pieces)
    encoded = z.by_partner(call(
        functools.partial(main_kernel, z),
        [shape((z.r, z.piece, z.c))] * n,
        middle,
        border,
        x,
        temporal,
        gain.reshape(1, z.c),
        q_w,
        k_w,
        v_w,
        o_w,
        flops=9 * one,
    ))
    back = exchange(encoded)
    pieces = lax.optimization_barrier((*z.ordered(pieces), *z.ordered(encoded)))[:n]
    bit = 0
    while 2 << bit < space:
        half = (pieces[0].shape[0] // 2, 3 * wide)
        keep, send = call(
            functools.partial(halve_kernel, z, width, bit), [shape(half, F32), shape(half)], *pieces
        )
        pieces = (keep, swap(send, "space", 2 << bit))
        bit += 1
    encoded, kernel_grad = joined(z, back, *pieces)
    return encoded, kernel_grad.transpose(0, 2, 1)


def solution(mesh):
    tiles = P("tm", "space", None, None)
    return jax.shard_map(
        on_device,
        mesh=mesh,
        in_specs=(tiles,) + (P(),) * 7 + (tiles,),
        out_specs=(tiles, P(None, "tm", "space")),
        check_vma=False,
    )
```

```python
import functools

import jax
import jax.numpy as jnp
from jax import lax
from jax.experimental import pallas as pl
from jax.experimental.pallas import tpu as pltpu
from jax.sharding import PartitionSpec as P

BF = jnp.bfloat16
F32 = jnp.float32
VMEM = pl.BlockSpec(memory_space=pltpu.VMEM)


def call(kernel, outs, *args, flops=0, scratch=(), limit=16, light=False):
    moved = sum(a.size * a.dtype.itemsize for a in args)
    moved += sum(o.size * o.dtype.itemsize for o in outs)
    return pl.pallas_call(
        kernel,
        out_shape=tuple(outs),
        in_specs=[VMEM] * len(args),
        out_specs=tuple(VMEM for _ in outs),
        scratch_shapes=scratch,
        compiler_params=pltpu.CompilerParams(vmem_limit_bytes=limit * 2**20),
        cost_estimate=pl.CostEstimate(flops=flops, bytes_accessed=0 if light else moved, transcendentals=0),
    )(*args)


def shape(dims, kind=BF):
    return jax.ShapeDtypeStruct(dims, kind)


def chooser(rows, cols, source):
    q = lax.broadcasted_iota(jnp.int32, (rows, cols), 0)
    m = lax.broadcasted_iota(jnp.int32, (rows, cols), 1)
    return jnp.where(source(q) == m, 1.0, 0.0).astype(BF)


def moved(matrix, rows):
    return jnp.dot(matrix, rows, preferred_element_type=F32).astype(BF)


class Sizes:
    def __init__(self, count, frames, rows, cols, chans):
        self.n, self.fl, self.r, self.w, self.c = count, frames, rows, cols, chans
        self.f = count * frames
        self.wc = cols // count
        self.block = self.f * self.wc
        self.piece = frames * self.wc
        self.main = rows * self.piece
        self.sides = 2 * rows * frames
        self.order = sorted(range(count), key=lambda k: -k.bit_count())

    def ordered(self, pieces):
        return [pieces[k] for k in self.order]

    def by_partner(self, pieces):
        return [pieces[self.order.index(k)] for k in range(self.n)]


def even(axis):
    return lax.axis_index(axis) % 2 == 0


def edge_kernel(z, x_ref, after_ref, near, far):
    top, bottom = (flat(x_ref[:, r]) for r in (0, z.r - 1))
    near[...] = jnp.where(even("space"), bottom, top)
    far[...] = jnp.where(even("space"), top, bottom)


def pack_kernel(z, x_ref, *outs):
    me = lax.axis_index("tm")

    def source(q):
        k = q // z.piece
        f = q % z.piece // z.wc
        return f * z.w + (me ^ k) * z.wc + q % z.wc

    def edge(r, q):
        k = q // z.sides
        side = q % z.sides // (z.r * z.fl)
        row = q % (z.r * z.fl) // z.fl
        col = (me ^ k) * z.wc - 1 + side * (z.wc + 1)
        inside = (col >= 0) & (col < z.w) & (row == r)
        return jnp.where(inside, q % z.fl * z.w + col, -1)

    matrix = chooser(z.n * z.piece, z.fl * z.w, source)
    tails = jnp.zeros((z.n * z.sides, z.c), F32)
    for r in range(z.r):
        rows = x_ref[:, r].reshape(z.fl * z.w, z.c)
        cut = moved(matrix, rows)
        for k in range(z.n):
            outs[k][r * z.piece : (r + 1) * z.piece] = cut[k * z.piece : (k + 1) * z.piece]
        picked = chooser(z.n * z.sides, z.fl * z.w, functools.partial(edge, r))
        tails += jnp.dot(picked, rows, preferred_element_type=F32)
    tails = tails.astype(BF)
    for k in range(z.n):
        outs[k][z.main : z.main + z.sides] = tails[k * z.sides : (k + 1) * z.sides]


def aside(z, rows):
    count = z.fl * z.w
    left = chooser(count, count, lambda q: jnp.where(q % z.w > 0, q - 1, -1))
    right = chooser(count, count, lambda q: jnp.where(q % z.w < z.w - 1, q + 1, -1))
    return moved(left, rows), rows, moved(right, rows)


def own_inner_kernel(z, x_ref, w_ref, out, beside):
    for r in range(z.r):
        for dj, rows in enumerate(aside(z, x_ref[:, r].reshape(z.fl * z.w, z.c))):
            beside[dj, r] = rows
    for r in range(z.r):
        low, high = max(0, 1 - r), min(3, z.r + 1 - r)
        pieces = [beside[dj, r + di - 1] for di in range(low, high) for dj in range(3)]
        out[r] = taps(pieces, w_ref[low:high])


def own_act_kernel(z, part_ref, near_ref, far_ref, w_ref, cot_ref, out, near, far):
    lower = even("space")
    first = even("tm")
    for r in range(z.r):
        total = part_ref[r]
        for edge, di in ((0, 0), (z.r - 1, 2)):
            if r == edge:
                rows = jnp.where(lower == (di == 2), near_ref[...], far_ref[...])
                total += taps(aside(z, rows), w_ref[di])
        act = silu(total).reshape(z.fl, z.w, z.c)
        out[:, r] = act
        last = act[z.fl - 1]
        near[r] = jnp.where(first, last, cot_ref[0, r])
        far[r] = jnp.where(first, cot_ref[0, r], last)


def silu(total):
    return (total / (1.0 + jnp.exp(-total))).astype(BF)


def flat(value):
    return value.reshape(-1, value.shape[-1])


def outer(left, right):
    return lax.dot_general(
        flat(left), flat(right), (((0,), (0,)), ((), ())), preferred_element_type=F32
    )


def own_grad_kernel(z, act_ref, cot_ref, out):
    for k in range(3):
        out[:, k * z.c : (k + 1) * z.c] = outer(cot_ref[k:], act_ref[: z.fl - k])


def cross_kernel(z, width, part_ref, near_ref, far_ref, act_ref, cot_ref, keep, send):
    mine = even("space")
    before = jnp.where(even("tm"), far_ref[...], near_ref[...])
    after = jnp.where(even("tm"), near_ref[...], far_ref[...])
    for k in range(3):
        lanes = slice(k * z.c, (k + 1) * z.c)
        grad = part_ref[:, lanes]
        if k == 1:
            grad += outer(cot_ref[0], before)
        if k == 2:
            grad += outer(cot_ref[1], before)
            grad += outer(after, act_ref[z.fl - 2])
        for i in range(z.c // (2 * width)):
            low = grad[2 * i * width : (2 * i + 1) * width]
            high = grad[(2 * i + 1) * width : (2 * i + 2) * width]
            keep[i * width : (i + 1) * width, lanes] = jnp.where(mine, low, high)
            send[i * width : (i + 1) * width, lanes] = jnp.where(mine, high, low).astype(BF)


def gather_matrix(z, me):
    def source(q):
        s = q % z.f // z.fl
        return ((me ^ s) * z.fl + q % z.fl) * z.wc + q // z.f

    return chooser(z.block, z.block, source)


def assemble_kernel(z, *refs):
    parts, (out, near, far) = z.by_partner(refs[: z.n]), refs[z.n :]
    me = lax.axis_index("tm")
    lower = even("space")
    matrix = gather_matrix(z, me)

    def edge(q):
        head = q // z.f
        s = q % z.f // z.fl
        return ((me ^ s) * 2 * z.r + head) * z.fl + q % z.fl

    count = z.n * z.sides
    tails = jnp.concatenate([p[z.main : z.main + z.sides] for p in parts], axis=0)
    tails = moved(chooser(count, count, edge), tails)
    last = z.f + z.block
    for r in range(z.r):
        rows = jnp.concatenate([p[r * z.piece : (r + 1) * z.piece] for p in parts], axis=0)
        rows = moved(matrix, rows)
        left = tails[r * z.f : (r + 1) * z.f]
        right = tails[(z.r + r) * z.f : (z.r + r + 1) * z.f]
        out[r, 0 : z.f] = left
        out[r, z.f : last] = rows
        out[r, last : last + z.f] = right
    near[...] = jnp.where(lower, out[z.r - 1], out[0])
    far[...] = jnp.where(lower, out[0], out[z.r - 1])


def taps(pieces, weights):
    rows = jnp.concatenate(pieces, axis=1)
    return jnp.dot(rows, flat(weights), preferred_element_type=F32)


def conv_row(z, w_ref, three):
    return silu(taps([rows[dj * z.f : dj * z.f + z.block] for rows in three for dj in range(3)], w_ref[...]))


def middle_kernel(z, x_ref, w_ref, out):
    for r in range(1, z.r - 1):
        out[r - 1] = conv_row(z, w_ref, [x_ref.at[r + di] for di in (-1, 0, 1)])


def border_kernel(z, x_ref, near_ref, far_ref, w_ref, out, edges):
    lower = even("space")
    edges[0] = jnp.where(lower, far_ref[...], near_ref[...])
    edges[1] = jnp.where(lower, near_ref[...], far_ref[...])
    out[0] = conv_row(z, w_ref, [edges.at[0], x_ref.at[0], x_ref.at[1]])
    out[1] = conv_row(z, w_ref, [x_ref.at[z.r - 2], x_ref.at[z.r - 1], edges.at[1]])


def staged(z, stages):
    for step in range(z.r + len(stages) - 1):
        for late, stage in reversed(list(enumerate(stages))):
            if 0 <= step - late < z.r:
                stage(step - late)


def norm_kernel(
    z, middle_ref, border_ref, x_ref, t_ref, gain_ref, hidden_ref, normed_ref
):
    frame = lax.broadcasted_iota(jnp.int32, (z.block, z.c), 0) % z.f
    held = {}

    def activate(r):
        act = border_ref[r // (z.r - 1)] if r in (0, z.r - 1) else middle_ref[r - 1]
        wide = act.astype(F32)
        held["a", r] = [act] + [
            jnp.where(frame >= k, pltpu.roll(wide, k, 0), 0.0).astype(BF) for k in (1, 2)
        ]

    def hide(r):
        temporal = taps(held.pop(("a", r)), t_ref[...])
        hidden = (x_ref[r, z.f : z.f + z.block].astype(F32) + temporal).astype(BF)
        hidden_ref[r] = hidden
        held["h", r] = hidden

    def norm(r):
        wide = held.pop(("h", r)).astype(F32)
        mean = jnp.mean(wide * wide, axis=1, keepdims=True)
        normed_ref[r] = (wide * (1.0 / jnp.sqrt(mean + 1e-06)) * gain_ref[...]).astype(BF)

    staged(z, (activate, hide, norm))


def attend_kernel(z, hidden_ref, normed_ref, q_ref, k_ref, v_ref, o_ref, *outs):
    me = lax.axis_index("tm")
    a = lax.broadcasted_iota(jnp.int32, (z.block, z.block), 0)
    b = lax.broadcasted_iota(jnp.int32, (z.block, z.block), 1)
    allowed = (a // z.f == b // z.f) & (b % z.f <= a % z.f)
    scale = float(z.c) ** -0.5

    def source(q):
        t = ((me ^ (q // z.piece)) * z.fl) + q % z.piece // z.wc
        return q % z.wc * z.f + t

    back = chooser(z.block, z.block, source)
    held = {}

    def project(r):
        rows = normed_ref[r]
        held["q", r], held["k", r], held["v", r] = (
            jnp.dot(rows, w[...], preferred_element_type=F32).astype(BF)
            for w in (q_ref, k_ref, v_ref)
        )

    def score(r):
        held["s", r] = lax.dot_general(
            held.pop(("q", r)),
            held.pop(("k", r)),
            (((1,), (1,)), ((), ())),
            preferred_element_type=F32,
        )

    def weigh(r):
        scores = jnp.where(allowed, held.pop(("s", r)) * scale, -1e30)
        top = jnp.max(scores, axis=1, keepdims=True)
        expon = jnp.where(allowed, jnp.exp(scores - top), 0.0)
        held["t", r] = 1.0 / jnp.sum(expon, axis=1, keepdims=True)
        held["p", r] = expon.astype(BF)

    def mix(r):
        mixed = jnp.dot(held.pop(("p", r)), held.pop(("v", r)), preferred_element_type=F32)
        held["a", r] = (mixed * held.pop(("t", r))).astype(BF)

    def finish(r):
        encoded = hidden_ref[r].astype(F32) + jnp.dot(
            held.pop(("a", r)), o_ref[...], preferred_element_type=F32
        )
        held["e", r] = encoded.astype(BF)

    def spread(r):
        encoded = moved(back, held.pop(("e", r)))
        for out, k in zip(outs, z.order):
            out[r] = encoded[k * z.piece : (k + 1) * z.piece]

    staged(z, (project, score, weigh, mix, finish, spread))


def split_kernel(z, keep_ref, got_ref, *outs):
    me = lax.axis_index("tm")
    wide = z.c // z.n
    for tap in range(3):
        place = slice(tap * wide, (tap + 1) * wide)
        if wide % 128 == 0:
            for k in range(z.n):
                lanes = pl.ds(pl.multiple_of(tap * z.c + (me ^ k) * wide, 128), wide)
                total = keep_ref[:, lanes] + got_ref[:, lanes].astype(F32)
                outs[k][:, place] = total.astype(outs[k].dtype)
            continue
        lanes = slice(tap * z.c, (tap + 1) * z.c)
        total = keep_ref[:, lanes] + got_ref[:, lanes].astype(F32)
        for k in range(z.n):
            cut = total[:, 0:wide]
            for i in range(1, z.n):
                cut = jnp.where((me ^ k) == i, total[:, i * wide : (i + 1) * wide], cut)
            outs[k][:, place] = cut.astype(outs[k].dtype)


def swap(value, axis, k):
    count = lax.axis_size(axis)
    return lax.ppermute(value, axis, [(i, i ^ k) for i in range(count)])


def swap_both(near, far, axis):
    pairs = [(i, i + 1) for i in range(1, lax.axis_size(axis) - 1, 2)]
    far = lax.ppermute(far, axis, pairs + [(b, a) for a, b in pairs])
    return swap(near, axis, 1), far


def halve_kernel(z, width, bit, *refs):
    parts, (keep, send) = refs[:-2], refs[-2:]
    total = sum(part[...].astype(F32) for part in parts)
    lower = lax.axis_index("space") // (2 << bit) % 2 == 0
    for i in range(keep.shape[0] // width):
        low = total[2 * i * width : (2 * i + 1) * width]
        high = total[(2 * i + 1) * width : (2 * i + 2) * width]
        rows = slice(i * width, (i + 1) * width)
        keep[rows] = jnp.where(lower, low, high)
        send[rows] = jnp.where(lower, high, low).astype(BF)


def add_up(z, kept_ref, got_ref, out):
    wide = z.c // z.n
    total = kept_ref[...] + got_ref[...].astype(F32)
    for k in range(3):
        out[k] = total[:, k * wide : (k + 1) * wide]


def join_kernel(z, kept_ref, got_ref, *refs):
    parts, (out, grad, whole, total, sem) = z.by_partner(refs[: z.n]), refs[z.n :]
    me = lax.axis_index("tm")
    add_up(z, kept_ref, got_ref, total)
    copies = [pltpu.make_async_copy(total, grad, sem.at[z.fl])]
    copies[0].start()
    for f in range(z.fl):
        for k in range(z.n):
            cols = pl.ds(pl.multiple_of((me ^ k) * z.wc, z.wc), z.wc)
            whole[f, :, cols] = parts[k][:, f * z.wc : (f + 1) * z.wc]
        copies.append(pltpu.make_async_copy(whole.at[f], out.at[f], sem.at[f]))
        copies[-1].start()
    for copy in copies:
        copy.wait()


def joined(z, back, kept, got):
    grad = shape((3, kept.shape[0], z.c // z.n), F32)
    if z.wc % 16 == 0:
        return pl.pallas_call(
            functools.partial(join_kernel, z),
            out_shape=(shape((z.fl, z.r, z.w, z.c)), grad),
            in_specs=[VMEM] * (2 + z.n),
            out_specs=(pl.BlockSpec(memory_space=pl.ANY),) * 2,
            scratch_shapes=[
                pltpu.VMEM((z.fl, z.r, z.w, z.c), BF),
                pltpu.VMEM(grad.shape, F32),
                pltpu.SemaphoreType.DMA((z.fl + 1,)),
            ],
            compiler_params=pltpu.CompilerParams(vmem_limit_bytes=16 * 2**20),
            cost_estimate=pl.CostEstimate(
                flops=0, bytes_accessed=8 * z.n * z.main * z.c, transcendentals=0
            ),
        )(kept, got, *z.ordered(back))
    whole = jnp.zeros((z.fl, z.r, z.n, z.wc, z.c), BF)
    for k in range(z.n):
        rows = back[k].reshape(z.r, z.fl, 1, z.wc, z.c).transpose(1, 0, 2, 3, 4)
        whole = lax.dynamic_update_slice_in_dim(whole, rows, lax.axis_index("tm") ^ k, 2)
    (grad,) = call(functools.partial(add_up, z), [grad], kept, got)
    return whole.reshape(z.fl, z.r, z.w, z.c), grad


def on_device(frames_in, spatial, temporal, gain, q_w, k_w, v_w, o_w, cotangent):
    n = lax.axis_size("tm")
    space = lax.axis_size("space")
    z = Sizes(n, *frames_in.shape)
    one = 2 * z.r * z.block * z.c * z.c
    width, wide = z.c // space, z.c // n

    def exchange(pieces):
        pieces = list(pieces)
        for k in z.order[:-1]:
            pieces[k] = swap(pieces[k], "tm", k)
        return pieces

    edge = shape((z.fl * z.w, z.c))
    packed = call(
        functools.partial(pack_kernel, z),
        [shape((z.main + z.sides, z.c))] * n,
        frames_in,
        flops=one // 2,
    )
    near, far = call(
        functools.partial(edge_kernel, z), [edge, edge], frames_in, packed[0], flops=8 * one
    )
    got = exchange(packed)
    near, far = swap_both(near, far, "space")
    (own,) = call(
        functools.partial(own_inner_kernel, z),
        [shape((z.r, z.fl * z.w, z.c), F32)],
        frames_in,
        spatial,
        flops=8 * one,
        scratch=[pltpu.VMEM((3, z.r, z.fl * z.w, z.c), BF)],
    )
    own_act, near, far = call(
        functools.partial(own_act_kernel, z),
        [shape(frames_in.shape), shape((z.r, z.w, z.c)), shape((z.r, z.w, z.c))],
        own,
        near,
        far,
        spatial,
        cotangent,
        flops=3 * one,
    )
    near, far = swap_both(near, far, "tm")
    (own_grad,) = call(
        functools.partial(own_grad_kernel, z),
        [shape((z.c, 3 * z.c), F32)],
        own_act,
        cotangent,
        flops=9 * one // 4,
    )
    line = z.block + 2 * z.f
    x, close, apart = call(
        functools.partial(assemble_kernel, z),
        [shape((z.r, line, z.c)), shape((line, z.c)), shape((line, z.c))],
        *z.ordered(got),
    )
    close, apart = swap_both(close, apart, "space")
    (middle,) = call(
        functools.partial(middle_kernel, z),
        [shape((z.r - 2, z.block, z.c))],
        x,
        spatial,
        flops=9 * one * (z.r - 2) // z.r,
    )
    (border,) = call(
        functools.partial(border_kernel, z),
        [shape((2, z.block, z.c))],
        x,
        close,
        apart,
        spatial,
        light=True,
        scratch=[pltpu.VMEM((2, line, z.c), BF)],
    )
    near, far, border, middle = lax.optimization_barrier((near, far, border, middle))
    keep, send = call(
        functools.partial(cross_kernel, z, width),
        [shape((z.c // 2, 3 * z.c), F32), shape((z.c // 2, 3 * z.c))],
        own_grad,
        near,
        far,
        own_act,
        cotangent,
        flops=3 * one // 4,
    )
    other = swap(send, "space", 1)
    border, _ = lax.optimization_barrier((border, send))
    hidden, normed = call(
        functools.partial(norm_kernel, z),
        [shape((z.r, z.block, z.c))] * 2,
        middle,
        border,
        x,
        temporal,
        gain.reshape(1, z.c),
        flops=3 * one,
    )
    pieces = call(
        functools.partial(split_kernel, z),
        [shape((z.c // 2, 3 * wide), F32)] + [shape((z.c // 2, 3 * wide))] * (n - 1),
        keep,
        other,
    )
    normed, *pieces = lax.optimization_barrier((normed, *pieces))
    pieces = exchange(pieces)
    encoded = call(
        functools.partial(attend_kernel, z),
        [shape((z.r, z.piece, z.c))] * n,
        hidden,
        normed,
        q_w,
        k_w,
        v_w,
        o_w,
        flops=5 * one,
    )
    encoded = z.by_partner(encoded)
    back = exchange(encoded)
    pieces = lax.optimization_barrier((*z.ordered(pieces), *z.ordered(encoded)))[:n]
    bit = 0
    while 2 << bit < space:
        half = (pieces[0].shape[0] // 2, 3 * wide)
        keep, send = call(
            functools.partial(halve_kernel, z, width, bit), [shape(half, F32), shape(half)], *pieces
        )
        pieces = (keep, swap(send, "space", 2 << bit))
        bit += 1
    encoded, kernel_grad = joined(z, back, *pieces)
    return encoded, kernel_grad.transpose(0, 2, 1)


def solution(mesh):
    tiles = P("tm", "space", None, None)
    return jax.shard_map(
        on_device,
        mesh=mesh,
        in_specs=(tiles,) + (P(),) * 7 + (tiles,),
        out_specs=(tiles, P(None, "tm", "space")),
        check_vma=False,
    )
```

```python
import functools

import jax
import jax.numpy as jnp
from jax import lax
from jax.experimental import pallas as pl
from jax.experimental.pallas import tpu as pltpu
from jax.sharding import PartitionSpec as P

BF = jnp.bfloat16
F32 = jnp.float32
VMEM = pl.BlockSpec(memory_space=pltpu.VMEM)


def call(kernel, outs, *args, flops=0, scratch=(), limit=16):
    moved = sum(a.size * a.dtype.itemsize for a in args)
    moved += sum(o.size * o.dtype.itemsize for o in outs)
    return pl.pallas_call(
        kernel,
        out_shape=tuple(outs),
        in_specs=[VMEM] * len(args),
        out_specs=tuple(VMEM for _ in outs),
        scratch_shapes=scratch,
        compiler_params=pltpu.CompilerParams(vmem_limit_bytes=limit * 2**20),
        cost_estimate=pl.CostEstimate(flops=flops, bytes_accessed=moved, transcendentals=0),
    )(*args)


def shape(dims, kind=BF):
    return jax.ShapeDtypeStruct(dims, kind)


def chooser(rows, cols, source):
    q = lax.broadcasted_iota(jnp.int32, (rows, cols), 0)
    m = lax.broadcasted_iota(jnp.int32, (rows, cols), 1)
    return jnp.where(source(q) == m, 1.0, 0.0).astype(BF)


def moved(matrix, rows):
    return jnp.dot(matrix, rows, preferred_element_type=F32).astype(BF)


class Sizes:
    def __init__(self, count, frames, rows, cols, chans):
        self.n, self.fl, self.r, self.w, self.c = count, frames, rows, cols, chans
        self.f = count * frames
        self.wc = cols // count
        self.block = self.f * self.wc
        self.piece = frames * self.wc
        self.main = rows * self.piece
        self.sides = 2 * rows * frames
        self.order = sorted(range(count), key=lambda k: -k.bit_count())

    def ordered(self, pieces):
        return [pieces[k] for k in self.order]

    def by_partner(self, pieces):
        return [pieces[self.order.index(k)] for k in range(self.n)]


def even(axis):
    return lax.axis_index(axis) % 2 == 0


def edge_kernel(z, x_ref, after_ref, near, far):
    top, bottom = (flat(x_ref[:, r]) for r in (0, z.r - 1))
    near[...] = jnp.where(even("space"), bottom, top)
    far[...] = jnp.where(even("space"), top, bottom)


def pack_kernel(z, x_ref, *outs):
    me = lax.axis_index("tm")

    def source(q):
        k = q // z.piece
        f = q % z.piece // z.wc
        return f * z.w + (me ^ k) * z.wc + q % z.wc

    def edge(r, q):
        k = q // z.sides
        side = q % z.sides // (z.r * z.fl)
        row = q % (z.r * z.fl) // z.fl
        col = (me ^ k) * z.wc - 1 + side * (z.wc + 1)
        inside = (col >= 0) & (col < z.w) & (row == r)
        return jnp.where(inside, q % z.fl * z.w + col, -1)

    matrix = chooser(z.n * z.piece, z.fl * z.w, source)
    tails = jnp.zeros((z.n * z.sides, z.c), F32)
    for r in range(z.r):
        rows = x_ref[:, r].reshape(z.fl * z.w, z.c)
        cut = moved(matrix, rows)
        for k in range(z.n):
            outs[k][r * z.piece : (r + 1) * z.piece] = cut[k * z.piece : (k + 1) * z.piece]
        picked = chooser(z.n * z.sides, z.fl * z.w, functools.partial(edge, r))
        tails += jnp.dot(picked, rows, preferred_element_type=F32)
    tails = tails.astype(BF)
    for k in range(z.n):
        outs[k][z.main : z.main + z.sides] = tails[k * z.sides : (k + 1) * z.sides]


def aside(z, rows):
    count = z.fl * z.w
    left = chooser(count, count, lambda q: jnp.where(q % z.w > 0, q - 1, -1))
    right = chooser(count, count, lambda q: jnp.where(q % z.w < z.w - 1, q + 1, -1))
    return moved(left, rows), rows, moved(right, rows)


def own_inner_kernel(z, x_ref, w_ref, out, beside):
    for r in range(z.r):
        for dj, rows in enumerate(aside(z, x_ref[:, r].reshape(z.fl * z.w, z.c))):
            beside[dj, r] = rows
    for r in range(z.r):
        low, high = max(0, 1 - r), min(3, z.r + 1 - r)
        pieces = [beside[dj, r + di - 1] for di in range(low, high) for dj in range(3)]
        out[r] = taps(pieces, w_ref[low:high])


def own_act_kernel(z, part_ref, near_ref, far_ref, w_ref, cot_ref, out, near, far):
    lower = even("space")
    first = even("tm")
    for r in range(z.r):
        total = part_ref[r]
        for edge, di in ((0, 0), (z.r - 1, 2)):
            if r == edge:
                rows = jnp.where(lower == (di == 2), near_ref[...], far_ref[...])
                total += taps(aside(z, rows), w_ref[di])
        act = silu(total).reshape(z.fl, z.w, z.c)
        out[:, r] = act
        last = act[z.fl - 1]
        near[r] = jnp.where(first, last, cot_ref[0, r])
        far[r] = jnp.where(first, cot_ref[0, r], last)


def silu(total):
    half = 0.5 * total
    return (half + half * jnp.tanh(half)).astype(BF)


def flat(value):
    return value.reshape(-1, value.shape[-1])


def outer(left, right):
    return lax.dot_general(
        flat(left), flat(right), (((0,), (0,)), ((), ())), preferred_element_type=F32
    )


def own_grad_kernel(z, act_ref, cot_ref, out):
    for k in range(3):
        out[:, k * z.c : (k + 1) * z.c] = outer(cot_ref[k:], act_ref[: z.fl - k])


def cross_kernel(z, width, part_ref, near_ref, far_ref, act_ref, cot_ref, keep, send):
    mine = even("space")
    before = jnp.where(even("tm"), far_ref[...], near_ref[...])
    after = jnp.where(even("tm"), near_ref[...], far_ref[...])
    for k in range(3):
        lanes = slice(k * z.c, (k + 1) * z.c)
        grad = part_ref[:, lanes]
        if k == 1:
            grad += outer(cot_ref[0], before)
        if k == 2:
            grad += outer(cot_ref[1], before)
            grad += outer(after, act_ref[z.fl - 2])
        for i in range(z.c // (2 * width)):
            low = grad[2 * i * width : (2 * i + 1) * width]
            high = grad[(2 * i + 1) * width : (2 * i + 2) * width]
            keep[i * width : (i + 1) * width, lanes] = jnp.where(mine, low, high)
            send[i * width : (i + 1) * width, lanes] = jnp.where(mine, high, low).astype(BF)


def gather_matrix(z, me):
    def source(q):
        s = q % z.f // z.fl
        return ((me ^ s) * z.fl + q % z.fl) * z.wc + q // z.f

    return chooser(z.block, z.block, source)


def assemble_kernel(z, *refs):
    parts, (out, near, far) = z.by_partner(refs[: z.n]), refs[z.n :]
    me = lax.axis_index("tm")
    lower = even("space")
    matrix = gather_matrix(z, me)

    def edge(q):
        head = q // z.f
        s = q % z.f // z.fl
        return ((me ^ s) * 2 * z.r + head) * z.fl + q % z.fl

    count = z.n * z.sides
    tails = jnp.concatenate([p[z.main : z.main + z.sides] for p in parts], axis=0)
    tails = moved(chooser(count, count, edge), tails)
    last = z.f + z.block
    for r in range(z.r):
        rows = jnp.concatenate([p[r * z.piece : (r + 1) * z.piece] for p in parts], axis=0)
        rows = moved(matrix, rows)
        left = tails[r * z.f : (r + 1) * z.f]
        right = tails[(z.r + r) * z.f : (z.r + r + 1) * z.f]
        out[r, 0 : z.f] = left
        out[r, z.f : last] = rows
        out[r, last : last + z.f] = right
    near[...] = jnp.where(lower, out[z.r - 1], out[0])
    far[...] = jnp.where(lower, out[0], out[z.r - 1])


def taps(pieces, weights):
    rows = jnp.concatenate(pieces, axis=1)
    return jnp.dot(rows, flat(weights), preferred_element_type=F32)


def conv_row(z, w_ref, three):
    return silu(taps([rows[dj * z.f : dj * z.f + z.block] for rows in three for dj in range(3)], w_ref[...]))


def middle_kernel(z, x_ref, w_ref, out):
    for r in range(1, z.r - 1):
        out[r - 1] = conv_row(z, w_ref, [x_ref.at[r + di] for di in (-1, 0, 1)])


def border_kernel(z, x_ref, near_ref, far_ref, w_ref, out, edges):
    lower = even("space")
    edges[0] = jnp.where(lower, far_ref[...], near_ref[...])
    edges[1] = jnp.where(lower, near_ref[...], far_ref[...])
    out[0] = conv_row(z, w_ref, [edges.at[0], x_ref.at[0], x_ref.at[1]])
    out[1] = conv_row(z, w_ref, [x_ref.at[z.r - 2], x_ref.at[z.r - 1], edges.at[1]])


def staged(z, stages):
    for step in range(z.r + len(stages) - 1):
        for late, stage in reversed(list(enumerate(stages))):
            if 0 <= step - late < z.r:
                stage(step - late)


def main_kernel(
    z, middle_ref, border_ref, x_ref, t_ref, gain_ref, q_ref, k_ref, v_ref, o_ref, *outs
):
    me = lax.axis_index("tm")
    a = lax.broadcasted_iota(jnp.int32, (z.block, z.block), 0)
    b = lax.broadcasted_iota(jnp.int32, (z.block, z.block), 1)
    allowed = (a // z.f == b // z.f) & (b % z.f <= a % z.f)
    scale = float(z.c) ** -0.5

    def source(q):
        t = ((me ^ (q // z.piece)) * z.fl) + q % z.piece // z.wc
        return q % z.wc * z.f + t

    back = chooser(z.block, z.block, source)
    frame = lax.broadcasted_iota(jnp.int32, (z.block, z.c), 0) % z.f
    held = {}

    def activate(r):
        act = border_ref[r // (z.r - 1)] if r in (0, z.r - 1) else middle_ref[r - 1]
        wide = act.astype(F32)
        held["a", r] = [act] + [
            jnp.where(frame >= k, pltpu.roll(wide, k, 0), 0.0).astype(BF) for k in (1, 2)
        ]

    def hide(r):
        temporal = taps(held.pop(("a", r)), t_ref[...])
        hidden = (x_ref[r, z.f : z.f + z.block].astype(F32) + temporal).astype(BF)
        held["h", r] = hidden

    def norm(r):
        wide = held["h", r].astype(F32)
        mean = jnp.mean(wide * wide, axis=1, keepdims=True)
        held["n", r] = (wide * lax.rsqrt(mean + 1e-06) * gain_ref[...]).astype(BF)

    def project(r):
        rows = held.pop(("n", r))
        held["q", r], held["k", r], held["v", r] = (
            jnp.dot(rows, w[...], preferred_element_type=F32).astype(BF)
            for w in (q_ref, k_ref, v_ref)
        )

    def score(r):
        held["s", r] = lax.dot_general(
            held.pop(("q", r)),
            held.pop(("k", r)),
            (((1,), (1,)), ((), ())),
            preferred_element_type=F32,
        )

    def weigh(r):
        scores = jnp.where(allowed, held.pop(("s", r)) * scale, -1e30)
        top = jnp.max(scores, axis=1, keepdims=True)
        expon = jnp.where(allowed, jnp.exp(scores - top), 0.0)
        held["t", r] = 1.0 / jnp.sum(expon, axis=1, keepdims=True)
        held["p", r] = expon.astype(BF)

    def mix(r):
        mixed = jnp.dot(held.pop(("p", r)), held.pop(("v", r)), preferred_element_type=F32)
        held["a", r] = (mixed * held.pop(("t", r))).astype(BF)

    def finish(r):
        encoded = held.pop(("h", r)).astype(F32) + jnp.dot(
            held.pop(("a", r)), o_ref[...], preferred_element_type=F32
        )
        held["e", r] = encoded.astype(BF)

    def spread(r):
        encoded = moved(back, held.pop(("e", r)))
        for out, k in zip(outs, z.order):
            out[r] = encoded[k * z.piece : (k + 1) * z.piece]

    staged(z, (activate, hide, norm, project, score, weigh, mix, finish, spread))


def split_kernel(z, keep_ref, got_ref, *outs):
    me = lax.axis_index("tm")
    wide = z.c // z.n
    for tap in range(3):
        place = slice(tap * wide, (tap + 1) * wide)
        if wide % 128 == 0:
            for k in range(z.n):
                lanes = pl.ds(pl.multiple_of(tap * z.c + (me ^ k) * wide, 128), wide)
                total = keep_ref[:, lanes] + got_ref[:, lanes].astype(F32)
                outs[k][:, place] = total.astype(outs[k].dtype)
            continue
        lanes = slice(tap * z.c, (tap + 1) * z.c)
        total = keep_ref[:, lanes] + got_ref[:, lanes].astype(F32)
        for k in range(z.n):
            cut = total[:, 0:wide]
            for i in range(1, z.n):
                cut = jnp.where((me ^ k) == i, total[:, i * wide : (i + 1) * wide], cut)
            outs[k][:, place] = cut.astype(outs[k].dtype)


def swap(value, axis, k):
    count = lax.axis_size(axis)
    return lax.ppermute(value, axis, [(i, i ^ k) for i in range(count)])


def swap_both(near, far, axis):
    pairs = [(i, i + 1) for i in range(1, lax.axis_size(axis) - 1, 2)]
    far = lax.ppermute(far, axis, pairs + [(b, a) for a, b in pairs])
    return swap(near, axis, 1), far


def halve_kernel(z, width, bit, *refs):
    parts, (keep, send) = refs[:-2], refs[-2:]
    total = sum(part[...].astype(F32) for part in parts)
    lower = lax.axis_index("space") // (2 << bit) % 2 == 0
    for i in range(keep.shape[0] // width):
        low = total[2 * i * width : (2 * i + 1) * width]
        high = total[(2 * i + 1) * width : (2 * i + 2) * width]
        rows = slice(i * width, (i + 1) * width)
        keep[rows] = jnp.where(lower, low, high)
        send[rows] = jnp.where(lower, high, low).astype(BF)


def add_up(z, kept_ref, got_ref, out):
    wide = z.c // z.n
    total = kept_ref[...] + got_ref[...].astype(F32)
    for k in range(3):
        out[k] = total[:, k * wide : (k + 1) * wide]


def join_kernel(z, kept_ref, got_ref, *refs):
    parts, (out, grad, whole, total, sem) = z.by_partner(refs[: z.n]), refs[z.n :]
    me = lax.axis_index("tm")
    add_up(z, kept_ref, got_ref, total)
    copies = [pltpu.make_async_copy(total, grad, sem.at[z.fl])]
    copies[0].start()
    for f in range(z.fl):
        for k in range(z.n):
            cols = pl.ds(pl.multiple_of((me ^ k) * z.wc, z.wc), z.wc)
            whole[f, :, cols] = parts[k][:, f * z.wc : (f + 1) * z.wc]
        copies.append(pltpu.make_async_copy(whole.at[f], out.at[f], sem.at[f]))
        copies[-1].start()
    for copy in copies:
        copy.wait()


def joined(z, back, kept, got):
    grad = shape((3, kept.shape[0], z.c // z.n), F32)
    if z.wc % 16 == 0:
        return pl.pallas_call(
            functools.partial(join_kernel, z),
            out_shape=(shape((z.fl, z.r, z.w, z.c)), grad),
            in_specs=[VMEM] * (2 + z.n),
            out_specs=(pl.BlockSpec(memory_space=pl.ANY),) * 2,
            scratch_shapes=[
                pltpu.VMEM((z.fl, z.r, z.w, z.c), BF),
                pltpu.VMEM(grad.shape, F32),
                pltpu.SemaphoreType.DMA((z.fl + 1,)),
            ],
            compiler_params=pltpu.CompilerParams(vmem_limit_bytes=16 * 2**20),
            cost_estimate=pl.CostEstimate(
                flops=0, bytes_accessed=8 * z.n * z.main * z.c, transcendentals=0
            ),
        )(kept, got, *z.ordered(back))
    whole = jnp.zeros((z.fl, z.r, z.n, z.wc, z.c), BF)
    for k in range(z.n):
        rows = back[k].reshape(z.r, z.fl, 1, z.wc, z.c).transpose(1, 0, 2, 3, 4)
        whole = lax.dynamic_update_slice_in_dim(whole, rows, lax.axis_index("tm") ^ k, 2)
    (grad,) = call(functools.partial(add_up, z), [grad], kept, got)
    return whole.reshape(z.fl, z.r, z.w, z.c), grad


def on_device(frames_in, spatial, temporal, gain, q_w, k_w, v_w, o_w, cotangent):
    n = lax.axis_size("tm")
    space = lax.axis_size("space")
    z = Sizes(n, *frames_in.shape)
    one = 2 * z.r * z.block * z.c * z.c
    width, wide = z.c // space, z.c // n

    def exchange(pieces):
        pieces = list(pieces)
        for k in z.order[:-1]:
            pieces[k] = swap(pieces[k], "tm", k)
        return pieces

    edge = shape((z.fl * z.w, z.c))
    packed = call(
        functools.partial(pack_kernel, z),
        [shape((z.main + z.sides, z.c))] * n,
        frames_in,
        flops=one // 2,
    )
    near, far = call(
        functools.partial(edge_kernel, z), [edge, edge], frames_in, packed[0], flops=8 * one
    )
    got = exchange(packed)
    near, far = swap_both(near, far, "space")
    (own,) = call(
        functools.partial(own_inner_kernel, z),
        [shape((z.r, z.fl * z.w, z.c), F32)],
        frames_in,
        spatial,
        flops=8 * one,
        scratch=[pltpu.VMEM((3, z.r, z.fl * z.w, z.c), BF)],
    )
    own_act, near, far = call(
        functools.partial(own_act_kernel, z),
        [shape(frames_in.shape), shape((z.r, z.w, z.c)), shape((z.r, z.w, z.c))],
        own,
        near,
        far,
        spatial,
        cotangent,
        flops=3 * one,
    )
    near, far = swap_both(near, far, "tm")
    (own_grad,) = call(
        functools.partial(own_grad_kernel, z),
        [shape((z.c, 3 * z.c), F32)],
        own_act,
        cotangent,
        flops=9 * one // 4,
    )
    line = z.block + 2 * z.f
    x, close, apart = call(
        functools.partial(assemble_kernel, z),
        [shape((z.r, line, z.c)), shape((line, z.c)), shape((line, z.c))],
        *z.ordered(got),
    )
    close, apart = swap_both(close, apart, "space")
    (middle,) = call(
        functools.partial(middle_kernel, z),
        [shape((z.r - 2, z.block, z.c))],
        x,
        spatial,
        flops=9 * one * (z.r - 2) // z.r,
    )
    tied = lax.optimization_barrier((near, far, middle, close, apart))
    near, far, middle, close, apart = tied
    keep, send = call(
        functools.partial(cross_kernel, z, width),
        [shape((z.c // 2, 3 * z.c), F32), shape((z.c // 2, 3 * z.c))],
        own_grad,
        near,
        far,
        own_act,
        cotangent,
        flops=3 * one // 4,
    )
    other = swap(send, "space", 1)
    x, _ = lax.optimization_barrier((x, send))
    (border,) = call(
        functools.partial(border_kernel, z),
        [shape((2, z.block, z.c))],
        x,
        close,
        apart,
        spatial,
        flops=18 * one // z.r,
        scratch=[pltpu.VMEM((2, line, z.c), BF)],
    )
    other, border = lax.optimization_barrier((other, border))
    pieces = call(
        functools.partial(split_kernel, z),
        [shape((z.c // 2, 3 * wide), F32)] + [shape((z.c // 2, 3 * wide))] * (n - 1),
        keep,
        other,
    )
    border, *pieces = lax.optimization_barrier((border, *pieces))
    pieces = exchange(pieces)
    encoded = z.by_partner(call(
        functools.partial(main_kernel, z),
        [shape((z.r, z.piece, z.c))] * n,
        middle,
        border,
        x,
        temporal,
        gain.reshape(1, z.c),
        q_w,
        k_w,
        v_w,
        o_w,
        flops=9 * one,
    ))
    back = exchange(encoded)
    pieces = lax.optimization_barrier((*z.ordered(pieces), *z.ordered(encoded)))[:n]
    bit = 0
    while 2 << bit < space:
        half = (pieces[0].shape[0] // 2, 3 * wide)
        keep, send = call(
            functools.partial(halve_kernel, z, width, bit), [shape(half, F32), shape(half)], *pieces
        )
        pieces = (keep, swap(send, "space", 2 << bit))
        bit += 1
    encoded, kernel_grad = joined(z, back, *pieces)
    return encoded, kernel_grad.transpose(0, 2, 1)


def solution(mesh):
    tiles = P("tm", "space", None, None)
    return jax.shard_map(
        on_device,
        mesh=mesh,
        in_specs=(tiles,) + (P(),) * 7 + (tiles,),
        out_specs=(tiles, P(None, "tm", "space")),
        check_vma=False,
    )
```

```python
import functools

import jax
import jax.numpy as jnp
from jax import lax
from jax.experimental import pallas as pl
from jax.experimental.pallas import tpu as pltpu
from jax.sharding import PartitionSpec as P

BF = jnp.bfloat16
F32 = jnp.float32
VMEM = pl.BlockSpec(memory_space=pltpu.VMEM)


def call(kernel, outs, *args, flops=0, scratch=(), limit=16):
    moved = sum(a.size * a.dtype.itemsize for a in args)
    moved += sum(o.size * o.dtype.itemsize for o in outs)
    return pl.pallas_call(
        kernel,
        out_shape=tuple(outs),
        in_specs=[VMEM] * len(args),
        out_specs=tuple(VMEM for _ in outs),
        scratch_shapes=scratch,
        compiler_params=pltpu.CompilerParams(vmem_limit_bytes=limit * 2**20),
        cost_estimate=pl.CostEstimate(flops=flops, bytes_accessed=moved, transcendentals=0),
    )(*args)


def shape(dims, kind=BF):
    return jax.ShapeDtypeStruct(dims, kind)


def chooser(rows, cols, source):
    q = lax.broadcasted_iota(jnp.int32, (rows, cols), 0)
    m = lax.broadcasted_iota(jnp.int32, (rows, cols), 1)
    return jnp.where(source(q) == m, 1.0, 0.0).astype(BF)


def moved(matrix, rows):
    return jnp.dot(matrix, rows, preferred_element_type=F32).astype(BF)


class Sizes:
    def __init__(self, count, frames, rows, cols, chans):
        self.n, self.fl, self.r, self.w, self.c = count, frames, rows, cols, chans
        self.f = count * frames
        self.wc = cols // count
        self.block = self.f * self.wc
        self.piece = frames * self.wc
        self.main = rows * self.piece
        self.sides = 2 * rows * frames
        self.order = sorted(range(count), key=lambda k: -k.bit_count())

    def ordered(self, pieces):
        return [pieces[k] for k in self.order]

    def by_partner(self, pieces):
        return [pieces[self.order.index(k)] for k in range(self.n)]


def even(axis):
    return lax.axis_index(axis) % 2 == 0


def edge_kernel(z, x_ref, after_ref, near, far):
    top, bottom = (flat(x_ref[:, r]) for r in (0, z.r - 1))
    near[...] = jnp.where(even("space"), bottom, top)
    far[...] = jnp.where(even("space"), top, bottom)


def pack_kernel(z, x_ref, *outs):
    me = lax.axis_index("tm")

    def source(q):
        k = q // z.piece
        f = q % z.piece // z.wc
        return f * z.w + (me ^ k) * z.wc + q % z.wc

    def edge(r, q):
        k = q // z.sides
        side = q % z.sides // (z.r * z.fl)
        row = q % (z.r * z.fl) // z.fl
        col = (me ^ k) * z.wc - 1 + side * (z.wc + 1)
        inside = (col >= 0) & (col < z.w) & (row == r)
        return jnp.where(inside, q % z.fl * z.w + col, -1)

    matrix = chooser(z.n * z.piece, z.fl * z.w, source)
    tails = jnp.zeros((z.n * z.sides, z.c), F32)
    for r in range(z.r):
        rows = x_ref[:, r].reshape(z.fl * z.w, z.c)
        cut = moved(matrix, rows)
        for k in range(z.n):
            outs[k][r * z.piece : (r + 1) * z.piece] = cut[k * z.piece : (k + 1) * z.piece]
        picked = chooser(z.n * z.sides, z.fl * z.w, functools.partial(edge, r))
        tails += jnp.dot(picked, rows, preferred_element_type=F32)
    tails = tails.astype(BF)
    for k in range(z.n):
        outs[k][z.main : z.main + z.sides] = tails[k * z.sides : (k + 1) * z.sides]


def aside(z, rows):
    count = z.fl * z.w
    left = chooser(count, count, lambda q: jnp.where(q % z.w > 0, q - 1, -1))
    right = chooser(count, count, lambda q: jnp.where(q % z.w < z.w - 1, q + 1, -1))
    return moved(left, rows), rows, moved(right, rows)


def own_inner_kernel(z, x_ref, w_ref, out, beside):
    for r in range(z.r):
        for dj, rows in enumerate(aside(z, x_ref[:, r].reshape(z.fl * z.w, z.c))):
            beside[dj, r] = rows
    for r in range(z.r):
        low, high = max(0, 1 - r), min(3, z.r + 1 - r)
        pieces = [beside[dj, r + di - 1] for di in range(low, high) for dj in range(3)]
        out[r] = taps(pieces, w_ref[low:high])


def own_act_kernel(z, part_ref, near_ref, far_ref, w_ref, cot_ref, out, far, near):
    lower = even("space")
    first = even("tm")
    for r in range(z.r):
        total = part_ref[r]
        for edge, di in ((0, 0), (z.r - 1, 2)):
            if r == edge:
                rows = jnp.where(lower == (di == 2), near_ref[...], far_ref[...])
                total += taps(aside(z, rows), w_ref[di])
        act = silu(total).reshape(z.fl, z.w, z.c)
        out[:, r] = act
        last = act[z.fl - 1]
        near[r] = jnp.where(first, last, cot_ref[0, r])
        far[r] = jnp.where(first, cot_ref[0, r], last)


def silu(total):
    return (total / (1.0 + jnp.exp(-total))).astype(BF)


def flat(value):
    return value.reshape(-1, value.shape[-1])


def outer(left, right):
    return lax.dot_general(
        flat(left), flat(right), (((0,), (0,)), ((), ())), preferred_element_type=F32
    )


def own_grad_kernel(z, act_ref, cot_ref, out):
    for k in range(3):
        out[:, k * z.c : (k + 1) * z.c] = outer(cot_ref[k:], act_ref[: z.fl - k])


def cross_kernel(z, width, part_ref, far_ref, near_ref, act_ref, cot_ref, keep, send):
    mine = even("space")
    before = jnp.where(even("tm"), far_ref[...], near_ref[...])
    after = jnp.where(even("tm"), near_ref[...], far_ref[...])
    for k in range(3):
        lanes = slice(k * z.c, (k + 1) * z.c)
        grad = part_ref[:, lanes]
        if k == 1:
            grad += outer(cot_ref[0], before)
        if k == 2:
            grad += outer(cot_ref[1], before)
            grad += outer(after, act_ref[z.fl - 2])
        for i in range(z.c // (2 * width)):
            low = grad[2 * i * width : (2 * i + 1) * width]
            high = grad[(2 * i + 1) * width : (2 * i + 2) * width]
            keep[i * width : (i + 1) * width, lanes] = jnp.where(mine, low, high)
            send[i * width : (i + 1) * width, lanes] = jnp.where(mine, high, low).astype(BF)


def gather_matrix(z, me):
    def source(q):
        s = q % z.f // z.fl
        return ((me ^ s) * z.fl + q % z.fl) * z.wc + q // z.f

    return chooser(z.block, z.block, source)


def assemble_kernel(z, *refs):
    parts, (out, near, far) = z.by_partner(refs[: z.n]), refs[z.n :]
    me = lax.axis_index("tm")
    lower = even("space")
    matrix = gather_matrix(z, me)

    def edge(q):
        head = q // z.f
        s = q % z.f // z.fl
        return ((me ^ s) * 2 * z.r + head) * z.fl + q % z.fl

    count = z.n * z.sides
    tails = jnp.concatenate([p[z.main : z.main + z.sides] for p in parts], axis=0)
    tails = moved(chooser(count, count, edge), tails)
    last = z.f + z.block
    for r in range(z.r):
        rows = jnp.concatenate([p[r * z.piece : (r + 1) * z.piece] for p in parts], axis=0)
        rows = moved(matrix, rows)
        left = tails[r * z.f : (r + 1) * z.f]
        right = tails[(z.r + r) * z.f : (z.r + r + 1) * z.f]
        out[r, 0 : z.f] = left
        out[r, z.f : last] = rows
        out[r, last : last + z.f] = right
    near[...] = jnp.where(lower, out[z.r - 1], out[0])
    far[...] = jnp.where(lower, out[0], out[z.r - 1])


def taps(pieces, weights):
    rows = jnp.concatenate(pieces, axis=1)
    return jnp.dot(rows, flat(weights), preferred_element_type=F32)


def conv_row(z, w_ref, three):
    return silu(taps([rows[dj * z.f : dj * z.f + z.block] for rows in three for dj in range(3)], w_ref[...]))


def middle_kernel(z, x_ref, w_ref, out):
    for r in range(1, z.r - 1):
        out[r - 1] = conv_row(z, w_ref, [x_ref.at[r + di] for di in (-1, 0, 1)])


def border_kernel(z, x_ref, near_ref, far_ref, w_ref, out, edges):
    lower = even("space")
    edges[0] = jnp.where(lower, far_ref[...], near_ref[...])
    edges[1] = jnp.where(lower, near_ref[...], far_ref[...])
    out[0] = conv_row(z, w_ref, [edges.at[0], x_ref.at[0], x_ref.at[1]])
    out[1] = conv_row(z, w_ref, [x_ref.at[z.r - 2], x_ref.at[z.r - 1], edges.at[1]])


def staged(z, stages):
    for step in range(z.r + len(stages) - 1):
        for late, stage in reversed(list(enumerate(stages))):
            if 0 <= step - late < z.r:
                stage(step - late)


def main_kernel(
    z, middle_ref, border_ref, x_ref, t_ref, gain_ref, q_ref, k_ref, v_ref, o_ref, *outs
):
    me = lax.axis_index("tm")
    a = lax.broadcasted_iota(jnp.int32, (z.block, z.block), 0)
    b = lax.broadcasted_iota(jnp.int32, (z.block, z.block), 1)
    allowed = (a // z.f == b // z.f) & (b % z.f <= a % z.f)
    scale = float(z.c) ** -0.5

    def source(q):
        t = ((me ^ (q // z.piece)) * z.fl) + q % z.piece // z.wc
        return q % z.wc * z.f + t

    back = chooser(z.block, z.block, source)
    frame = lax.broadcasted_iota(jnp.int32, (z.block, z.c), 0) % z.f
    held = {}

    def activate(r):
        act = border_ref[r // (z.r - 1)] if r in (0, z.r - 1) else middle_ref[r - 1]
        wide = act.astype(F32)
        held["a", r] = [act] + [
            jnp.where(frame >= k, pltpu.roll(wide, k, 0), 0.0).astype(BF) for k in (1, 2)
        ]

    def hide(r):
        temporal = taps(held.pop(("a", r)), t_ref[...])
        hidden = (x_ref[r, z.f : z.f + z.block].astype(F32) + temporal).astype(BF)
        held["h", r] = hidden

    def norm(r):
        wide = held["h", r].astype(F32)
        mean = jnp.mean(wide * wide, axis=1, keepdims=True)
        held["n", r] = (wide * (1.0 / jnp.sqrt(mean + 1e-06)) * gain_ref[...]).astype(BF)

    def project(r):
        rows = held.pop(("n", r))
        held["q", r], held["k", r], held["v", r] = (
            jnp.dot(rows, w[...], preferred_element_type=F32).astype(BF)
            for w in (q_ref, k_ref, v_ref)
        )

    def score(r):
        held["s", r] = lax.dot_general(
            held.pop(("q", r)),
            held.pop(("k", r)),
            (((1,), (1,)), ((), ())),
            preferred_element_type=F32,
        )

    def weigh(r):
        scores = jnp.where(allowed, held.pop(("s", r)) * scale, -1e30)
        top = jnp.max(scores, axis=1, keepdims=True)
        expon = jnp.where(allowed, jnp.exp(scores - top), 0.0)
        held["t", r] = 1.0 / jnp.sum(expon, axis=1, keepdims=True)
        held["p", r] = expon.astype(BF)

    def mix(r):
        mixed = jnp.dot(held.pop(("p", r)), held.pop(("v", r)), preferred_element_type=F32)
        held["a", r] = (mixed * held.pop(("t", r))).astype(BF)

    def finish(r):
        encoded = held.pop(("h", r)).astype(F32) + jnp.dot(
            held.pop(("a", r)), o_ref[...], preferred_element_type=F32
        )
        held["e", r] = encoded.astype(BF)

    def spread(r):
        encoded = moved(back, held.pop(("e", r)))
        for out, k in zip(outs, z.order):
            out[r] = encoded[k * z.piece : (k + 1) * z.piece]

    staged(z, (activate, hide, norm, project, score, weigh, mix, finish, spread))


def split_kernel(z, keep_ref, got_ref, *outs):
    me = lax.axis_index("tm")
    wide = z.c // z.n
    for tap in range(3):
        place = slice(tap * wide, (tap + 1) * wide)
        if wide % 128 == 0:
            for k in range(z.n):
                lanes = pl.ds(pl.multiple_of(tap * z.c + (me ^ k) * wide, 128), wide)
                total = keep_ref[:, lanes] + got_ref[:, lanes].astype(F32)
                outs[k][:, place] = total.astype(outs[k].dtype)
            continue
        lanes = slice(tap * z.c, (tap + 1) * z.c)
        total = keep_ref[:, lanes] + got_ref[:, lanes].astype(F32)
        for k in range(z.n):
            cut = total[:, 0:wide]
            for i in range(1, z.n):
                cut = jnp.where((me ^ k) == i, total[:, i * wide : (i + 1) * wide], cut)
            outs[k][:, place] = cut.astype(outs[k].dtype)


def swap(value, axis, k):
    count = lax.axis_size(axis)
    return lax.ppermute(value, axis, [(i, i ^ k) for i in range(count)])


def swap_both(near, far, axis):
    pairs = [(i, i + 1) for i in range(1, lax.axis_size(axis) - 1, 2)]
    far = lax.ppermute(far, axis, pairs + [(b, a) for a, b in pairs])
    return swap(near, axis, 1), far


def halve_kernel(z, width, bit, *refs):
    parts, (keep, send) = refs[:-2], refs[-2:]
    total = sum(part[...].astype(F32) for part in parts)
    lower = lax.axis_index("space") // (2 << bit) % 2 == 0
    for i in range(keep.shape[0] // width):
        low = total[2 * i * width : (2 * i + 1) * width]
        high = total[(2 * i + 1) * width : (2 * i + 2) * width]
        rows = slice(i * width, (i + 1) * width)
        keep[rows] = jnp.where(lower, low, high)
        send[rows] = jnp.where(lower, high, low).astype(BF)


def add_up(z, kept_ref, got_ref, out):
    wide = z.c // z.n
    total = kept_ref[...] + got_ref[...].astype(F32)
    for k in range(3):
        out[k] = total[:, k * wide : (k + 1) * wide]


def join_kernel(z, kept_ref, got_ref, *refs):
    parts, (out, grad, whole, total, sem) = z.by_partner(refs[: z.n]), refs[z.n :]
    me = lax.axis_index("tm")
    add_up(z, kept_ref, got_ref, total)
    copies = [pltpu.make_async_copy(total, grad, sem.at[z.fl])]
    copies[0].start()
    for f in range(z.fl):
        for k in range(z.n):
            cols = pl.ds(pl.multiple_of((me ^ k) * z.wc, z.wc), z.wc)
            whole[f, :, cols] = parts[k][:, f * z.wc : (f + 1) * z.wc]
        copies.append(pltpu.make_async_copy(whole.at[f], out.at[f], sem.at[f]))
        copies[-1].start()
    for copy in copies:
        copy.wait()


def joined(z, back, kept, got):
    grad = shape((3, kept.shape[0], z.c // z.n), F32)
    if z.wc % 16 == 0:
        return pl.pallas_call(
            functools.partial(join_kernel, z),
            out_shape=(shape((z.fl, z.r, z.w, z.c)), grad),
            in_specs=[VMEM] * (2 + z.n),
            out_specs=(pl.BlockSpec(memory_space=pl.ANY),) * 2,
            scratch_shapes=[
                pltpu.VMEM((z.fl, z.r, z.w, z.c), BF),
                pltpu.VMEM(grad.shape, F32),
                pltpu.SemaphoreType.DMA((z.fl + 1,)),
            ],
            compiler_params=pltpu.CompilerParams(vmem_limit_bytes=16 * 2**20),
            cost_estimate=pl.CostEstimate(
                flops=0, bytes_accessed=8 * z.n * z.main * z.c, transcendentals=0
            ),
        )(kept, got, *z.ordered(back))
    whole = jnp.zeros((z.fl, z.r, z.n, z.wc, z.c), BF)
    for k in range(z.n):
        rows = back[k].reshape(z.r, z.fl, 1, z.wc, z.c).transpose(1, 0, 2, 3, 4)
        whole = lax.dynamic_update_slice_in_dim(whole, rows, lax.axis_index("tm") ^ k, 2)
    (grad,) = call(functools.partial(add_up, z), [grad], kept, got)
    return whole.reshape(z.fl, z.r, z.w, z.c), grad


def on_device(frames_in, spatial, temporal, gain, q_w, k_w, v_w, o_w, cotangent):
    n = lax.axis_size("tm")
    space = lax.axis_size("space")
    z = Sizes(n, *frames_in.shape)
    one = 2 * z.r * z.block * z.c * z.c
    width, wide = z.c // space, z.c // n

    def exchange(pieces):
        pieces = list(pieces)
        for k in z.order[:-1]:
            pieces[k] = swap(pieces[k], "tm", k)
        return pieces

    edge = shape((z.fl * z.w, z.c))
    packed = call(
        functools.partial(pack_kernel, z),
        [shape((z.main + z.sides, z.c))] * n,
        frames_in,
        flops=one // 2,
    )
    near, far = call(
        functools.partial(edge_kernel, z), [edge, edge], frames_in, packed[0], flops=8 * one
    )
    got = exchange(packed)
    near, far = swap_both(near, far, "space")
    (own,) = call(
        functools.partial(own_inner_kernel, z),
        [shape((z.r, z.fl * z.w, z.c), F32)],
        frames_in,
        spatial,
        flops=8 * one,
        scratch=[pltpu.VMEM((3, z.r, z.fl * z.w, z.c), BF)],
    )
    own_act, far, near = call(
        functools.partial(own_act_kernel, z),
        [shape(frames_in.shape), shape((z.r, z.w, z.c)), shape((z.r, z.w, z.c))],
        own,
        near,
        far,
        spatial,
        cotangent,
        flops=3 * one,
    )
    near, far = swap_both(near, far, "tm")
    (own_grad,) = call(
        functools.partial(own_grad_kernel, z),
        [shape((z.c, 3 * z.c), F32)],
        own_act,
        cotangent,
        flops=9 * one // 4,
    )
    line = z.block + 2 * z.f
    x, close, apart = call(
        functools.partial(assemble_kernel, z),
        [shape((z.r, line, z.c)), shape((line, z.c)), shape((line, z.c))],
        *z.ordered(got),
    )
    close, apart = swap_both(close, apart, "space")
    (middle,) = call(
        functools.partial(middle_kernel, z),
        [shape((z.r - 2, z.block, z.c))],
        x,
        spatial,
        flops=9 * one * (z.r - 2) // z.r,
    )
    tied = lax.optimization_barrier((far, near, middle, close, apart))
    far, near, middle, close, apart = tied
    keep, send = call(
        functools.partial(cross_kernel, z, width),
        [shape((z.c // 2, 3 * z.c), F32), shape((z.c // 2, 3 * z.c))],
        own_grad,
        far,
        near,
        own_act,
        cotangent,
        flops=3 * one // 4,
    )
    other = swap(send, "space", 1)
    x, _ = lax.optimization_barrier((x, send))
    (border,) = call(
        functools.partial(border_kernel, z),
        [shape((2, z.block, z.c))],
        x,
        close,
        apart,
        spatial,
        flops=18 * one // z.r,
        scratch=[pltpu.VMEM((2, line, z.c), BF)],
    )
    other, border = lax.optimization_barrier((other, border))
    pieces = call(
        functools.partial(split_kernel, z),
        [shape((z.c // 2, 3 * wide), F32)] + [shape((z.c // 2, 3 * wide))] * (n - 1),
        keep,
        other,
    )
    border, *pieces = lax.optimization_barrier((border, *pieces))
    pieces = exchange(pieces)
    encoded = z.by_partner(call(
        functools.partial(main_kernel, z),
        [shape((z.r, z.piece, z.c))] * n,
        middle,
        border,
        x,
        temporal,
        gain.reshape(1, z.c),
        q_w,
        k_w,
        v_w,
        o_w,
        flops=9 * one,
    ))
    back = exchange(encoded)
    pieces = lax.optimization_barrier((*z.ordered(pieces), *z.ordered(encoded)))[:n]
    bit = 0
    while 2 << bit < space:
        half = (pieces[0].shape[0] // 2, 3 * wide)
        keep, send = call(
            functools.partial(halve_kernel, z, width, bit), [shape(half, F32), shape(half)], *pieces
        )
        pieces = (keep, swap(send, "space", 2 << bit))
        bit += 1
    encoded, kernel_grad = joined(z, back, *pieces)
    return encoded, kernel_grad.transpose(0, 2, 1)


def solution(mesh):
    tiles = P("tm", "space", None, None)
    return jax.shard_map(
        on_device,
        mesh=mesh,
        in_specs=(tiles,) + (P(),) * 7 + (tiles,),
        out_specs=(tiles, P(None, "tm", "space")),
        check_vma=False,
    )
```

```python
import functools

import jax
import jax.numpy as jnp
from jax import lax
from jax.experimental import pallas as pl
from jax.experimental.pallas import tpu as pltpu
from jax.sharding import PartitionSpec as P

BF = jnp.bfloat16
F32 = jnp.float32
VMEM = pl.BlockSpec(memory_space=pltpu.VMEM)


def call(kernel, outs, *args, flops=0, scratch=(), limit=16):
    moved = sum(a.size * a.dtype.itemsize for a in args)
    moved += sum(o.size * o.dtype.itemsize for o in outs)
    return pl.pallas_call(
        kernel,
        out_shape=tuple(outs),
        in_specs=[VMEM] * len(args),
        out_specs=tuple(VMEM for _ in outs),
        scratch_shapes=scratch,
        compiler_params=pltpu.CompilerParams(vmem_limit_bytes=limit * 2**20),
        cost_estimate=pl.CostEstimate(flops=flops, bytes_accessed=moved, transcendentals=0),
    )(*args)


def shape(dims, kind=BF):
    return jax.ShapeDtypeStruct(dims, kind)


def chooser(rows, cols, source):
    q = lax.broadcasted_iota(jnp.int32, (rows, cols), 0)
    m = lax.broadcasted_iota(jnp.int32, (rows, cols), 1)
    return jnp.where(source(q) == m, 1.0, 0.0).astype(BF)


def moved(matrix, rows):
    return jnp.dot(matrix, rows, preferred_element_type=F32).astype(BF)


class Sizes:
    def __init__(self, count, frames, rows, cols, chans):
        self.n, self.fl, self.r, self.w, self.c = count, frames, rows, cols, chans
        self.f = count * frames
        self.wc = cols // count
        self.block = self.f * self.wc
        self.piece = frames * self.wc
        self.main = rows * self.piece
        self.sides = 2 * rows * frames
        self.order = sorted(range(count), key=lambda k: -k.bit_count())

    def ordered(self, pieces):
        return [pieces[k] for k in self.order]

    def by_partner(self, pieces):
        return [pieces[self.order.index(k)] for k in range(self.n)]


def even(axis):
    return lax.axis_index(axis) % 2 == 0


def edge_kernel(z, x_ref, after_ref, near, far):
    top, bottom = (flat(x_ref[:, r]) for r in (0, z.r - 1))
    near[...] = jnp.where(even("space"), bottom, top)
    far[...] = jnp.where(even("space"), top, bottom)


def pack_kernel(z, x_ref, *outs):
    me = lax.axis_index("tm")

    def source(q):
        k = q // z.piece
        f = q % z.piece // z.wc
        return f * z.w + (me ^ k) * z.wc + q % z.wc

    def edge(r, q):
        k = q // z.sides
        side = q % z.sides // (z.r * z.fl)
        row = q % (z.r * z.fl) // z.fl
        col = (me ^ k) * z.wc - 1 + side * (z.wc + 1)
        inside = (col >= 0) & (col < z.w) & (row == r)
        return jnp.where(inside, q % z.fl * z.w + col, -1)

    matrix = chooser(z.n * z.piece, z.fl * z.w, source)
    tails = jnp.zeros((z.n * z.sides, z.c), F32)
    for r in range(z.r):
        rows = x_ref[:, r].reshape(z.fl * z.w, z.c)
        cut = moved(matrix, rows)
        for k in range(z.n):
            outs[k][r * z.piece : (r + 1) * z.piece] = cut[k * z.piece : (k + 1) * z.piece]
        picked = chooser(z.n * z.sides, z.fl * z.w, functools.partial(edge, r))
        tails += jnp.dot(picked, rows, preferred_element_type=F32)
    tails = tails.astype(BF)
    for k in range(z.n):
        outs[k][z.main : z.main + z.sides] = tails[k * z.sides : (k + 1) * z.sides]


def aside(z, rows):
    count = z.fl * z.w
    left = chooser(count, count, lambda q: jnp.where(q % z.w > 0, q - 1, -1))
    right = chooser(count, count, lambda q: jnp.where(q % z.w < z.w - 1, q + 1, -1))
    return moved(left, rows), rows, moved(right, rows)


def own_inner_kernel(z, x_ref, w_ref, out, beside):
    for r in range(z.r):
        for dj, rows in enumerate(aside(z, x_ref[:, r].reshape(z.fl * z.w, z.c))):
            beside[dj, r] = rows
    for r in range(z.r):
        low, high = max(0, 1 - r), min(3, z.r + 1 - r)
        pieces = [beside[dj, r + di - 1] for di in range(low, high) for dj in range(3)]
        out[r] = taps(pieces, w_ref[low:high])


def own_act_kernel(z, part_ref, far_ref, near_ref, w_ref, cot_ref, out, near, far):
    lower = even("space")
    first = even("tm")
    for r in range(z.r):
        total = part_ref[r]
        for edge, di in ((0, 0), (z.r - 1, 2)):
            if r == edge:
                rows = jnp.where(lower == (di == 2), near_ref[...], far_ref[...])
                total += taps(aside(z, rows), w_ref[di])
        act = silu(total).reshape(z.fl, z.w, z.c)
        out[:, r] = act
        last = act[z.fl - 1]
        near[r] = jnp.where(first, last, cot_ref[0, r])
        far[r] = jnp.where(first, cot_ref[0, r], last)


def silu(total):
    return (total / (1.0 + jnp.exp(-total))).astype(BF)


def flat(value):
    return value.reshape(-1, value.shape[-1])


def outer(left, right):
    return lax.dot_general(
        flat(left), flat(right), (((0,), (0,)), ((), ())), preferred_element_type=F32
    )


def own_grad_kernel(z, act_ref, cot_ref, out):
    for k in range(3):
        out[:, k * z.c : (k + 1) * z.c] = outer(cot_ref[k:], act_ref[: z.fl - k])


def cross_kernel(z, width, part_ref, near_ref, far_ref, act_ref, cot_ref, keep, send):
    mine = even("space")
    before = jnp.where(even("tm"), far_ref[...], near_ref[...])
    after = jnp.where(even("tm"), near_ref[...], far_ref[...])
    for k in range(3):
        lanes = slice(k * z.c, (k + 1) * z.c)
        grad = part_ref[:, lanes]
        if k == 1:
            grad += outer(cot_ref[0], before)
        if k == 2:
            grad += outer(cot_ref[1], before)
            grad += outer(after, act_ref[z.fl - 2])
        for i in range(z.c // (2 * width)):
            low = grad[2 * i * width : (2 * i + 1) * width]
            high = grad[(2 * i + 1) * width : (2 * i + 2) * width]
            keep[i * width : (i + 1) * width, lanes] = jnp.where(mine, low, high)
            send[i * width : (i + 1) * width, lanes] = jnp.where(mine, high, low).astype(BF)


def gather_matrix(z, me):
    def source(q):
        s = q % z.f // z.fl
        return ((me ^ s) * z.fl + q % z.fl) * z.wc + q // z.f

    return chooser(z.block, z.block, source)


def assemble_kernel(z, *refs):
    parts, (out, near, far) = z.by_partner(refs[: z.n]), refs[z.n :]
    me = lax.axis_index("tm")
    lower = even("space")
    matrix = gather_matrix(z, me)

    def edge(q):
        head = q // z.f
        s = q % z.f // z.fl
        return ((me ^ s) * 2 * z.r + head) * z.fl + q % z.fl

    count = z.n * z.sides
    tails = jnp.concatenate([p[z.main : z.main + z.sides] for p in parts], axis=0)
    tails = moved(chooser(count, count, edge), tails)
    last = z.f + z.block
    for r in range(z.r):
        rows = jnp.concatenate([p[r * z.piece : (r + 1) * z.piece] for p in parts], axis=0)
        rows = moved(matrix, rows)
        left = tails[r * z.f : (r + 1) * z.f]
        right = tails[(z.r + r) * z.f : (z.r + r + 1) * z.f]
        out[r, 0 : z.f] = left
        out[r, z.f : last] = rows
        out[r, last : last + z.f] = right
    near[...] = jnp.where(lower, out[z.r - 1], out[0])
    far[...] = jnp.where(lower, out[0], out[z.r - 1])


def taps(pieces, weights):
    rows = jnp.concatenate(pieces, axis=1)
    return jnp.dot(rows, flat(weights), preferred_element_type=F32)


def conv_row(z, w_ref, three):
    return silu(taps([rows[dj * z.f : dj * z.f + z.block] for rows in three for dj in range(3)], w_ref[...]))


def middle_kernel(z, x_ref, w_ref, out):
    for r in range(1, z.r - 1):
        out[r - 1] = conv_row(z, w_ref, [x_ref.at[r + di] for di in (-1, 0, 1)])


def border_kernel(z, x_ref, far_ref, near_ref, w_ref, out, edges):
    lower = even("space")
    edges[0] = jnp.where(lower, far_ref[...], near_ref[...])
    edges[1] = jnp.where(lower, near_ref[...], far_ref[...])
    out[0] = conv_row(z, w_ref, [edges.at[0], x_ref.at[0], x_ref.at[1]])
    out[1] = conv_row(z, w_ref, [x_ref.at[z.r - 2], x_ref.at[z.r - 1], edges.at[1]])


def staged(z, stages):
    for step in range(z.r + len(stages) - 1):
        for late, stage in reversed(list(enumerate(stages))):
            if 0 <= step - late < z.r:
                stage(step - late)


def main_kernel(
    z, middle_ref, border_ref, x_ref, t_ref, gain_ref, q_ref, k_ref, v_ref, o_ref, *outs
):
    me = lax.axis_index("tm")
    a = lax.broadcasted_iota(jnp.int32, (z.block, z.block), 0)
    b = lax.broadcasted_iota(jnp.int32, (z.block, z.block), 1)
    allowed = (a // z.f == b // z.f) & (b % z.f <= a % z.f)
    scale = float(z.c) ** -0.5

    def source(q):
        t = ((me ^ (q // z.piece)) * z.fl) + q % z.piece // z.wc
        return q % z.wc * z.f + t

    back = chooser(z.block, z.block, source)
    frame = lax.broadcasted_iota(jnp.int32, (z.block, z.c), 0) % z.f
    held = {}

    def activate(r):
        act = border_ref[r // (z.r - 1)] if r in (0, z.r - 1) else middle_ref[r - 1]
        wide = act.astype(F32)
        held["a", r] = [act] + [
            jnp.where(frame >= k, pltpu.roll(wide, k, 0), 0.0).astype(BF) for k in (1, 2)
        ]

    def hide(r):
        temporal = taps(held.pop(("a", r)), t_ref[...])
        hidden = (x_ref[r, z.f : z.f + z.block].astype(F32) + temporal).astype(BF)
        held["h", r] = hidden

    def norm(r):
        wide = held["h", r].astype(F32)
        mean = jnp.mean(wide * wide, axis=1, keepdims=True)
        held["n", r] = (wide * (1.0 / jnp.sqrt(mean + 1e-06)) * gain_ref[...]).astype(BF)

    def project(r):
        rows = held.pop(("n", r))
        held["q", r], held["k", r], held["v", r] = (
            jnp.dot(rows, w[...], preferred_element_type=F32).astype(BF)
            for w in (q_ref, k_ref, v_ref)
        )

    def score(r):
        held["s", r] = lax.dot_general(
            held.pop(("q", r)),
            held.pop(("k", r)),
            (((1,), (1,)), ((), ())),
            preferred_element_type=F32,
        )

    def weigh(r):
        scores = jnp.where(allowed, held.pop(("s", r)) * scale, -1e30)
        top = jnp.max(scores, axis=1, keepdims=True)
        expon = jnp.where(allowed, jnp.exp(scores - top), 0.0)
        held["t", r] = 1.0 / jnp.sum(expon, axis=1, keepdims=True)
        held["p", r] = expon.astype(BF)

    def mix(r):
        mixed = jnp.dot(held.pop(("p", r)), held.pop(("v", r)), preferred_element_type=F32)
        held["a", r] = (mixed * held.pop(("t", r))).astype(BF)

    def finish(r):
        encoded = held.pop(("h", r)).astype(F32) + jnp.dot(
            held.pop(("a", r)), o_ref[...], preferred_element_type=F32
        )
        held["e", r] = encoded.astype(BF)

    def spread(r):
        encoded = moved(back, held.pop(("e", r)))
        for out, k in zip(outs, z.order):
            out[r] = encoded[k * z.piece : (k + 1) * z.piece]

    staged(z, (activate, hide, norm, project, score, weigh, mix, finish, spread))


def split_kernel(z, keep_ref, got_ref, *outs):
    me = lax.axis_index("tm")
    wide = z.c // z.n
    for tap in range(3):
        place = slice(tap * wide, (tap + 1) * wide)
        if wide % 128 == 0:
            for k in range(z.n):
                lanes = pl.ds(pl.multiple_of(tap * z.c + (me ^ k) * wide, 128), wide)
                total = keep_ref[:, lanes] + got_ref[:, lanes].astype(F32)
                outs[k][:, place] = total.astype(outs[k].dtype)
            continue
        lanes = slice(tap * z.c, (tap + 1) * z.c)
        total = keep_ref[:, lanes] + got_ref[:, lanes].astype(F32)
        for k in range(z.n):
            cut = total[:, 0:wide]
            for i in range(1, z.n):
                cut = jnp.where((me ^ k) == i, total[:, i * wide : (i + 1) * wide], cut)
            outs[k][:, place] = cut.astype(outs[k].dtype)


def swap(value, axis, k):
    count = lax.axis_size(axis)
    return lax.ppermute(value, axis, [(i, i ^ k) for i in range(count)])


def swap_both(near, far, axis):
    pairs = [(i, i + 1) for i in range(1, lax.axis_size(axis) - 1, 2)]
    far = lax.ppermute(far, axis, pairs + [(b, a) for a, b in pairs])
    return swap(near, axis, 1), far


def halve_kernel(z, width, bit, *refs):
    parts, (keep, send) = refs[:-2], refs[-2:]
    total = sum(part[...].astype(F32) for part in parts)
    lower = lax.axis_index("space") // (2 << bit) % 2 == 0
    for i in range(keep.shape[0] // width):
        low = total[2 * i * width : (2 * i + 1) * width]
        high = total[(2 * i + 1) * width : (2 * i + 2) * width]
        rows = slice(i * width, (i + 1) * width)
        keep[rows] = jnp.where(lower, low, high)
        send[rows] = jnp.where(lower, high, low).astype(BF)


def add_up(z, kept_ref, got_ref, out):
    wide = z.c // z.n
    total = kept_ref[...] + got_ref[...].astype(F32)
    for k in range(3):
        out[k] = total[:, k * wide : (k + 1) * wide]


def join_kernel(z, kept_ref, got_ref, *refs):
    parts, (out, grad, whole, total, sem) = z.by_partner(refs[: z.n]), refs[z.n :]
    me = lax.axis_index("tm")
    add_up(z, kept_ref, got_ref, total)
    copies = [pltpu.make_async_copy(total, grad, sem.at[z.fl])]
    copies[0].start()
    for f in range(z.fl):
        for k in range(z.n):
            cols = pl.ds(pl.multiple_of((me ^ k) * z.wc, z.wc), z.wc)
            whole[f, :, cols] = parts[k][:, f * z.wc : (f + 1) * z.wc]
        copies.append(pltpu.make_async_copy(whole.at[f], out.at[f], sem.at[f]))
        copies[-1].start()
    for copy in copies:
        copy.wait()


def joined(z, back, kept, got):
    grad = shape((3, kept.shape[0], z.c // z.n), F32)
    if z.wc % 16 == 0:
        return pl.pallas_call(
            functools.partial(join_kernel, z),
            out_shape=(shape((z.fl, z.r, z.w, z.c)), grad),
            in_specs=[VMEM] * (2 + z.n),
            out_specs=(pl.BlockSpec(memory_space=pl.ANY),) * 2,
            scratch_shapes=[
                pltpu.VMEM((z.fl, z.r, z.w, z.c), BF),
                pltpu.VMEM(grad.shape, F32),
                pltpu.SemaphoreType.DMA((z.fl + 1,)),
            ],
            compiler_params=pltpu.CompilerParams(vmem_limit_bytes=16 * 2**20),
            cost_estimate=pl.CostEstimate(
                flops=0, bytes_accessed=8 * z.n * z.main * z.c, transcendentals=0
            ),
        )(kept, got, *z.ordered(back))
    whole = jnp.zeros((z.fl, z.r, z.n, z.wc, z.c), BF)
    for k in range(z.n):
        rows = back[k].reshape(z.r, z.fl, 1, z.wc, z.c).transpose(1, 0, 2, 3, 4)
        whole = lax.dynamic_update_slice_in_dim(whole, rows, lax.axis_index("tm") ^ k, 2)
    (grad,) = call(functools.partial(add_up, z), [grad], kept, got)
    return whole.reshape(z.fl, z.r, z.w, z.c), grad


def on_device(frames_in, spatial, temporal, gain, q_w, k_w, v_w, o_w, cotangent):
    n = lax.axis_size("tm")
    space = lax.axis_size("space")
    z = Sizes(n, *frames_in.shape)
    one = 2 * z.r * z.block * z.c * z.c
    width, wide = z.c // space, z.c // n

    def exchange(pieces):
        pieces = list(pieces)
        for k in z.order[:-1]:
            pieces[k] = swap(pieces[k], "tm", k)
        return pieces

    edge = shape((z.fl * z.w, z.c))
    packed = call(
        functools.partial(pack_kernel, z),
        [shape((z.main + z.sides, z.c))] * n,
        frames_in,
        flops=one // 2,
    )
    near, far = call(
        functools.partial(edge_kernel, z), [edge, edge], frames_in, packed[0], flops=8 * one
    )
    got = exchange(packed)
    near, far = swap_both(near, far, "space")
    (own,) = call(
        functools.partial(own_inner_kernel, z),
        [shape((z.r, z.fl * z.w, z.c), F32)],
        frames_in,
        spatial,
        flops=8 * one,
        scratch=[pltpu.VMEM((3, z.r, z.fl * z.w, z.c), BF)],
    )
    own_act, near, far = call(
        functools.partial(own_act_kernel, z),
        [shape(frames_in.shape), shape((z.r, z.w, z.c)), shape((z.r, z.w, z.c))],
        own,
        far,
        near,
        spatial,
        cotangent,
        flops=3 * one,
    )
    near, far = swap_both(near, far, "tm")
    (own_grad,) = call(
        functools.partial(own_grad_kernel, z),
        [shape((z.c, 3 * z.c), F32)],
        own_act,
        cotangent,
        flops=9 * one // 4,
    )
    line = z.block + 2 * z.f
    x, close, apart = call(
        functools.partial(assemble_kernel, z),
        [shape((z.r, line, z.c)), shape((line, z.c)), shape((line, z.c))],
        *z.ordered(got),
    )
    close, apart = swap_both(close, apart, "space")
    (middle,) = call(
        functools.partial(middle_kernel, z),
        [shape((z.r - 2, z.block, z.c))],
        x,
        spatial,
        flops=9 * one * (z.r - 2) // z.r,
    )
    tied = lax.optimization_barrier((near, far, middle, apart, close))
    near, far, middle, apart, close = tied
    keep, send = call(
        functools.partial(cross_kernel, z, width),
        [shape((z.c // 2, 3 * z.c), F32), shape((z.c // 2, 3 * z.c))],
        own_grad,
        near,
        far,
        own_act,
        cotangent,
        flops=3 * one // 4,
    )
    other = swap(send, "space", 1)
    x, _ = lax.optimization_barrier((x, send))
    (border,) = call(
        functools.partial(border_kernel, z),
        [shape((2, z.block, z.c))],
        x,
        apart,
        close,
        spatial,
        flops=18 * one // z.r,
        scratch=[pltpu.VMEM((2, line, z.c), BF)],
    )
    other, border = lax.optimization_barrier((other, border))
    pieces = call(
        functools.partial(split_kernel, z),
        [shape((z.c // 2, 3 * wide), F32)] + [shape((z.c // 2, 3 * wide))] * (n - 1),
        keep,
        other,
    )
    border, *pieces = lax.optimization_barrier((border, *pieces))
    pieces = exchange(pieces)
    encoded = z.by_partner(call(
        functools.partial(main_kernel, z),
        [shape((z.r, z.piece, z.c))] * n,
        middle,
        border,
        x,
        temporal,
        gain.reshape(1, z.c),
        q_w,
        k_w,
        v_w,
        o_w,
        flops=9 * one,
    ))
    back = exchange(encoded)
    pieces = lax.optimization_barrier((*z.ordered(pieces), *z.ordered(encoded)))[:n]
    bit = 0
    while 2 << bit < space:
        half = (pieces[0].shape[0] // 2, 3 * wide)
        keep, send = call(
            functools.partial(halve_kernel, z, width, bit), [shape(half, F32), shape(half)], *pieces
        )
        pieces = (keep, swap(send, "space", 2 << bit))
        bit += 1
    encoded, kernel_grad = joined(z, back, *pieces)
    return encoded, kernel_grad.transpose(0, 2, 1)


def solution(mesh):
    tiles = P("tm", "space", None, None)
    return jax.shard_map(
        on_device,
        mesh=mesh,
        in_specs=(tiles,) + (P(),) * 7 + (tiles,),
        out_specs=(tiles, P(None, "tm", "space")),
        check_vma=False,
    )
```
